32 devices in a mesh: seq: 8 (over z, y), head: 4 (over x, core).
Axes of the slice: x: 2, y: 2, z: 4, core: 2. Of those that a mesh axis runs over, the one named last changes fastest.
Arguments:
- tokens: bfloat16 [8, 1024, 2048], P(None, 'seq'), may hold values from -6 to 6
- cotangent: bfloat16 [8, 1024, 2048], P(None, 'seq'), may hold values from -6 to 6
- first_norm_gain: bfloat16 [2048], replicated, may hold values from 0.5 to 1.5
- second_norm_gain: bfloat16 [2048], replicated, may hold values from 0.5 to 1.5
- query_weight: bfloat16 [2048, 2048], P('seq', 'head'), may hold values from -0.125 to 0.125
- key_weight: bfloat16 [2048, 512], P('seq', 'head'), may hold values from -0.125 to 0.125
- value_weight: bfloat16 [2048, 512], P('seq', 'head'), may hold values from -0.125 to 0.125
- output_weight: bfloat16 [2048, 2048], P('head', 'seq'), may hold values from -0.75 to 0.75
- gate_weight: bfloat16 [2048, 8192], P('seq', 'head'), may hold values from -0.125 to 0.125
- up_weight: bfloat16 [2048, 8192], P('seq', 'head'), may hold values from -0.125 to 0.125
- down_weight: bfloat16 [8192, 2048], P('head', 'seq'), may hold values from -0.0625 to 0.0625
- adapter_down_weight: bfloat16 [2048, 24], replicated, may hold values from -0.125 to 0.125
- adapter_query_weight: bfloat16 [8, 2048], P(None, 'head'), may hold values from -0.5 to 0.5
- adapter_key_weight: bfloat16 [8, 512], P(None, 'head'), may hold values from -0.5 to 0.5
- adapter_value_weight: bfloat16 [8, 512], P(None, 'head'), may hold values from -0.5 to 0.5
- adapter_output_down: bfloat16 [2048, 8], P('head'), may hold values from -0.75 to 0.75
- adapter_output_up: bfloat16 [8, 2048], replicated, may hold values from -1 to 1
- hedgehog_query_weight: bfloat16 [32, 64, 64], P('head'), may hold values from -1 to 1
- hedgehog_key_weight: bfloat16 [8, 64, 64], P('head'), may hold values from -1 to 1
- document_index: int32 [8, 1024], replicated, may hold values from 0 to 4, as said below
Outputs:
- layer_out: bfloat16 [8, 1024, 2048], P(None, 'seq')
- grad_tokens: float32 [8, 1024, 2048], P(None, 'seq')
- grad_gain_one: float32 [2048], replicated
- grad_gain_two: float32 [2048], replicated
- grad_w_query: float32 [2048, 2048], P('seq', 'head')
- grad_w_key: float32 [2048, 512], P('seq', 'head')
- grad_w_value: float32 [2048, 512], P('seq', 'head')
- grad_w_out: float32 [2048, 2048], P('head', 'seq')
- grad_w_gate: float32 [2048, 8192], P('seq', 'head')
- grad_w_up: float32 [2048, 8192], P('seq', 'head')
- grad_w_down: float32 [8192, 2048], P('head', 'seq')
- adapter_down_gradient: float32 [2048, 24], replicated
- adapter_query_gradient: float32 [8, 2048], P(None, 'head')
- adapter_key_gradient: float32 [8, 512], P(None, 'head')
- adapter_value_gradient: float32 [8, 512], P(None, 'head')
- adapter_output_down_gradient: float32 [2048, 8], P('head')
- adapter_output_up_gradient: float32 [8, 2048], replicated
- grad_map_query: float32 [32, 64, 64], P('head')
- grad_map_key: float32 [8, 64, 64], P('head')
The draws below stay inside these ranges and needn't reach their ends.
Inputs may be any that keep to these rules, and one draw needn't show every extreme that they name: `document_index`: in each row the ids start at 0, never fall, and end at 4; where the id changes a new document begins.
All inputs are finite; a program needn't handle non-finite values.
Results may differ from the reference program's by a relative error of at most 0.023.
Values may be sent and summed in bfloat16 or wider, within the bound.
No kernel may reach another device: no remote copies, remote signals or barrier semaphores. Data moves between devices by JAX's collectives and lax.ppermute only.
A program may use at most 256 MiB of HBM per device.

```python
import jax
import jax.numpy as jnp
from jax import lax

MODEL_WIDTH = 2048
QUERY_HEADS = 32
KEY_VALUE_HEADS = 8
HEAD_FEATURES = 64
FF = 8192
HEDGEHOG_OUTPUTS = 64
FEATURE_SIZE = 128
ADAPTER_RANK = 8
WIN = 64
SHARD_POSITIONS = 128
ROWS = 8
LEN = 1024


def draw_document_index(key, part):
    key = jax.random.fold_in(key, 11)
    streams = jax.random.split(key, 6)
    spread = jax.random.randint(streams[0], (ROWS, 4), 1, LEN)
    first = jax.random.randint(streams[1], (ROWS,), 1, SHARD_POSITIONS // 2)
    second = jax.random.randint(streams[2], (ROWS,), SHARD_POSITIONS // 2, SHARD_POSITIONS)
    third = LEN - SHARD_POSITIONS + jax.random.randint(streams[3], (ROWS,), 0, SHARD_POSITIONS // 2)
    fourth = LEN - SHARD_POSITIONS // 2 + jax.random.randint(streams[4], (ROWS,), 1, SHARD_POSITIONS // 2)
    chosen = jax.random.randint(streams[5], (), 0, ROWS)
    planned = jnp.stack([first, second, third, fourth], axis=1)
    spanning = (jnp.arange(ROWS) == chosen)[:, None]
    bounds = jnp.where(spanning, planned, spread)
    positions = jnp.arange(LEN)
    passed = (positions[None, :, None] >= bounds[:, None, :]).astype(jnp.int32)
    return jnp.sum(passed, axis=-1).astype(jnp.int32)


def strengthened(array, key, source, target, shards_of, factor):
    def block_of(axis_at):
        return (jnp.arange(array.shape[axis_at]) // (array.shape[axis_at] // shards_of)).reshape((-1,) + (1,) * (array.ndim - 1 - axis_at))

    first = jax.random.permutation(key, shards_of)[block_of(target)]
    second = (block_of(target) + shards_of // 2) % shards_of
    return jnp.where((block_of(source) == first) | (block_of(source) == second), factor * array, array)


def level_of(key, extent, cuts, least, high):
    def one(axis_at, shards_of):
        draws = jax.random.uniform(jax.random.fold_in(jax.random.fold_in(key, 6), axis_at), (shards_of,), jnp.float32, least / len(cuts), high / len(cuts))
        return jnp.repeat(jnp.exp(draws), extent[axis_at] // shards_of).reshape((-1,) + (1,) * (len(extent) - axis_at - 1))

    level = one(*cuts[0])
    for cut in cuts[1:]:
        level = level * one(*cut)
    return level


def noise(own_key, extent, scale, reach, cuts=(), held_as=jnp.bfloat16):
    values = scale * jax.random.normal(own_key, extent, jnp.float32)
    if cuts:
        values = values * level_of(own_key, extent, cuts, -0.22, 0.18)
    return jnp.clip(values, -reach, reach).astype(held_as)


def noise_with(own_key, shape, scale, limit, cuts, heavy, held_as=jnp.bfloat16):
    values = scale * jax.random.normal(own_key, shape, jnp.float32)
    if cuts:
        values = values * level_of(own_key, shape, cuts, -0.22, 0.18)
    return jnp.clip(strengthened(values, jax.random.fold_in(own_key, 3), *heavy), -limit, limit).astype(held_as)


def setup_inputs(seed: int = 0) -> dict:
    splits = jax.random.split(jax.random.key(seed), 21)
    tokens = noise(splits[0], (ROWS, LEN, MODEL_WIDTH), 1.0, 6.0, ((1, 8),))
    cotangent = noise_with(splits[1], (ROWS, LEN, MODEL_WIDTH), 1.0, 6.0, ((1, 8),), (1, 2, 8, 2.0))
    first_norm_gain = jnp.clip(1.0 + 0.1 * jax.random.normal(splits[2], (MODEL_WIDTH,), jnp.float32), 0.5, 1.5).astype(jnp.bfloat16)
    second_norm_gain = jnp.clip(1.0 + 0.1 * jax.random.normal(splits[3], (MODEL_WIDTH,), jnp.float32), 0.5, 1.5).astype(jnp.bfloat16)
    query_weight = noise(splits[4], (MODEL_WIDTH, QUERY_HEADS * HEAD_FEATURES), MODEL_WIDTH ** -0.5, 0.125, ((0, 8), (1, 4)))
    key_weight = noise(splits[5], (MODEL_WIDTH, KEY_VALUE_HEADS * HEAD_FEATURES), MODEL_WIDTH ** -0.5, 0.125, ((0, 8), (1, 4)))
    value_weight = noise(splits[6], (MODEL_WIDTH, KEY_VALUE_HEADS * HEAD_FEATURES), MODEL_WIDTH ** -0.5, 0.125, ((0, 8), (1, 4)))
    output_weight = noise(splits[7], (QUERY_HEADS * HEAD_FEATURES, MODEL_WIDTH), HEAD_FEATURES ** -0.5, 0.75, ((0, 4), (1, 8)))
    gate_weight = noise(splits[8], (MODEL_WIDTH, FF), MODEL_WIDTH ** -0.5, 0.125, ((0, 8), (1, 4)))
    up_weight = noise(splits[9], (MODEL_WIDTH, FF), MODEL_WIDTH ** -0.5, 0.125, ((0, 8), (1, 4)))
    down_weight = noise(splits[10], (FF, MODEL_WIDTH), FF ** -0.5, 0.0625, ((0, 4), (1, 8)))
    adapter_down_weight = noise(splits[11], (MODEL_WIDTH, 3 * ADAPTER_RANK), MODEL_WIDTH ** -0.5, 0.125)
    adapter_query_weight = noise(splits[12], (ADAPTER_RANK, QUERY_HEADS * HEAD_FEATURES), (16 * ADAPTER_RANK) ** -0.5, 0.5, ((1, 4),))
    adapter_key_weight = noise(splits[13], (ADAPTER_RANK, KEY_VALUE_HEADS * HEAD_FEATURES), (16 * ADAPTER_RANK) ** -0.5, 0.5, ((1, 4),))
    adapter_value_weight = noise(splits[14], (ADAPTER_RANK, KEY_VALUE_HEADS * HEAD_FEATURES), (16 * ADAPTER_RANK) ** -0.5, 0.5, ((1, 4),))
    adapter_output_down = noise(splits[15], (QUERY_HEADS * HEAD_FEATURES, ADAPTER_RANK), HEAD_FEATURES ** -0.5, 0.75, ((0, 4),))
    adapter_output_up = noise(splits[16], (ADAPTER_RANK, MODEL_WIDTH), (4 * ADAPTER_RANK) ** -0.5, 1.0)
    hedgehog_query_weight = noise(splits[17], (QUERY_HEADS, HEAD_FEATURES, HEDGEHOG_OUTPUTS), (HEAD_FEATURES // 2) ** -0.5, 1.0, ((0, 4),))
    hedgehog_key_weight = noise(splits[18], (KEY_VALUE_HEADS, HEAD_FEATURES, HEDGEHOG_OUTPUTS), (HEAD_FEATURES // 2) ** -0.5, 1.0, ((0, 4),))
    document_index = draw_document_index(jax.random.fold_in(splits[20], 71), 0)
    return {"tokens": tokens, "cotangent": cotangent, "first_norm_gain": first_norm_gain, "second_norm_gain": second_norm_gain, "query_weight": query_weight, "key_weight": key_weight, "value_weight": value_weight, "output_weight": output_weight, "gate_weight": gate_weight, "up_weight": up_weight, "down_weight": down_weight, "adapter_down_weight": adapter_down_weight, "adapter_query_weight": adapter_query_weight, "adapter_key_weight": adapter_key_weight, "adapter_value_weight": adapter_value_weight, "adapter_output_down": adapter_output_down, "adapter_output_up": adapter_output_up, "hedgehog_query_weight": hedgehog_query_weight, "hedgehog_key_weight": hedgehog_key_weight, "document_index": document_index}


@jax.custom_vjp
def lowrank_part(v):
    return lax.optimization_barrier(v.astype(jnp.bfloat16)).astype(jnp.float32)

@jax.custom_vjp
def lowrank_backward(v):
    return v

def low_keep(v):
    return (lowrank_part(v), None)

def low_pass(kept, grad):
    return (grad,)

def back_keep(v):
    return (v, None)

def back_low(kept, grad):
    return (lowrank_part(grad),)
lowrank_part.defvjp(low_keep, low_pass)
lowrank_backward.defvjp(back_keep, back_low)
epsilon = 1e-05
rope_base = 500000.0
highest = lax.Precision.HIGHEST
adapter_scale = 2.0

def matrix_product(left, right):
    return jnp.matmul(left, right, precision=highest)

def rms_scale(values, gain):
    stat = lax.optimization_barrier(jnp.mean(values * values, axis=-1, keepdims=True))
    return values * lax.rsqrt(stat + epsilon) * gain

def rope_tables(sequence_length):
    inverse = rope_base ** (-jnp.arange(0, HEAD_FEATURES, 2, dtype=jnp.float32) / HEAD_FEATURES)
    angle = jnp.arange(sequence_length, dtype=jnp.float32)[:, None] * inverse[None, :]
    cosine_table = jnp.concatenate([jnp.cos(angle), jnp.cos(angle)], axis=-1)
    sine_table = jnp.concatenate([jnp.sin(angle), jnp.sin(angle)], axis=-1)
    return (cosine_table, sine_table)

def apply_rotation(values, cosine_table, sine_table):
    half = values.shape[-1] // 2
    swapped = jnp.concatenate([-values[..., half:], values[..., :half]], axis=-1)
    return values * cosine_table[:, None, :] + swapped * sine_table[:, None, :]

def feature_map(values, maps):
    projected = lowrank_backward(jnp.einsum('rthd,hdf->rthf', values, maps, precision=highest))
    both = jnp.concatenate([jax.nn.softmax(projected, axis=-1), jax.nn.softmax(-projected, axis=-1)], axis=-1)
    return lowrank_part(both)

def pad_front(values):
    zero_filled = jnp.zeros((values.shape[0], WIN) + values.shape[2:], values.dtype)
    return jnp.concatenate([zero_filled, values], axis=1)

def block_attention(query_rows, phiq, key, value_rows, phik, query_seg, key_seg, state, total, label):
    shard = query_rows.shape[1]
    span = key.shape[1]
    same = query_seg[:, :, None] == key_seg[:, None, :]
    row_pos = jnp.arange(shard)[:, None]
    col_pos = jnp.arange(span)[None, :]
    inside = (same & (col_pos > row_pos) & (col_pos <= row_pos + WIN))[:, None, None]
    older = (same & (col_pos <= row_pos))[:, None, None]
    scores = lowrank_backward(jnp.einsum('rigch,rjgh->rgcij', query_rows, key, precision=highest) * HEAD_FEATURES ** (-0.5))
    weights = jnp.where(inside, jnp.exp(scores), 0.0)
    num_window = lowrank_backward(jnp.einsum('rgcij,rjgh->rigch', lowrank_part(weights), value_rows, precision=highest))
    den_window = lax.optimization_barrier(jnp.sum(weights, axis=-1)).transpose(0, 3, 1, 2)
    kernel = jnp.where(older, jnp.einsum('rigcf,rjgf->rgcij', phiq, phik, precision=highest), 0.0)
    num_linear = jnp.einsum('rgcij,rjgh->rigch', kernel, value_rows, precision=highest)
    den_linear = lax.optimization_barrier(jnp.sum(kernel, axis=-1)).transpose(0, 3, 1, 2)
    reaches = (query_seg == label[:, None])[:, :, None, None]
    carried = jnp.einsum('rigcf,rgfh->rigch', phiq, state, precision=highest)
    num_linear = num_linear + jnp.where(reaches[..., None], carried, 0.0)
    carried_total = jnp.einsum('rigcf,rgf->rigc', phiq, total, precision=highest)
    den_linear = den_linear + jnp.where(reaches, carried_total, 0.0)
    return (num_window + num_linear) / (den_window + den_linear)[..., None]

def attend(query_rows, key, value_rows, hedgehog_query_weight, hedgehog_key_weight, document_labels):
    row_count, sequence_length = document_labels.shape
    head_group = QUERY_HEADS // KEY_VALUE_HEADS
    query_features = feature_map(query_rows, hedgehog_query_weight)
    phi_key = feature_map(key, hedgehog_key_weight)
    key_pad = pad_front(key)
    value_pad = pad_front(value_rows)
    phi_pad = pad_front(phi_key)
    seg_pad = jnp.concatenate([jnp.full((row_count, WIN), -1, jnp.int32), document_labels.astype(jnp.int32)], axis=1)

    def block_step(carry, start_offset):
        state, total, label = carry
        query_block_rows = lax.dynamic_slice_in_dim(query_rows, start_offset, SHARD_POSITIONS, 1).reshape(row_count, SHARD_POSITIONS, KEY_VALUE_HEADS, head_group, HEAD_FEATURES)
        block_query_features = lax.dynamic_slice_in_dim(query_features, start_offset, SHARD_POSITIONS, 1).reshape(row_count, SHARD_POSITIONS, KEY_VALUE_HEADS, head_group, FEATURE_SIZE)
        block_key = lax.dynamic_slice_in_dim(key_pad, start_offset, SHARD_POSITIONS + WIN, 1)
        block_value = lax.dynamic_slice_in_dim(value_pad, start_offset, SHARD_POSITIONS + WIN, 1)
        block_phik = lax.dynamic_slice_in_dim(phi_pad, start_offset, SHARD_POSITIONS + WIN, 1)
        key_seg = lax.dynamic_slice_in_dim(seg_pad, start_offset, SHARD_POSITIONS + WIN, 1)
        query_seg = key_seg[:, WIN:]
        output = block_attention(query_block_rows, block_query_features, block_key, block_value, block_phik, query_seg, key_seg, state, total, label)
        new_label = key_seg[:, SHARD_POSITIONS - 1]
        keep = (key_seg[:, :SHARD_POSITIONS] == new_label[:, None]).astype(jnp.float32)[:, :, None, None]
        kept_phi = block_phik[:, :SHARD_POSITIONS] * keep
        element_state = jnp.einsum('rjgf,rjgh->rgfh', kept_phi, block_value[:, :SHARD_POSITIONS], precision=highest)
        element_total = lax.optimization_barrier(jnp.sum(kept_phi, axis=1))
        joined = (label == new_label)[:, None, None]
        state = jnp.where(joined[..., None], state + element_state, element_state)
        total = jnp.where(joined, total + element_total, element_total)
        return ((state, total, new_label), output.reshape(row_count, SHARD_POSITIONS, QUERY_HEADS * HEAD_FEATURES))
    initial_value = (jnp.zeros((row_count, KEY_VALUE_HEADS, FEATURE_SIZE, HEAD_FEATURES), jnp.float32), jnp.zeros((row_count, KEY_VALUE_HEADS, FEATURE_SIZE), jnp.float32), jnp.full((row_count,), -1, jnp.int32))
    starts = (jnp.arange(sequence_length // SHARD_POSITIONS) * SHARD_POSITIONS).astype(jnp.int32)
    unused, outputs = lax.scan(jax.checkpoint(block_step), initial_value, starts)
    return outputs.transpose(1, 0, 2, 3).reshape(row_count, sequence_length, QUERY_HEADS * HEAD_FEATURES)

def forward_pass(tokens, first_norm_gain, second_norm_gain, query_weight, key_weight, value_weight, output_weight, gate_weight, up_weight, down_weight, adapter_down_weight, adapter_query_weight, adapter_key_weight, adapter_value_weight, adapter_output_down, adapter_output_up, hedgehog_query_weight, hedgehog_key_weight, document_labels):
    row_count, sequence_length, width = tokens.shape
    flattened = tokens.reshape(row_count * sequence_length, width)
    normalized_input = lowrank_part(rms_scale(flattened, first_norm_gain))
    lowrank_input = matrix_product(normalized_input, adapter_down_weight)
    query_rows = lowrank_backward(matrix_product(normalized_input, query_weight) + adapter_scale * matrix_product(lowrank_input[:, :ADAPTER_RANK], adapter_query_weight))
    key = lowrank_backward(matrix_product(normalized_input, key_weight) + adapter_scale * matrix_product(lowrank_input[:, ADAPTER_RANK:2 * ADAPTER_RANK], adapter_key_weight))
    value_rows = lowrank_backward(matrix_product(normalized_input, value_weight) + adapter_scale * matrix_product(lowrank_input[:, 2 * ADAPTER_RANK:], adapter_value_weight))
    cosine_table, sine_table = rope_tables(sequence_length)
    query_rows = lowrank_part(apply_rotation(query_rows.reshape(row_count, sequence_length, QUERY_HEADS, HEAD_FEATURES), cosine_table, sine_table))
    key = lowrank_part(apply_rotation(key.reshape(row_count, sequence_length, KEY_VALUE_HEADS, HEAD_FEATURES), cosine_table, sine_table))
    value_rows = lowrank_part(value_rows.reshape(row_count, sequence_length, KEY_VALUE_HEADS, HEAD_FEATURES))
    mixed = attend(query_rows, key, value_rows, hedgehog_query_weight, hedgehog_key_weight, document_labels)
    attention_result = lowrank_part(lowrank_backward(mixed)).reshape(row_count * sequence_length, QUERY_HEADS * HEAD_FEATURES)
    branch_output = lowrank_backward(matrix_product(attention_result, output_weight) + adapter_scale * matrix_product(matrix_product(attention_result, adapter_output_down), adapter_output_up))
    hidden_state = flattened + branch_output
    normed_two = lowrank_part(rms_scale(hidden_state, second_norm_gain))
    gate = lowrank_backward(matrix_product(normed_two, gate_weight))
    up = lowrank_backward(matrix_product(normed_two, up_weight))
    inner = lowrank_part(jax.nn.silu(gate) * up)
    result = hidden_state + matrix_product(inner, down_weight)
    return result.reshape(row_count, sequence_length, width)

def reference(tokens, cotangent, first_norm_gain, second_norm_gain, query_weight, key_weight, value_weight, output_weight, gate_weight, up_weight, down_weight, adapter_down_weight, adapter_query_weight, adapter_key_weight, adapter_value_weight, adapter_output_down, adapter_output_up, hedgehog_query_weight, hedgehog_key_weight, document_index):
    float_values = [element_item.astype(jnp.float32) for element_item in (tokens, first_norm_gain, second_norm_gain, query_weight, key_weight, value_weight, output_weight, gate_weight, up_weight, down_weight, adapter_down_weight, adapter_query_weight, adapter_key_weight, adapter_value_weight, adapter_output_down, adapter_output_up, hedgehog_query_weight, hedgehog_key_weight)]

    def wrapped(*params):
        return forward_pass(*params, document_index)
    result, pullback = jax.vjp(wrapped, *float_values)
    grads = pullback(cotangent.astype(jnp.float32))
    return (result.astype(jnp.bfloat16), grads[0], grads[1], grads[2], grads[3], grads[4], grads[5], grads[6], grads[7], grads[8], grads[9], grads[10], grads[11], grads[12], grads[13], grads[14], grads[15], grads[16], grads[17])
```

```python
import jax
import jax.numpy as jnp
from jax import lax
from jax.sharding import PartitionSpec as P

WIN = 64


epsilon = 1e-05
rope_base = 500000.0
highest = lax.Precision.HIGHEST
adapter_scale = 2.0


def shifted(block, axis, distance):
    devices = range(lax.axis_size(axis))
    route = [(i - distance, i) for i in devices if i - distance in devices]
    return lax.ppermute(block, axis, route)


def carried_in(value, axis, join, neutral):
    count, mine = (lax.axis_size(axis), lax.axis_index(axis))
    pieces = jax.tree.map(lambda part: lax.all_gather(part, axis), value)
    so_far = jax.tree.map(
        lambda part, zero: jnp.full_like(part, 0) + jnp.asarray(zero, part.dtype), value, neutral
    )

    def turn(position, so_far):
        longer = join(so_far, jax.tree.map(lambda part: part[position], pieces))
        return jax.tree.map(lambda new, old: jnp.where(position < mine, new, old), longer, so_far)

    return lax.fori_loop(0, count - 1, turn, so_far)


def carried_in_2(value, axis, join, neutral):
    count = lax.axis_size(axis)
    place = lax.axis_index(axis)
    ahead = count - 1 - place
    gathered = jax.tree.map(
        lambda a, kind: lax.all_gather(a.astype(kind), axis),
        value,
        (jnp.bfloat16, jnp.bfloat16, jnp.bfloat16),
    )
    state = jax.tree.map(lambda a, e: jnp.zeros_like(a) + jnp.asarray(e, a.dtype), value, neutral)

    def one(turn, state):
        source = count - 1 - turn
        return join(
            state,
            jax.tree.map(
                lambda a, own: lax.dynamic_index_in_dim(a, source, 0, False).astype(own.dtype),
                gathered,
                value,
            ),
        )

    return lax.fori_loop(0, ahead, one, state)


def precise_product(left, right):
    return jnp.matmul(left, right, precision=highest)


def forward_product(left, right):
    return jnp.dot(left, right, preferred_element_type=jnp.float32)


def left_dot(left, right):
    return lax.dot_general(
        left, right, (((0,), (0,)), ((), ())), preferred_element_type=jnp.float32
    )


def right_dot(left, right):
    return lax.dot_general(
        left, right, (((1,), (1,)), ((), ())), preferred_element_type=jnp.float32
    )


def rope_tables(positions, size):
    inverse = rope_base ** (-jnp.arange(0, size, 2, dtype=jnp.float32) / size)
    angle = positions.astype(jnp.float32)[:, None] * inverse[None, :]
    cosine_table = jnp.concatenate([jnp.cos(angle), jnp.cos(angle)], axis=-1)
    sine_table = jnp.concatenate([jnp.sin(angle), jnp.sin(angle)], axis=-1)
    return (cosine_table, sine_table)


def apply_rotation(values, cosine_table, sine_table):
    half = values.shape[-1] // 2
    swapped = jnp.concatenate([-values[..., half:], values[..., :half]], axis=-1)
    return values * cosine_table[:, None, :] + swapped * sine_table[:, None, :]


def unrotate(grads, cosine_table, sine_table):
    half = grads.shape[-1] // 2
    scaled = grads * sine_table[:, None, :]
    swapped = jnp.concatenate([scaled[..., half:], -scaled[..., :half]], axis=-1)
    return grads * cosine_table[:, None, :] + swapped


def feature_pair(projected):
    return (jax.nn.softmax(projected, axis=-1), jax.nn.softmax(-projected, axis=-1))


def feature_back(grads, plus, minus):
    half = plus.shape[-1]
    grad_plus = grads[..., :half]
    grad_minus = grads[..., half:]
    first = plus * (grad_plus - jnp.sum(grad_plus * plus, axis=-1, keepdims=True))
    second = minus * (grad_minus - jnp.sum(grad_minus * minus, axis=-1, keepdims=True))
    return first - second


def combine_states(earlier, later):
    state_a, total_a, label_a = earlier
    state_b, total_b, label_b = later
    empty = label_b < 0
    joined = label_a == label_b

    def choose(first, second):
        extra = (1,) * (first.ndim - 1)
        vacant = empty.reshape(empty.shape + extra)
        linked = joined.reshape(joined.shape + extra)
        return jnp.where(vacant, first, jnp.where(linked, first + second, second))

    return (choose(state_a, state_b), choose(total_a, total_b), jnp.where(empty, label_a, label_b))


def ring_tables(count):
    order = list(range(0, count, 2)) + list(range(count - 1, 0, -2))
    place = [order.index(i) for i in range(count)]
    return order, place


def ring_move(block, step):
    order, _ = ring_tables(lax.axis_size("seq"))
    count = len(order)
    return lax.ppermute(block, "seq", [(order[i], order[(i + step) % count]) for i in range(count)])


def ring_index(offset):
    order, place = ring_tables(lax.axis_size("seq"))
    mine = jnp.asarray(place, jnp.int32)[lax.axis_index("seq")]
    return jnp.asarray(order, jnp.int32)[(mine + offset) % len(order)]


def after(value, *others):
    return lax.optimization_barrier((value,) + others)[0]


def ring_gather(own):
    half = lax.axis_size("seq") // 2
    found = {0: own}
    up = down = own
    for step in range(1, half):
        up, down = ring_move(up, 1), ring_move(down, -1)
        found[-step], found[step] = up, down
    cut = own.shape[0] // 2
    found[half] = (ring_move(up[:cut], 1), ring_move(down[cut:], -1))
    return found


def assemble(found, first, last):
    count = lax.axis_size("seq")
    rows = found[0].shape[0]
    whole = jnp.zeros((count * rows, last - first), found[0].dtype)
    for offset, block in found.items():
        at = ring_index(offset) * rows
        if isinstance(block, tuple):
            for part in block:
                whole = lax.dynamic_update_slice(whole, part[:, first:last], (at, 0))
                at = at + part.shape[0]
        else:
            whole = lax.dynamic_update_slice(whole, block[:, first:last], (at, 0))
    return whole


def ring_scatter(grads, rows):
    half = lax.axis_size("seq") // 2
    cut = rows // 2

    def own(offset):
        at = ring_index(offset) * rows
        return jnp.concatenate(
            [lax.dynamic_slice_in_dim(part, at, rows, 0) for part in grads], axis=1
        )

    far = own(half)
    up, down = ring_move(far[:cut], 1), ring_move(far[cut:], -1)
    for step in range(half - 1, 0, -1):
        above, below = own(step), own(-step)
        if step == half - 1:
            up = jnp.concatenate([above[:cut] + up, above[cut:]], axis=0)
            down = jnp.concatenate([below[:cut], below[cut:] + down], axis=0)
        else:
            up, down = above + up, below + down
        up, down = ring_move(up, 1), ring_move(down, -1)
    mine = own(0).astype(jnp.float32)
    return mine + up.astype(jnp.float32) + down.astype(jnp.float32)


def core_swap(block):
    count = lax.axis_size("head")
    return lax.ppermute(block, "head", [(i, i ^ 1) for i in range(count)])


def chip_move(block, step):
    count = lax.axis_size("head")
    return lax.ppermute(block, "head", [(i, (i + 2 * step) % count) for i in range(count)])


def head_scatter(part):
    chips = lax.axis_size("head") // 2
    place = lax.axis_index("head")
    chip, core = place // 2, place % 2
    rows = part.shape[0] // (2 * chips)
    split = part.reshape(chips, 2, rows, part.shape[1])
    theirs = core_swap(lax.dynamic_index_in_dim(split, 1 - core, 1, False))
    both = lax.dynamic_index_in_dim(split, core, 1, False).astype(jnp.float32) + theirs
    total = lax.dynamic_index_in_dim(both, chip, 0, False)
    for step in range(1, chips):
        sent = lax.dynamic_index_in_dim(both, (chip + step) % chips, 0, False)
        total = total + chip_move(sent.astype(part.dtype), step)
    return total


def head_gather(own):
    chips = lax.axis_size("head") // 2
    place = lax.axis_index("head")
    chip, core = place // 2, place % 2
    whole = jnp.zeros((2 * chips,) + own.shape, own.dtype)
    for step in range(chips):
        block = chip_move(own, step) if step else own
        at = 2 * ((chip - step + chips) % chips)
        whole = lax.dynamic_update_index_in_dim(whole, block, at + core, 0)
        whole = lax.dynamic_update_index_in_dim(whole, core_swap(block), at + 1 - core, 0)
    return whole.reshape((2 * chips * own.shape[0],) + own.shape[1:])


MLP_CHUNKS = 4


def body(
    tokens,
    cotangent,
    first_norm_gain,
    second_norm_gain,
    query_weight,
    key_weight,
    value_weight,
    output_weight,
    gate_weight,
    up_weight,
    down_weight,
    adapter_down_weight,
    adapter_query_weight,
    adapter_key_weight,
    adapter_value_weight,
    adapter_output_down,
    adapter_output_up,
    hedgehog_query_weight,
    hedgehog_key_weight,
    document_index,
):
    row_count, shard, width = tokens.shape
    window = WIN
    seq_index = lax.axis_index("seq")
    heads_here = hedgehog_query_weight.shape[0]
    kv_here = hedgehog_key_weight.shape[0]
    head_group = heads_here // kv_here
    size = hedgehog_query_weight.shape[1]
    adapter_rank = adapter_query_weight.shape[0]
    tokens_here = row_count * shard
    block_rows = query_weight.shape[0]
    hidden_units = gate_weight.shape[1]
    chunk = hidden_units // MLP_CHUNKS
    down_turned = down_weight.T
    qkv_found = ring_gather(jnp.concatenate([query_weight, key_weight, value_weight], axis=1))
    query_width, key_width = query_weight.shape[1], key_weight.shape[1]
    out_found = ring_gather(after(output_weight.T, qkv_found[1]))
    mlp_found = []
    earlier = out_found[1]
    for turn in range(MLP_CHUNKS):
        span = slice(turn * chunk, (turn + 1) * chunk)
        payload = jnp.concatenate(
            [gate_weight[:, span], up_weight[:, span], down_turned[:, span]], axis=1
        )
        mlp_found.append(ring_gather(after(payload, earlier)))
        earlier = mlp_found[-1][2]
    complete_qkv = assemble(qkv_found, 0, query_width + 2 * key_width)
    out_turned = assemble(out_found, 0, output_weight.shape[0])
    adapters = jnp.zeros((3 * adapter_rank, query_width + 2 * key_width), jnp.bfloat16)
    adapters = lax.dynamic_update_slice(adapters, adapter_query_weight, (0, 0))
    adapters = lax.dynamic_update_slice(adapters, adapter_key_weight, (adapter_rank, query_width))
    adapters = lax.dynamic_update_slice(
        adapters, adapter_value_weight, (2 * adapter_rank, query_width + key_width)
    )
    flattened = tokens.reshape(tokens_here, width).astype(jnp.float32)
    scale_one = lax.rsqrt(jnp.mean(flattened * flattened, axis=-1, keepdims=True) + epsilon)
    unit_one = flattened * scale_one
    normalized_input = (unit_one * first_norm_gain.astype(jnp.float32)).astype(jnp.bfloat16)
    lowrank_input = forward_product(normalized_input, adapter_down_weight)
    lowrank_low = lowrank_input.astype(jnp.bfloat16)
    linear = forward_product(normalized_input, complete_qkv) + adapter_scale * forward_product(
        lowrank_low, adapters
    )
    query_linear = linear[:, :query_width]
    key_linear = linear[:, query_width : query_width + key_width]
    value_linear = linear[:, query_width + key_width :]
    positions = seq_index * shard + jnp.arange(shard)
    cosine_table, sine_table = rope_tables(positions, size)
    query_rot = apply_rotation(
        query_linear.reshape(row_count, shard, heads_here, size), cosine_table, sine_table
    ).astype(jnp.bfloat16)
    key_rot = apply_rotation(
        key_linear.reshape(row_count, shard, kv_here, size), cosine_table, sine_table
    ).astype(jnp.bfloat16)
    value_low = value_linear.reshape(row_count, shard, kv_here, size).astype(jnp.bfloat16)
    query_plus, query_minus = feature_pair(
        jnp.einsum(
            "rthd,hdf->rthf", query_rot, hedgehog_query_weight, preferred_element_type=jnp.float32
        )
    )
    key_plus, key_minus = feature_pair(
        jnp.einsum(
            "rthd,hdf->rthf", key_rot, hedgehog_key_weight, preferred_element_type=jnp.float32
        )
    )
    query_features = jnp.concatenate([query_plus, query_minus], axis=-1).astype(jnp.bfloat16)
    phi_key = jnp.concatenate([key_plus, key_minus], axis=-1).astype(jnp.bfloat16)
    tails = (
        key_rot[:, shard - window :],
        value_low[:, shard - window :],
        phi_key[:, shard - window :],
    )
    halo_key, halo_value, halo_phi = shifted((tails[0], tails[1], tails[2]), "seq", 1)
    all_key = jnp.concatenate([halo_key, key_rot], axis=1)
    all_value = jnp.concatenate([halo_value, value_low], axis=1)
    all_phi = jnp.concatenate([halo_phi, phi_key], axis=1)
    padded_seg = jnp.concatenate(
        [jnp.full((row_count, window), -1, jnp.int32), document_index], axis=1
    )
    key_seg = lax.dynamic_slice_in_dim(padded_seg, seq_index * shard, shard + window, 1)
    query_seg = key_seg[:, window:]
    label_here = key_seg[:, shard - 1].astype(jnp.float32)
    keep = key_seg[:, :shard] == key_seg[:, shard - 1 : shard]
    kept_phi = all_phi[:, :shard] * keep[:, :, None, None].astype(jnp.bfloat16)
    element_state = jnp.einsum(
        "rjgf,rjgh->rgfh", kept_phi, all_value[:, :shard], preferred_element_type=jnp.float32
    )
    element_total = jnp.sum(kept_phi.astype(jnp.float32), axis=1)
    identity = (
        jnp.zeros_like(element_state),
        jnp.zeros_like(element_total),
        jnp.full_like(label_here, -1.0),
    )
    carry_state, carry_total, carry_label = carried_in(
        (element_state, element_total, label_here), "seq", combine_states, identity
    )
    query_grouped = query_rot.reshape(row_count, shard, kv_here, head_group, size)
    phi_grouped = query_features.reshape(
        row_count, shard, kv_here, head_group, query_features.shape[-1]
    )
    same = query_seg[:, :, None] == key_seg[:, None, :]
    row_pos = jnp.arange(shard)[:, None]
    col_pos = jnp.arange(shard + window)[None, :]
    inside = (same & (col_pos > row_pos) & (col_pos <= row_pos + window))[:, None, None]
    older = (same & (col_pos <= row_pos))[:, None, None]
    factor = size ** (-0.5)
    scores = (
        jnp.einsum("rigch,rjgh->rgcij", query_grouped, all_key, preferred_element_type=jnp.float32)
        * factor
    )
    near_weight = jnp.where(inside, jnp.exp(scores), 0.0)
    probs = near_weight.astype(jnp.bfloat16)
    num_window = jnp.einsum(
        "rgcij,rjgh->rigch", probs, all_value, preferred_element_type=jnp.float32
    )
    den_window = jnp.sum(near_weight, axis=-1).transpose(0, 3, 1, 2)
    kernel = jnp.where(
        older,
        jnp.einsum("rigcf,rjgf->rgcij", phi_grouped, all_phi, preferred_element_type=jnp.float32),
        0.0,
    )
    value_wide = all_value
    phi_wide = phi_grouped.astype(jnp.float32)
    num_linear = jnp.einsum("rgcij,rjgh->rigch", kernel, value_wide, preferred_element_type=jnp.float32)
    den_linear = jnp.sum(kernel, axis=-1).transpose(0, 3, 1, 2)
    reaches = (query_seg.astype(jnp.float32) == carry_label[:, None])[:, :, None, None]
    carried = jnp.einsum("rigcf,rgfh->rigch", phi_wide, carry_state, preferred_element_type=jnp.float32)
    num_linear = num_linear + jnp.where(reaches[..., None], carried, 0.0)
    carried_total = jnp.einsum("rigcf,rgf->rigc", phi_wide, carry_total, preferred_element_type=jnp.float32)
    den_linear = den_linear + jnp.where(reaches, carried_total, 0.0)
    denominator = den_window + den_linear
    mixed = (num_window + num_linear) / denominator[..., None]
    attention_result = mixed.astype(jnp.bfloat16).reshape(tokens_here, heads_here * size)
    lowrank_output = forward_product(attention_result, adapter_output_down)
    out_part = right_dot(attention_result, out_turned) + adapter_scale * forward_product(
        lowrank_output.astype(jnp.bfloat16), adapter_output_up
    )
    own_rows = row_count // lax.axis_size("head")
    first_row = lax.axis_index("head") * own_rows
    own_tokens = lax.dynamic_slice_in_dim(tokens, first_row, own_rows, 0)
    own_tokens = own_tokens.reshape(own_rows * shard, width).astype(jnp.float32)
    own_cotangent = lax.dynamic_slice_in_dim(cotangent, first_row, own_rows, 0)
    own_cotangent = own_cotangent.reshape(own_rows * shard, width).astype(jnp.float32)
    hidden_state = own_tokens + head_scatter(out_part.astype(jnp.bfloat16))
    scale_two = lax.rsqrt(jnp.mean(hidden_state * hidden_state, axis=-1, keepdims=True) + epsilon)
    unit_two = hidden_state * scale_two
    own_normed = (unit_two * second_norm_gain.astype(jnp.float32)).astype(jnp.bfloat16)
    normed_rows = head_gather(own_normed)
    grad_out = cotangent.reshape(tokens_here, width)
    down_part, normed_two_part = 0.0, 0.0
    mlp_sums = []
    for found in mlp_found:
        gate_up_weight = assemble(found, 0, 2 * chunk)
        down_chunk = assemble(found, 2 * chunk, 3 * chunk)
        grad_inner = forward_product(grad_out, down_chunk)
        gate_up = forward_product(normed_rows, gate_up_weight)
        gate, up = gate_up[:, :chunk], gate_up[:, chunk:]
        sigmoid_gate = jax.nn.sigmoid(gate)
        swish = gate * sigmoid_gate
        inner = (swish * up).astype(jnp.bfloat16)
        grad_gate = grad_inner * up * sigmoid_gate * (1.0 + gate * (1.0 - sigmoid_gate))
        grad_gate_up = jnp.concatenate([grad_gate, grad_inner * swish], axis=1).astype(jnp.bfloat16)
        normed_two_part = normed_two_part + right_dot(grad_gate_up, gate_up_weight)
        down_part = down_part + right_dot(inner, down_chunk)
        grad_w_gate_up = left_dot(normed_rows, grad_gate_up).astype(jnp.bfloat16)
        grad_w_down = left_dot(grad_out, inner).astype(jnp.bfloat16)
        mlp_sums.append(ring_scatter([grad_w_gate_up, grad_w_down], block_rows))
    grad_normed_two = head_scatter(normed_two_part.astype(jnp.bfloat16))
    layer_rows = head_gather(
        (hidden_state + head_scatter(down_part.astype(jnp.bfloat16))).astype(jnp.bfloat16)
    )
    grad_gain_two = jnp.sum(grad_normed_two * unit_two, axis=0)
    inner_two = grad_normed_two * second_norm_gain.astype(jnp.float32)
    grad_hidden = own_cotangent + scale_two * (
        inner_two - unit_two * jnp.mean(inner_two * unit_two, axis=-1, keepdims=True)
    )
    branch_gradient_rows = head_gather(grad_hidden.astype(jnp.bfloat16))
    adapter_output_up_gradient = adapter_scale * left_dot(
        lowrank_output.astype(jnp.bfloat16), branch_gradient_rows
    )
    grad_w_out = left_dot(branch_gradient_rows, attention_result).astype(jnp.bfloat16)
    lowrank_output_gradient = adapter_scale * right_dot(branch_gradient_rows, adapter_output_up)
    lowrank_output_gradient = lowrank_output_gradient.astype(jnp.bfloat16)
    adapter_output_down_gradient = left_dot(attention_result, lowrank_output_gradient)
    grad_attended = forward_product(branch_gradient_rows, out_turned) + right_dot(
        lowrank_output_gradient, adapter_output_down
    )
    grad_mixed = (
        grad_attended.astype(jnp.bfloat16)
        .astype(jnp.float32)
        .reshape(row_count, shard, kv_here, head_group, size)
    )
    grad_num = grad_mixed / denominator[..., None]
    grad_den = -jnp.sum(grad_mixed * mixed, axis=-1) / denominator
    grad_near = grad_num.astype(jnp.bfloat16)
    grad_den_cols = grad_den.transpose(0, 2, 3, 1)[..., None]
    grad_probs = jnp.einsum(
        "rigch,rjgh->rgcij", grad_near, all_value, preferred_element_type=jnp.float32
    )
    grad_value_all = jnp.einsum(
        "rgcij,rigch->rjgh", probs, grad_near, preferred_element_type=jnp.float32
    )
    grad_scores = ((grad_probs + grad_den_cols) * near_weight).astype(jnp.bfloat16)
    grad_query_att = (
        jnp.einsum("rgcij,rjgh->rigch", grad_scores, all_key, preferred_element_type=jnp.float32)
        * factor
    )
    grad_key_all = (
        jnp.einsum(
            "rgcij,rigch->rjgh", grad_scores, query_grouped, preferred_element_type=jnp.float32
        )
        * factor
    )
    grad_kernel = jnp.where(
        older,
        jnp.einsum("rigch,rjgh->rgcij", grad_num, value_wide, preferred_element_type=jnp.float32) + grad_den_cols,
        0.0,
    )
    grad_value_all = grad_value_all + jnp.einsum(
        "rgcij,rigch->rjgh", kernel, grad_num, preferred_element_type=jnp.float32
    )
    grad_phi_q = jnp.einsum(
        "rgcij,rjgf->rigcf", grad_kernel, all_phi.astype(jnp.float32), preferred_element_type=jnp.float32
    )
    grad_phi_all = jnp.einsum("rgcij,rigcf->rjgf", grad_kernel, phi_wide, preferred_element_type=jnp.float32)
    masked_num = jnp.where(reaches[..., None], grad_num, 0.0)
    masked_den = jnp.where(reaches, grad_den, 0.0)
    grad_phi_q = grad_phi_q + jnp.einsum(
        "rigch,rgfh->rigcf", masked_num, carry_state, preferred_element_type=jnp.float32
    )
    grad_phi_q = grad_phi_q + masked_den[..., None] * carry_total[:, None, :, None, :]
    grad_carry_state = jnp.einsum("rigcf,rigch->rgfh", phi_wide, masked_num, preferred_element_type=jnp.float32)
    grad_carry_total = jnp.einsum("rigcf,rigc->rgf", phi_wide, masked_den, preferred_element_type=jnp.float32)
    back_identity = (
        jnp.zeros_like(grad_carry_state),
        jnp.zeros_like(grad_carry_total),
        jnp.full_like(carry_label, -1.0),
    )
    grad_element_state, grad_element_total, unused = carried_in_2(
        (grad_carry_state, grad_carry_total, carry_label), "seq", combine_states, back_identity
    )
    keep_wide = keep[:, :, None, None].astype(jnp.float32)
    element_phi = keep_wide * (
        jnp.einsum("rjgh,rgfh->rjgf", value_wide[:, :shard], grad_element_state, preferred_element_type=jnp.float32)
        + grad_element_total[:, None]
    )
    element_value = keep_wide * jnp.einsum(
        "rjgf,rgfh->rjgh",
        all_phi[:, :shard].astype(jnp.float32),
        grad_element_state,
        preferred_element_type=jnp.float32,
    )
    grad_phi_all = grad_phi_all + jnp.concatenate(
        [element_phi, jnp.zeros_like(element_phi[:, :window])], axis=1
    )
    grad_value_all = grad_value_all + jnp.concatenate(
        [element_value, jnp.zeros_like(element_value[:, :window])], axis=1
    )
    sent = (grad_key_all[:, :window], grad_value_all[:, :window], grad_phi_all[:, :window])
    back_key, back_value, back_phi = (
        shifted(sent[0].astype(jnp.bfloat16), "seq", -1).astype(jnp.float32),
        shifted(sent[1].astype(jnp.bfloat16), "seq", -1).astype(jnp.float32),
        shifted(sent[2].astype(jnp.bfloat16), "seq", -1).astype(jnp.float32),
    )

    def own(grads_all, returned):
        filler = jnp.zeros((row_count, shard - window) + returned.shape[2:], jnp.float32)
        return grads_all[:, window:] + jnp.concatenate([filler, returned], axis=1)

    grad_key_rot = own(grad_key_all, back_key)
    grad_value_rot = own(grad_value_all, back_value)
    grad_phi_key = own(grad_phi_all, back_phi)
    grad_proj_q = feature_back(
        grad_phi_q.reshape(row_count, shard, heads_here, query_features.shape[-1]),
        query_plus,
        query_minus,
    ).astype(jnp.bfloat16)
    grad_proj_k = feature_back(grad_phi_key, key_plus, key_minus).astype(jnp.bfloat16)
    grad_query_rot = grad_query_att.reshape(row_count, shard, heads_here, size) + jnp.einsum(
        "rthf,hdf->rthd", grad_proj_q, hedgehog_query_weight, preferred_element_type=jnp.float32
    )
    grad_key_rot = grad_key_rot + jnp.einsum(
        "rthf,hdf->rthd", grad_proj_k, hedgehog_key_weight, preferred_element_type=jnp.float32
    )
    grad_map_query = jnp.einsum(
        "rthd,rthf->hdf", query_rot, grad_proj_q, preferred_element_type=jnp.float32
    )
    grad_map_key = jnp.einsum(
        "rthd,rthf->hdf", key_rot, grad_proj_k, preferred_element_type=jnp.float32
    )
    grad_query_lin = (
        unrotate(grad_query_rot, cosine_table, sine_table)
        .astype(jnp.bfloat16)
        .reshape(tokens_here, heads_here * size)
    )
    grad_key_lin = (
        unrotate(grad_key_rot, cosine_table, sine_table)
        .astype(jnp.bfloat16)
        .reshape(tokens_here, kv_here * size)
    )
    grad_value_lin = grad_value_rot.astype(jnp.bfloat16).reshape(tokens_here, kv_here * size)
    grad_linear = jnp.concatenate([grad_query_lin, grad_key_lin, grad_value_lin], axis=1)
    grad_w_qkv = left_dot(normalized_input, grad_linear).astype(jnp.bfloat16)
    adapter_gradient = adapter_scale * left_dot(lowrank_low, grad_linear)
    lowrank_gradient = (adapter_scale * right_dot(grad_linear, adapters)).astype(jnp.bfloat16)
    normed_part = right_dot(grad_linear, complete_qkv) + right_dot(
        lowrank_gradient, adapter_down_weight
    )
    adapter_down_gradient = left_dot(normalized_input, lowrank_gradient)
    normalized_gradient = head_scatter(normed_part.astype(jnp.bfloat16))
    own_scale = lax.rsqrt(jnp.mean(own_tokens * own_tokens, axis=-1, keepdims=True) + epsilon)
    own_unit = own_tokens * own_scale
    grad_gain_one = jnp.sum(normalized_gradient * own_unit, axis=0)
    inner_one = normalized_gradient * first_norm_gain.astype(jnp.float32)
    own_grad_tokens = grad_hidden + own_scale * (
        inner_one - own_unit * jnp.mean(inner_one * own_unit, axis=-1, keepdims=True)
    )
    grad_tokens_rows = head_gather(own_grad_tokens.astype(jnp.bfloat16)).astype(jnp.float32)
    out_sum = ring_scatter([grad_w_out], block_rows)
    qkv_sum = ring_scatter([grad_w_qkv], block_rows)
    query_adapter_sum = adapter_gradient[:adapter_rank, :query_width]
    key_adapter_sum = adapter_gradient[
        adapter_rank : 2 * adapter_rank, query_width : query_width + key_width
    ]
    value_adapter_sum = adapter_gradient[2 * adapter_rank :, query_width + key_width :]
    everywhere = (grad_gain_one, grad_gain_two, adapter_down_gradient, adapter_output_up_gradient)
    everywhere = jax.tree.map(
        lambda part: lax.psum(part.astype(jnp.bfloat16), ("seq", "head")).astype(jnp.float32),
        everywhere,
    )
    along = (
        query_adapter_sum,
        key_adapter_sum,
        value_adapter_sum,
        adapter_output_down_gradient,
        grad_map_query,
        grad_map_key,
    )
    along = jax.tree.map(
        lambda part: lax.psum(part.astype(jnp.bfloat16), "seq").astype(jnp.float32), along
    )
    grad_gate_sum = jnp.concatenate([part[:, :chunk] for part in mlp_sums], axis=1)
    grad_up_sum = jnp.concatenate([part[:, chunk : 2 * chunk] for part in mlp_sums], axis=1)
    grad_down_sum = jnp.concatenate([part[:, 2 * chunk :].T for part in mlp_sums], axis=0)
    return (
        layer_rows.reshape(row_count, shard, width),
        grad_tokens_rows.reshape(row_count, shard, width),
        everywhere[0],
        everywhere[1],
        qkv_sum[:, :query_width],
        qkv_sum[:, query_width : query_width + key_width],
        qkv_sum[:, query_width + key_width :],
        out_sum.T,
        grad_gate_sum,
        grad_up_sum,
        grad_down_sum,
        everywhere[2],
        along[0],
        along[1],
        along[2],
        along[3],
        everywhere[3],
        along[4],
        along[5],
    )


def solution(mesh):
    in_specs = (
        P(None, "seq", None),
        P(None, "seq", None),
        P(),
        P(),
        P("seq", "head"),
        P("seq", "head"),
        P("seq", "head"),
        P("head", "seq"),
        P("seq", "head"),
        P("seq", "head"),
        P("head", "seq"),
        P(),
        P(None, "head"),
        P(None, "head"),
        P(None, "head"),
        P("head", None),
        P(),
        P("head", None, None),
        P("head", None, None),
        P(),
    )
    out_specs = (
        P(None, "seq", None),
        P(None, "seq", None),
        P(),
        P(),
        P("seq", "head"),
        P("seq", "head"),
        P("seq", "head"),
        P("head", "seq"),
        P("seq", "head"),
        P("seq", "head"),
        P("head", "seq"),
        P(),
        P(None, "head"),
        P(None, "head"),
        P(None, "head"),
        P("head", None),
        P(),
        P("head", None, None),
        P("head", None, None),
    )
    return jax.shard_map(body, mesh=mesh, in_specs=in_specs, out_specs=out_specs, check_vma=False)
```

```python
import functools

import jax
import jax.numpy as jnp
from jax import lax
from jax.experimental import pallas as pl
from jax.experimental.pallas import tpu as pltpu
from jax.sharding import PartitionSpec as P

WIN = 64
LANES = 128
STATE_ROWS = 80
MLP_CHUNKS = 2

epsilon = 1e-05
rope_base = 500000.0
adapter_scale = 2.0


def forward_product(left, right):
    return jnp.dot(left, right, preferred_element_type=jnp.float32)


def left_dot(left, right):
    return lax.dot_general(
        left, right, (((0,), (0,)), ((), ())), preferred_element_type=jnp.float32
    )


def right_dot(left, right):
    return lax.dot_general(
        left, right, (((1,), (1,)), ((), ())), preferred_element_type=jnp.float32
    )


def shifted(block, distance):
    devices = range(lax.axis_size("seq"))
    route = [(i - distance, i) for i in devices if i - distance in devices]
    return lax.ppermute(block, "seq", route)


def ring_order(count):
    return list(range(0, count, 2)) + list(range(count - 1, 0, -2))


def ring_move(block, step):
    order = ring_order(lax.axis_size("seq"))
    count = len(order)
    return lax.ppermute(block, "seq", [(order[i], order[(i + step) % count]) for i in range(count)])


def ring_index(offset):
    count = lax.axis_size("seq")
    mine = lax.axis_index("seq")
    place = jnp.where(mine % 2 == 0, mine // 2, count - 1 - mine // 2)
    there = (place + offset + count) % count
    return jnp.where(there < count // 2, 2 * there, 2 * (count - 1 - there) + 1)


def after(value, *others):
    return lax.optimization_barrier((value,) + others)[0]


class Gather:
    def __init__(self, own):
        self.half = lax.axis_size("seq") // 2
        self.found = {0: own}
        self.up = self.down = own
        self.step = 0

    def advance(self, *gates, quarters=1):
        for _ in range(quarters * max(1, self.half // 4)):
            if self.step == self.half:
                return
            self.step += 1
            cut = self.up.shape[0] // 2
            up, down = self.up, self.down
            if gates:
                up, down = after(up, *gates), after(down, *gates)
            if self.step < self.half:
                self.up, self.down = ring_move(up, 1), ring_move(down, -1)
                self.found[-self.step], self.found[self.step] = self.up, self.down
            else:
                self.found[self.half] = (ring_move(up[:cut], 1), ring_move(down[cut:], -1))

    def edge(self):
        return self.up, self.down

    def assemble(self, *widths):
        self.advance(quarters=4)
        count = lax.axis_size("seq")
        rows = self.found[0].shape[0]
        offsets = sorted(self.found)
        places = jnp.stack([ring_index(offset) * rows for offset in offsets]).astype(jnp.int32)
        pieces, origins = [], []
        for at, offset in enumerate(offsets):
            block, shift = self.found[offset], 0
            for part in block if isinstance(block, tuple) else (block,):
                pieces.append(part)
                origins.append((at, shift))
                shift += part.shape[0]
        starts = [sum(widths[:i]) for i in range(len(widths))]

        def kernel(places_ref, *refs):
            sources, rest = refs[: len(pieces)], refs[len(pieces) :]
            targets, buffers, semaphores = rest[: len(widths)], rest[len(widths) : -1], rest[-1]
            inward, outward = [], []
            for turn, (source, (at, shift)) in enumerate(zip(sources, origins, strict=True)):
                length = source.shape[0]
                held = buffers[turn]
                inward.append(pltpu.make_async_copy(source, held, semaphores.at[turn]))
                first = pl.multiple_of(places_ref[at] + shift, length)
                for target, start, width in zip(targets, starts, widths, strict=True):
                    outward.append(
                        pltpu.make_async_copy(
                            held.at[:, pl.ds(start, width)],
                            target.at[pl.ds(first, length), :],
                            semaphores.at[len(sources) + len(outward)],
                        )
                    )
            for copy in inward:
                copy.start()
            for turn, copy in enumerate(inward):
                copy.wait()
                for back in outward[turn * len(widths) : (turn + 1) * len(widths)]:
                    back.start()
            for copy in outward:
                copy.wait()

        anywhere = pl.BlockSpec(memory_space=pl.ANY)
        size = sum(piece.size for piece in pieces) * 2
        return pl.pallas_call(
            kernel,
            grid_spec=pltpu.PrefetchScalarGridSpec(
                num_scalar_prefetch=1,
                grid=(1,),
                in_specs=[anywhere] * len(pieces),
                out_specs=[anywhere] * len(widths),
                scratch_shapes=[pltpu.VMEM(piece.shape, piece.dtype) for piece in pieces]
                + [pltpu.SemaphoreType.DMA((len(pieces) * (1 + len(widths)),))],
            ),
            out_shape=[
                jax.ShapeDtypeStruct((count * rows, width), pieces[0].dtype) for width in widths
            ],
            compiler_params=pltpu.CompilerParams(vmem_limit_bytes=size + 4 * 1024 * 1024),
            cost_estimate=told(1 + size // 4_000_000),
            name="assemble",
        )(places, *pieces)


class Scatter:
    def __init__(self, grads, rows):
        self.grads, self.rows = grads, rows
        self.half = lax.axis_size("seq") // 2
        self.step = 0

    def own(self, offset):
        at = ring_index(offset) * self.rows
        parts = [lax.dynamic_slice_in_dim(part, at, self.rows, 0) for part in self.grads]
        return parts[0] if len(parts) == 1 else jnp.concatenate(parts, axis=1)

    def advance(self, *gates, quarters=1):
        for _ in range(quarters * max(1, self.half // 4)):
            if self.step == self.half:
                return
            self.step += 1
            offset = self.half - self.step + 1
            cut = self.rows // 2
            if self.step == 1:
                far = self.own(offset)
                up, down = far[:cut], far[cut:]
            else:
                above, below = self.own(offset), self.own(-offset)
                if self.step == 2:
                    up = jnp.concatenate([above[:cut] + self.up, above[cut:]], axis=0)
                    down = jnp.concatenate([below[:cut], below[cut:] + self.down], axis=0)
                else:
                    up, down = above + self.up, below + self.down
            if gates:
                up, down = after(up, *gates), after(down, *gates)
            self.up, self.down = ring_move(up, 1), ring_move(down, -1)

    def edge(self):
        return self.up, self.down

    def total(self):
        self.advance(quarters=4)
        mine = self.own(0).astype(jnp.float32)
        return mine + self.up.astype(jnp.float32) + self.down.astype(jnp.float32)


def core_swap(block):
    count = lax.axis_size("head")
    return lax.ppermute(block, "head", [(i, i ^ 1) for i in range(count)])


def chip_move(block, step):
    count = lax.axis_size("head")
    return lax.ppermute(block, "head", [(i, (i + 2 * step) % count) for i in range(count)])


def head_pair_sum(part):
    chips = lax.axis_size("head") // 2
    core = lax.axis_index("head") % 2
    rows = part.shape[0] // (2 * chips)
    split = part.reshape(chips, 2, rows, part.shape[1])
    theirs = core_swap(lax.dynamic_index_in_dim(split, 1 - core, 1, False))
    return lax.dynamic_index_in_dim(split, core, 1, False).astype(jnp.float32) + theirs


def head_finish(both, *gates):
    chips = lax.axis_size("head") // 2
    chip = lax.axis_index("head") // 2
    total = lax.dynamic_index_in_dim(both, chip, 0, False)
    for step in range(1, chips):
        sent = lax.dynamic_index_in_dim(both, (chip + step) % chips, 0, False)
        sent = sent.astype(jnp.bfloat16)
        total = total + chip_move(after(sent, *gates) if gates else sent, step)
    return total


def head_scatter(part):
    return head_finish(head_pair_sum(part))


def head_gather(own):
    chips = lax.axis_size("head") // 2
    place = lax.axis_index("head")
    chip, core = place // 2, place % 2
    whole = jnp.zeros((2 * chips,) + own.shape, own.dtype)
    for step in range(chips):
        block = chip_move(own, step) if step else own
        at = 2 * ((chip - step + chips) % chips)
        whole = lax.dynamic_update_index_in_dim(whole, block, at + core, 0)
        whole = lax.dynamic_update_index_in_dim(whole, core_swap(block), at + 1 - core, 0)
    return whole.reshape((2 * chips * own.shape[0],) + own.shape[1:])


def exchange_sum(block, axis, bits):
    devices = range(lax.axis_size(axis))
    block = block.astype(jnp.bfloat16)
    for bit in bits:
        other = lax.ppermute(block, axis, [(i, i ^ bit) for i in devices])
        block = (block.astype(jnp.float32) + other.astype(jnp.float32)).astype(jnp.bfloat16)
    return block


def bits_of(axis):
    bits, bit = [], 1
    while bit < lax.axis_size(axis):
        bits.append(bit)
        bit *= 2
    return bits


def lane_of(shape):
    return lax.broadcasted_iota(jnp.int32, shape, 1)


def rolled(values, shift):
    return pltpu.roll(values, shift % LANES, 1)


def swapped_halves(values):
    lane = lane_of(values.shape)
    return jnp.where(lane % 64 < 32, rolled(values, -32), rolled(values, 32))


def half_lanes(values, half):
    lane = lane_of(values.shape)
    return jnp.where(lane < 64 if half == 0 else lane >= 64, values, 0.0)


def in_half(values, have, want):
    kept = half_lanes(values, have)
    return kept if have == want else rolled(kept, 64)


def half_sums(values):
    row = lax.broadcasted_iota(jnp.int32, (LANES, LANES), 0)
    ones = jnp.where(row // 64 == lane_of((LANES, LANES)) // 64, 1.0, 0.0).astype(jnp.bfloat16)
    return forward_product(values.astype(jnp.bfloat16), ones)


def half_softmax(values):
    lane = lane_of(values.shape)
    low = lane < 64
    first = jnp.max(jnp.where(low, values, -jnp.inf), axis=1, keepdims=True)
    second = jnp.max(jnp.where(low, -jnp.inf, values), axis=1, keepdims=True)
    powers = jnp.exp(values - jnp.where(low, first, second))
    first = jnp.sum(jnp.where(low, powers, 0.0), axis=1, keepdims=True)
    second = jnp.sum(jnp.where(low, 0.0, powers), axis=1, keepdims=True)
    return powers * jnp.where(low, 1.0 / first, 1.0 / second)


def group(ref_or_value, index):
    return ref_or_value[:, index * LANES : (index + 1) * LANES]


class Sizes:
    def __init__(self, shard, heads, kv_heads):
        self.shard, self.heads, self.kv = shard, heads, kv_heads
        self.each = heads // kv_heads
        self.query_groups = heads // 2
        self.key_groups = (kv_heads + 1) // 2
        self.linear = (heads + 2 * kv_heads) * 64
        self.span = shard + WIN
        self.kv_lanes = 2 * kv_heads * 64
        self.halo_lanes = self.kv_lanes + kv_heads * LANES

    def key_place(self, g):
        return g // 2, g % 2

    def value_place(self, g):
        return (self.kv + g) // 2, (self.kv + g) % 2


def prepare_kernel(sizes, lin_ref, cos_ref, sin_ref, meta_ref, mapq_ref, mapk_ref, rot_ref, phi_ref, halo_ref, whole_ref, first_ref):
    shard = sizes.shard
    wide = []
    for index in range(sizes.linear // LANES):
        part = group(lin_ref, index)
        turned = part * group(cos_ref, index) + swapped_halves(part) * group(sin_ref, index)
        rot_ref[:, index * LANES : (index + 1) * LANES] = turned.astype(jnp.bfloat16)
        wide.append(turned.astype(jnp.bfloat16))
    for index in range(sizes.query_groups):
        both = forward_product(wide[index], mapq_ref[index])
        for half in range(2):
            at = (2 * index + half) * LANES
            phi = half_softmax(group(both, half))
            phi_ref[:, at : at + LANES] = phi.astype(jnp.bfloat16)
    kv_groups = wide[sizes.query_groups :]
    phis = []
    for index in range(sizes.key_groups):
        both = forward_product(kv_groups[index], mapk_ref[index])
        for half in range(min(2, sizes.kv - 2 * index)):
            at = (sizes.heads + 2 * index + half) * LANES
            phi = half_softmax(group(both, half)).astype(jnp.bfloat16)
            phi_ref[:, at : at + LANES] = phi
            phis.append(phi)
    halo_ref[:, : sizes.kv_lanes] = jnp.concatenate(kv_groups, axis=1)[shard - WIN :]
    halo_ref[:, sizes.kv_lanes :] = jnp.concatenate(phis, axis=1)[shard - WIN :]
    keep_whole, keep_first = meta_ref[:, 0:1], meta_ref[:, 1:2]
    for g in range(sizes.kv):
        at, half = sizes.value_place(g)
        values = in_half(kv_groups[at].astype(jnp.float32), half, 0)
        values = jnp.where(lane_of(values.shape) == 64, 1.0, values).astype(jnp.bfloat16)
        phi = phis[g].astype(jnp.float32)
        for keep, ref in ((keep_whole, whole_ref), (keep_first, first_ref)):
            state = left_dot(values, (phi * keep).astype(jnp.bfloat16))
            ref[g] = state[:STATE_ROWS].astype(jnp.bfloat16)


def near_and_far(sizes, meta_ref, keys_ref):
    shape = (sizes.shard, sizes.span)
    row = lax.broadcasted_iota(jnp.int32, shape, 0)
    column = lax.broadcasted_iota(jnp.int32, shape, 1)
    same = meta_ref[:, 2:3] == keys_ref[0:1, :]
    near = same & (column > row) & (column <= row + WIN)
    far = same & (column <= row)
    return near, far


def twice(values):
    return jnp.concatenate([values] * 2, axis=0)


def stacked(parts):
    return jnp.concatenate(parts, axis=0)


def with_halo(sizes, rot_ref, phi_ref, halo_ref, g):
    out = []
    for at, half in (sizes.key_place(g), sizes.value_place(g)):
        own = group(rot_ref, sizes.query_groups + at)
        before = group(halo_ref, at)
        wide = stacked([before, own]).astype(jnp.float32)
        out.append([in_half(wide, half, want) for want in range(2)])
    phi = stacked(
        [
            halo_ref[:, sizes.kv_lanes + g * LANES : sizes.kv_lanes + (g + 1) * LANES],
            group(phi_ref, sizes.heads + g),
        ]
    )
    return out[0], out[1], phi


def value_sides(values, weight):
    ones = jnp.full(values[0].shape, weight, jnp.float32)
    sides = []
    for half in range(2):
        side = jnp.concatenate([values[half], half_lanes(ones, half)], axis=1)
        sides.append(side.astype(jnp.bfloat16))
    return sides


def state_sides(state, weight):
    totals = jnp.broadcast_to(state[64:65].astype(jnp.float32) * weight, (64, LANES))
    totals = totals.astype(jnp.bfloat16)
    none = jnp.zeros_like(totals)
    return [
        stacked([state[:64], none, totals, none]),
        stacked([none, state[:64], none, totals]),
    ]


def pairs_of(sizes, g):
    return range(g * sizes.each // 2, (g + 1) * sizes.each // 2)


def attend_kernel(sizes, rot_ref, phi_ref, halo_ref, state_ref, meta_ref, keys_ref, att_ref, den_ref):
    shard = sizes.shard
    near, far = near_and_far(sizes, meta_ref, keys_ref)
    reach = meta_ref[:, 3:4]
    for g in range(sizes.kv):
        pairs = pairs_of(sizes, g)
        count = len(pairs)
        near_all, far_all = stacked([near] * count), stacked([far] * count)
        keys, values, phi_key = with_halo(sizes, rot_ref, phi_ref, halo_ref, g)
        value_pair = value_sides(values, 1.0)
        state_pair = state_sides(state_ref[g], 1.0)
        queries = stacked([group(rot_ref, p) for p in pairs])
        total = None
        for half in range(2):
            scores = right_dot(queries, keys[half].astype(jnp.bfloat16)) * 0.125
            phi = stacked([group(phi_ref, 2 * p + half) for p in pairs])
            kernel = right_dot(phi, phi_key)
            weights = jnp.where(near_all, jnp.exp(scores), jnp.where(far_all, kernel, 0.0))
            reached = (phi.astype(jnp.float32) * stacked([reach] * count)).astype(jnp.bfloat16)
            term = forward_product(weights.astype(jnp.bfloat16), value_pair[half])
            term = term + right_dot(reached, state_pair[half])
            total = term if total is None else total + term
        mixed = total[:, :LANES] / total[:, LANES:]
        for turn, p in enumerate(pairs):
            rows = slice(turn * shard, (turn + 1) * shard)
            lanes = slice(p * LANES, (p + 1) * LANES)
            att_ref[:, lanes] = mixed[rows].astype(jnp.bfloat16)
            den_ref[:, lanes] = total[rows, LANES:]


def feature_back(phi, grads):
    phi = phi.astype(jnp.float32)
    return (phi * (grads - half_sums(phi * grads))).astype(jnp.bfloat16)


def unrotated(grads, cos, sin):
    return grads * cos - swapped_halves(grads) * sin


def backward_kernel(sizes, rot_ref, phi_ref, halo_ref, state_ref, meta_ref, keys_ref, att_ref, den_ref, grad_ref, cos_ref, sin_ref, mapq_ref, lin_ref, own_ref, back_ref, carry_ref, map_ref):
    shard = sizes.shard
    near, far = near_and_far(sizes, meta_ref, keys_ref)
    reach = meta_ref[:, 3:4]

    @pl.when(pl.program_id(0) == 0)
    def _():
        map_ref[...] = jnp.zeros_like(map_ref)

    kv_grads = [jnp.zeros((sizes.span, LANES), jnp.float32) for _ in range(sizes.kv_lanes // LANES)]
    for g in range(sizes.kv):
        pairs = pairs_of(sizes, g)
        count = len(pairs)
        near_all, far_all = stacked([near] * count), stacked([far] * count)
        reach_all = stacked([reach] * count)
        keys, values, phi_key = with_halo(sizes, rot_ref, phi_ref, halo_ref, g)
        value_pair = value_sides(values, 1.0 / 32.0)
        state_pair = state_sides(state_ref[g], 1.0 / 32.0)
        queries = stacked([group(rot_ref, p) for p in pairs])
        grads = stacked([group(grad_ref, p) for p in pairs]).astype(jnp.float32)
        mixed = stacked([group(att_ref, p) for p in pairs]).astype(jnp.float32)
        inverse = 1.0 / stacked([group(den_ref, p) for p in pairs])
        grad_num = (grads * inverse).astype(jnp.bfloat16)
        grad_den = -half_sums(grads * mixed) * inverse
        rough = grad_den.astype(jnp.bfloat16)
        rest = (grad_den - rough.astype(jnp.float32)).astype(jnp.bfloat16)
        lane = lane_of(grad_den.shape)
        grad_den = jnp.where(
            lane % 64 < 32, rough.astype(jnp.float32), rest.astype(jnp.float32)
        ).astype(jnp.bfloat16)
        both = jnp.concatenate([grad_num, grad_den], axis=1)
        grad_query = None
        key_sum, value_sum, phi_sum, state_sum = [], [], None, []
        back = [[None, None] for _ in pairs]
        for half in range(2):
            key_half = keys[half].astype(jnp.bfloat16)
            scores = right_dot(queries, key_half) * 0.125
            phi = stacked([group(phi_ref, 2 * p + half) for p in pairs])
            kernel = right_dot(phi, phi_key)
            powers = jnp.exp(scores)
            weights = jnp.where(near_all, powers, jnp.where(far_all, kernel, 0.0))
            weights = weights.astype(jnp.bfloat16)
            grad_weights = right_dot(both, value_pair[half])
            grad_scores = jnp.where(near_all, grad_weights * powers, 0.0).astype(jnp.bfloat16)
            grad_kernel = jnp.where(far_all, grad_weights, 0.0).astype(jnp.bfloat16)
            term = forward_product(grad_scores, key_half)
            grad_query = term if grad_query is None else grad_query + term
            key_sum.append(left_dot(grad_scores, queries))
            value_sum.append(left_dot(weights, grad_num))
            term = left_dot(grad_kernel, phi)
            phi_sum = term if phi_sum is None else phi_sum + term
            reached = (phi.astype(jnp.float32) * reach_all).astype(jnp.bfloat16)
            state_sum.append(left_dot(both, reached))
            grad_phi = forward_product(grad_kernel, phi_key)
            grad_phi = grad_phi + forward_product(both, state_pair[half]) * reach_all
            projected = feature_back(phi, grad_phi)
            for turn in range(count):
                back[turn][half] = projected[turn * shard : (turn + 1) * shard]
        for turn, p in enumerate(pairs):
            pair = jnp.concatenate(back[turn], axis=1)
            grad = grad_query[turn * shard : (turn + 1) * shard] * 0.125
            grad = grad + right_dot(pair, mapq_ref[p])
            grad = unrotated(grad, group(cos_ref, p), group(sin_ref, p))
            lin_ref[:, p * LANES : (p + 1) * LANES] = grad.astype(jnp.bfloat16)
            map_ref[p] += left_dot(group(rot_ref, p), pair)
        for (at, half), sums, scale in (
            (sizes.key_place(g), key_sum, 0.125),
            (sizes.value_place(g), value_sum, 1.0),
        ):
            total = in_half(sums[0], 0, half) + in_half(sums[1], 1, half)
            kv_grads[at] = kv_grads[at] + total * scale
        low, high = state_sum
        totals = low[128:129] + low[160:161] + high[192:193] + high[224:225]
        state_grad = stacked(
            [low[:64] + high[64:128], jnp.broadcast_to(totals, (STATE_ROWS - 64, LANES))]
        )
        carry_ref[g] = state_grad.astype(jnp.bfloat16)
        at = sizes.kv_lanes + g * LANES
        own_ref[:, at : at + LANES] = phi_sum[WIN:]
        back_ref[:, at : at + LANES] = phi_sum[:WIN].astype(jnp.bfloat16)
    for at, grads in enumerate(kv_grads):
        lanes = slice(at * LANES, (at + 1) * LANES)
        own_ref[:, lanes] = grads[WIN:]
        back_ref[:, lanes] = grads[:WIN].astype(jnp.bfloat16)


def key_kernel(sizes, rot_ref, phi_ref, meta_ref, own_ref, back_ref, whole_ref, first_ref, cos_ref, sin_ref, mapk_ref, lin_ref, map_ref):
    shard = sizes.shard

    @pl.when(pl.program_id(0) == 0)
    def _():
        map_ref[...] = jnp.zeros_like(map_ref)

    total = own_ref[...]
    returned = back_ref[...].astype(jnp.float32)
    if shard > WIN:
        total = stacked([total[: shard - WIN], total[shard - WIN :] + returned])
    else:
        total = total + returned
    kv_groups = sizes.kv_lanes // LANES
    kv_grads = [group(total, at) for at in range(kv_groups)]
    back = []
    for g in range(sizes.kv):
        at, half = sizes.value_place(g)
        values = in_half(group(rot_ref, sizes.query_groups + at).astype(jnp.float32), half, 0)
        values = jnp.where(lane_of(values.shape) == 64, 1.0, values).astype(jnp.bfloat16)
        phi = group(phi_ref, sizes.heads + g)
        grad_phi = total[:, sizes.kv_lanes + g * LANES : sizes.kv_lanes + (g + 1) * LANES]
        grad_value = None
        for column, ref in ((0, whole_ref), (1, first_ref)):
            keep = meta_ref[:, column : column + 1]
            state = stacked([ref[g], jnp.zeros((LANES - STATE_ROWS, LANES), jnp.bfloat16)])
            grad_phi = grad_phi + forward_product(values, state) * keep
            term = right_dot(phi, state) * keep
            grad_value = term if grad_value is None else grad_value + term
        kv_grads[at] = kv_grads[at] + in_half(grad_value, 0, half)
        back.append(feature_back(phi, grad_phi))
    if len(back) % 2:
        back.append(jnp.zeros_like(back[0]))
    for index in range(sizes.key_groups):
        pair = jnp.concatenate(back[2 * index : 2 * index + 2], axis=1)
        kv_grads[index] = kv_grads[index] + right_dot(pair, mapk_ref[index])
        map_ref[index] += left_dot(group(rot_ref, sizes.query_groups + index), pair)
    for at in range(kv_groups):
        cos = group(cos_ref, sizes.query_groups + at)
        sin = group(sin_ref, sizes.query_groups + at)
        lanes = slice(at * LANES, (at + 1) * LANES)
        lin_ref[:, lanes] = unrotated(kv_grads[at], cos, sin).astype(jnp.bfloat16)


def told(microseconds):
    return pl.CostEstimate(
        flops=int(microseconds * 500_000_000), bytes_accessed=0, transcendentals=0
    )


def by_row(kernel, name, rows, inputs, outputs, microseconds):
    def spec(shape, kind):
        rest = tuple(shape[1:])
        none = (0,) * len(rest)
        if kind == "all":
            return pl.BlockSpec(shape, lambda r: (0,) + none)
        first = shape[0] // rows if kind == "flat" else None
        return pl.BlockSpec((first,) + rest, lambda r: (r,) + none)

    return pl.pallas_call(
        kernel,
        grid=(rows,),
        in_specs=[spec(a.shape, kind) for a, kind in inputs],
        out_specs=[spec(shape.shape, kind) for shape, kind in outputs],
        out_shape=[shape for shape, _ in outputs],
        compiler_params=pltpu.CompilerParams(vmem_limit_bytes=48 * 1024 * 1024),
        cost_estimate=told(microseconds),
        name=name,
    )(*[a for a, _ in inputs])


def map_pairs(maps):
    count = maps.shape[0]
    wide = jnp.concatenate([maps, -maps], axis=2)
    if count % 2:
        wide = jnp.concatenate([wide, jnp.zeros_like(wide[:1])], axis=0)
    wide = wide.reshape(-1, 2, 64, LANES)
    none = jnp.zeros_like(wide[:, 0])
    return jnp.concatenate(
        [
            jnp.concatenate([wide[:, 0], none], axis=2),
            jnp.concatenate([none, wide[:, 1]], axis=2),
        ],
        axis=1,
    )


def maps_from_pairs(pairs, count):
    first = pairs[:, :64, :64] - pairs[:, :64, 64:128]
    second = pairs[:, 64:, 128:192] - pairs[:, 64:, 192:]
    return jnp.stack([first, second], axis=1).reshape(-1, 64, 64)[:count]


def rope_tables(positions, sizes):
    inverse = rope_base ** (-jnp.arange(0, 64, 2, dtype=jnp.float32) / 64)
    angle = positions.astype(jnp.float32)[:, None] * inverse[None, :]
    cosine, sine = jnp.cos(angle), jnp.sin(angle)
    turning = sizes.heads + sizes.kv
    cosine = jnp.tile(jnp.concatenate([cosine, cosine], axis=1), (1, turning))
    sine = jnp.tile(jnp.concatenate([-sine, sine], axis=1), (1, turning))
    rest = (positions.shape[0], sizes.kv * 64)
    return (
        jnp.concatenate([cosine, jnp.ones(rest, jnp.float32)], axis=1),
        jnp.concatenate([sine, jnp.zeros(rest, jnp.float32)], axis=1),
    )


def fixed(shape):
    return pl.BlockSpec(shape, lambda t: (0,) * len(shape), pipeline_mode=pl.Buffered(1))


def kernel_params():
    return pltpu.CompilerParams(vmem_limit_bytes=56 * 1024 * 1024)


def mlp_forward(rows, cotangent, weights, microseconds):
    count, width = rows.shape
    chunk = weights.shape[1] // 3
    tile = min(256, chunk)
    tiles = chunk // tile
    part = min(512, count)

    def kernel(x_ref, c_ref, gate_ref, up_ref, down_ref, grad_gate_ref, grad_up_ref, inner_ref):
        def one(turn, nothing):
            at = pl.ds(pl.multiple_of(turn * part, part), part)
            x = x_ref[at, :]
            gate = forward_product(x, gate_ref[...])
            up = forward_product(x, up_ref[...])
            grad_inner = forward_product(c_ref[at, :], down_ref[...])
            sigmoid = 1.0 / (1.0 + jnp.exp(-gate))
            swish = gate * sigmoid
            grad_gate = grad_inner * up * (sigmoid * (1.0 + gate * (1.0 - sigmoid)))
            grad_gate_ref[at, :] = grad_gate.astype(jnp.bfloat16)
            grad_up_ref[at, :] = (grad_inner * swish).astype(jnp.bfloat16)
            inner_ref[at, :] = (swish * up).astype(jnp.bfloat16)
            return nothing

        lax.fori_loop(0, count // part, one, 0)

    def columns(shift):
        return pl.BlockSpec((width, tile), lambda t: (0, t + shift))

    out = pl.BlockSpec((count, tile), lambda t: (0, t))
    shape = jax.ShapeDtypeStruct((count, chunk), jnp.bfloat16)
    return pl.pallas_call(
        kernel,
        grid=(tiles,),
        in_specs=[fixed(rows.shape), fixed(cotangent.shape)]
        + [columns(shift * tiles) for shift in range(3)],
        out_specs=[out] * 3,
        out_shape=[shape] * 3,
        compiler_params=kernel_params(),
        cost_estimate=told(microseconds),
        name="hidden_units",
    )(rows, cotangent, weights, weights, weights)


def turned_product(terms, before, dtype, microseconds):
    count, width = terms[0][0].shape[0], terms[0][1].shape[0]
    tile = min(512, width)

    def kernel(*refs):
        total = None if before is None else refs[-2][...]
        for left_ref, weight_ref in zip(refs, refs[len(terms) : 2 * len(terms)], strict=False):
            term = right_dot(left_ref[...], weight_ref[...])
            total = term if total is None else total + term
        refs[-1][...] = total.astype(dtype)

    def rows_of(section, chunk):
        return pl.BlockSpec((tile, chunk), lambda t: (t, section))

    out = pl.BlockSpec((count, tile), lambda t: (0, t))
    lefts = [left for left, _, _ in terms]
    return pl.pallas_call(
        kernel,
        grid=(width // tile,),
        in_specs=[fixed(left.shape) for left in lefts]
        + [rows_of(section, left.shape[1]) for left, _, section in terms]
        + ([] if before is None else [out]),
        out_specs=out,
        out_shape=jax.ShapeDtypeStruct((count, width), dtype),
        compiler_params=kernel_params(),
        cost_estimate=told(microseconds),
        name="turned_product",
    )(*lefts, *[weights for _, weights, _ in terms], *([] if before is None else [before]))


def weight_gradients(rows, cotangent, grad_gate, grad_up, inner, microseconds):
    count, width = rows.shape
    chunk = inner.shape[1]
    tile = min(512, width)

    def kernel(x_ref, c_ref, gate_ref, up_ref, inner_ref, out_ref):
        sides = ((x_ref, gate_ref), (x_ref, up_ref), (c_ref, inner_ref))
        for at, (left_ref, right_ref) in enumerate(sides):
            total = left_dot(left_ref[...], right_ref[...])
            out_ref[:, at * chunk : (at + 1) * chunk] = total.astype(jnp.bfloat16)

    column = pl.BlockSpec((count, tile), lambda t: (0, t))
    return pl.pallas_call(
        kernel,
        grid=(width // tile,),
        in_specs=[column, column] + [fixed(inner.shape)] * 3,
        out_specs=pl.BlockSpec((tile, 3 * chunk), lambda t: (t, 0)),
        out_shape=jax.ShapeDtypeStruct((width, 3 * chunk), jnp.bfloat16),
        compiler_params=kernel_params(),
        cost_estimate=told(microseconds),
        name="weight_gradients",
    )(rows, cotangent, grad_gate, grad_up, inner)


def document_facts(document_index, shard):
    seq_index = lax.axis_index("seq")
    count = lax.axis_size("seq")
    rows = document_index.shape[0]
    documents = document_index.astype(jnp.float32)
    missing = jnp.full((rows, 1), -1.0, jnp.float32)

    def last_of(block):
        at = jnp.clip(block * shard + shard - 1, 0, count * shard - 1)
        found = lax.dynamic_slice_in_dim(documents, at, 1, 1)
        return jnp.where((block >= 0) & (block < count), found, missing)

    def carried_of(block):
        at = jnp.clip(block * shard - WIN - 1, 0, count * shard - 1)
        found = lax.dynamic_slice_in_dim(documents, at, 1, 1)
        return jnp.where((block >= 1) & (block < count), found, missing - 1.0)

    padded = jnp.concatenate([jnp.broadcast_to(missing, (rows, WIN)), documents], axis=1)
    key_documents = lax.dynamic_slice_in_dim(padded, seq_index * shard, shard + WIN, 1)
    own = key_documents[:, WIN:]
    position = jnp.arange(shard)[None, :]
    keep_whole = own == own[:, shard - 1 :]
    keep_first = (position < shard - WIN) & (own == own[:, shard - WIN - 1 : shard - WIN])
    reach = own == carried_of(seq_index)
    columns = [keep_whole, keep_first, own, reach]
    meta = jnp.stack([column.astype(jnp.float32) for column in columns], axis=-1)
    meta = jnp.concatenate([meta, jnp.zeros_like(meta)], axis=-1)
    return meta, key_documents[:, None, :], last_of, carried_of


def masked(block, mask):
    return block.astype(jnp.float32) * mask.astype(jnp.float32).reshape(-1, 1, 1, 1)


class Carries:
    def __init__(self, last_of, carried_of, rows):
        self.index = lax.axis_index("seq")
        self.count = lax.axis_size("seq")
        self.even = self.index % 2 == 0
        self.rows = rows // 2
        self.pair = self.index - self.index % 2
        self.last_of, self.carried_of = last_of, carried_of
        self.steps = []
        distance = 1
        while distance < self.count // 2:
            self.steps.append(distance)
            distance *= 2

    def half(self, values, own):
        at = jnp.where(self.even == own, 0, self.rows)
        return lax.dynamic_slice_in_dim(values, at, self.rows, 0)

    def end(self, back):
        return self.half(self.last_of(self.pair - back), True)

    def other(self, values):
        values = values.astype(jnp.bfloat16)
        return lax.ppermute(values, "seq", [(i, i ^ 1) for i in range(self.count)])

    def pick(self, first, second):
        return jnp.where(self.even, first.astype(jnp.float32), second.astype(jnp.float32))

    def split(self, values):
        mine, theirs = self.half(values, True), self.other(self.half(values, False))
        return self.pick(mine, theirs), self.pick(theirs, mine)

    def join(self, even, odd):
        kept, got = self.pick(even, odd), self.other(self.pick(odd, even))
        return jnp.concatenate([self.pick(kept, got), self.pick(got, kept)], axis=0)

    def reach(self):
        even = self.half(self.carried_of(self.pair), True) == self.end(2)
        odd = self.half(self.carried_of(self.pair + 1), True) == self.end(1)
        return even, odd

    def forward(self, whole, first):
        before = shifted(first, 1)
        even, odd = self.split(whole)
        window = odd + masked(even, self.end(0) == self.end(-1))
        sums = None
        for distance in self.steps:
            if sums is None:
                got = shifted(jnp.stack([window, even]).astype(jnp.bfloat16), 2)
                got = got.astype(jnp.float32)
                sums = got[1], got[0]
                got = got[0]
            else:
                got = shifted(window.astype(jnp.bfloat16), 2 * distance)
                there = self.end(2 * distance - 1)
                sums = (
                    sums[0] + masked(got, there == self.end(2)),
                    sums[1] + masked(got, there == self.end(1)),
                )
            window = window + masked(got, self.end(2 * distance - 1) == self.end(-1))
        reach = self.reach()
        total = self.join(masked(sums[0], reach[0]), masked(sums[1], reach[1]))
        return (total + before.astype(jnp.float32)).astype(jnp.bfloat16)

    def backward(self, grads):
        first = shifted(grads, -1)
        even, odd = self.split(grads)
        reach = self.reach()
        even, odd = masked(even, reach[0]), masked(odd, reach[1])
        window = None
        for distance in reversed(self.steps):
            there = self.end(2 * distance - 1)
            linked = 0.0 if window is None else masked(window, there == self.end(-1))
            if distance == 1:
                sent = jnp.stack([linked + odd, even]).astype(jnp.bfloat16)
                got = shifted(sent, -2).astype(jnp.float32)
                window = got[0] if window is None else window + got[0]
                direct = got[1]
            else:
                sent = linked + masked(odd, there == self.end(1))
                sent = sent + masked(even, there == self.end(2))
                got = shifted(sent.astype(jnp.bfloat16), -2 * distance).astype(jnp.float32)
                window = got if window is None else window + got
        even = masked(window, self.end(0) == self.end(-1)) + direct
        return self.join(even, window).astype(jnp.bfloat16), first


def body(
    tokens,
    cotangent,
    first_norm_gain,
    second_norm_gain,
    query_weight,
    key_weight,
    value_weight,
    output_weight,
    gate_weight,
    up_weight,
    down_weight,
    adapter_down_weight,
    adapter_query_weight,
    adapter_key_weight,
    adapter_value_weight,
    adapter_output_down,
    adapter_output_up,
    hedgehog_query_weight,
    hedgehog_key_weight,
    document_index,
):
    row_count, shard, width = tokens.shape
    seq_index = lax.axis_index("seq")
    heads_here = hedgehog_query_weight.shape[0]
    kv_here = hedgehog_key_weight.shape[0]
    sizes = Sizes(shard, heads_here, kv_here)
    rank = adapter_query_weight.shape[0]
    tokens_here = row_count * shard
    block_rows = query_weight.shape[0]
    hidden_units = gate_weight.shape[1]
    chunk = hidden_units // MLP_CHUNKS
    query_width, key_width = query_weight.shape[1], key_weight.shape[1]
    key_end = query_width + key_width

    out_width = output_weight.shape[0]
    first_gather = Gather(
        jnp.concatenate([query_weight, key_weight, value_weight, output_weight.T], axis=1)
    )
    first_gather.advance(quarters=4)
    down_turned = down_weight.T
    gathers = []
    for turn in range(MLP_CHUNKS):
        span = slice(turn * chunk, (turn + 1) * chunk)
        gathers.append(
            Gather(
                jnp.concatenate(
                    [gate_weight[:, span], up_weight[:, span], down_turned[:, span]], axis=1
                )
            )
        )
    early, late = gathers
    early.advance(*first_gather.found[first_gather.half])
    complete_qkv, out_turned = first_gather.assemble(sizes.linear, out_width)

    adapters = jnp.zeros((3 * rank, sizes.linear), jnp.bfloat16)
    adapters = lax.dynamic_update_slice(adapters, adapter_query_weight, (0, 0))
    adapters = lax.dynamic_update_slice(adapters, adapter_key_weight, (rank, query_width))
    adapters = lax.dynamic_update_slice(adapters, adapter_value_weight, (2 * rank, key_end))
    positions = seq_index * shard + jnp.arange(shard)
    cosine, sine = rope_tables(positions, sizes)
    map_query, map_key = map_pairs(hedgehog_query_weight), map_pairs(hedgehog_key_weight)
    meta, key_documents, last_of, carried_of = document_facts(document_index, shard)

    flattened = tokens.reshape(tokens_here, width).astype(jnp.float32)
    scale_one = lax.rsqrt(jnp.mean(flattened * flattened, axis=-1, keepdims=True) + epsilon)
    normalized_input = flattened * scale_one * first_norm_gain.astype(jnp.float32)
    normalized_input = normalized_input.astype(jnp.bfloat16)
    lowrank_input = forward_product(normalized_input, adapter_down_weight).astype(jnp.bfloat16)
    linear = forward_product(normalized_input, complete_qkv) + adapter_scale * forward_product(
        lowrank_input, adapters
    )
    low = functools.partial(jax.ShapeDtypeStruct, dtype=jnp.bfloat16)
    wide = functools.partial(jax.ShapeDtypeStruct, dtype=jnp.float32)
    phi_lanes = (heads_here + kv_here) * LANES
    states = low((row_count, kv_here, STATE_ROWS, LANES))
    rotated, phi, tail, whole, first = by_row(
        functools.partial(prepare_kernel, sizes),
        "prepare",
        row_count,
        [
            (linear, "flat"),
            (cosine, "all"),
            (sine, "all"),
            (meta, "row"),
            (map_query, "all"),
            (map_key, "all"),
        ],
        [
            (low((tokens_here, sizes.linear)), "flat"),
            (low((tokens_here, phi_lanes)), "flat"),
            (low((row_count, WIN, sizes.halo_lanes)), "row"),
            (states, "row"),
            (states, "row"),
        ],
        16,
    )
    tail, whole, first = after((tail, whole, first), *early.edge())
    halo = shifted(tail, 1)
    carries = Carries(last_of, carried_of, row_count)
    carry = carries.forward(whole, first)
    early.advance(carry, halo)
    attended, denominator = by_row(
        functools.partial(attend_kernel, sizes),
        "attend",
        row_count,
        [
            (rotated, "flat"),
            (phi, "flat"),
            (halo, "row"),
            (carry, "row"),
            (meta, "row"),
            (key_documents, "row"),
        ],
        [
            (low((tokens_here, query_width)), "flat"),
            (wide((tokens_here, query_width)), "flat"),
        ],
        8,
    )

    lowrank_output = forward_product(attended, adapter_output_down).astype(jnp.bfloat16)
    out_part = right_dot(attended, out_turned) + adapter_scale * forward_product(
        lowrank_output, adapter_output_up
    )
    out_part = after(out_part.astype(jnp.bfloat16), *early.edge())
    early.advance(out_part)
    own_rows = row_count // lax.axis_size("head")
    first_row = lax.axis_index("head") * own_rows
    own_tokens = lax.dynamic_slice_in_dim(tokens, first_row, own_rows, 0)
    own_tokens = own_tokens.reshape(own_rows * shard, width).astype(jnp.float32)
    own_cotangent = lax.dynamic_slice_in_dim(cotangent, first_row, own_rows, 0)
    own_cotangent = own_cotangent.reshape(own_rows * shard, width).astype(jnp.float32)
    out_sum = head_scatter(out_part)
    hidden_state = own_tokens + out_sum
    scale_two = lax.rsqrt(jnp.mean(hidden_state * hidden_state, axis=-1, keepdims=True) + epsilon)
    unit_two = hidden_state * scale_two
    own_normed = (unit_two * second_norm_gain.astype(jnp.float32)).astype(jnp.bfloat16)
    own_normed = after(own_normed, *early.edge())
    early.advance(own_normed)
    late.advance(own_normed)
    normed_rows = head_gather(own_normed)

    grad_out = cotangent.reshape(tokens_here, width)

    (weights_early,) = early.assemble(3 * chunk)
    gate_early, up_early, inner_early = mlp_forward(normed_rows, grad_out, weights_early, 22)
    gate_early = after(gate_early, *late.edge())
    late.advance()
    part_early = turned_product(
        [(gate_early, weights_early, 0), (up_early, weights_early, 1)], None, jnp.float32, 14
    )
    grads_early = weight_gradients(
        normed_rows, grad_out, gate_early, up_early, after(inner_early, part_early), 19
    )
    grads_early = after(grads_early, *late.edge())
    late.advance()
    scatter_early = Scatter([grads_early], block_rows)
    scatter_early.advance(*late.edge())
    late.advance()
    (weights_late,) = late.assemble(3 * chunk)
    gate_late, up_late, inner_late = mlp_forward(normed_rows, grad_out, weights_late, 22)
    gate_late = after(gate_late, *scatter_early.edge())
    scatter_early.advance()
    normed_two_part = turned_product(
        [(gate_late, weights_late, 0), (up_late, weights_late, 1)], part_early, jnp.bfloat16, 14
    )
    both_cores = head_pair_sum(normed_two_part)
    scatter_early.advance(normed_two_part)
    grads_late = weight_gradients(
        normed_rows, grad_out, gate_late, up_late, after(inner_late, both_cores), 19
    )
    grad_normed_two = head_finish(both_cores)
    scatter_late = Scatter([grads_late], block_rows)
    scatter_late.advance(*scatter_early.edge())
    scatter_early.advance(grads_late)
    grad_gain_two = jnp.sum(grad_normed_two * unit_two, axis=0, keepdims=True)
    inner_two = grad_normed_two * second_norm_gain.astype(jnp.float32)
    grad_hidden = own_cotangent + scale_two * (
        inner_two - unit_two * jnp.mean(inner_two * unit_two, axis=-1, keepdims=True)
    )
    grad_branch = head_gather(grad_hidden.astype(jnp.bfloat16))
    down_part = turned_product(
        [(inner_early, weights_early, 2), (after(inner_late, grads_late), weights_late, 2)],
        None,
        jnp.bfloat16,
        13,
    )
    down_sum = head_finish(head_pair_sum(down_part), grad_branch)
    scatter_late.advance(grad_hidden)
    grad_branch = after(grad_branch, *scatter_late.edge())
    scatter_late.advance()
    out_up_gradient = adapter_scale * left_dot(lowrank_output, grad_branch)
    grad_w_out = left_dot(grad_branch, attended).astype(jnp.bfloat16)
    grad_lowrank_out = adapter_scale * right_dot(grad_branch, adapter_output_up)
    grad_lowrank_out = grad_lowrank_out.astype(jnp.bfloat16)
    out_down_gradient = left_dot(grad_lowrank_out, attended)
    grad_attended = forward_product(grad_branch, out_turned) + right_dot(
        grad_lowrank_out, adapter_output_down
    )

    own_lanes = sizes.halo_lanes
    grad_query_lin, own_grads, back, carry_grads, map_query_pairs = by_row(
        functools.partial(backward_kernel, sizes),
        "backward",
        row_count,
        [
            (rotated, "flat"),
            (phi, "flat"),
            (halo, "row"),
            (carry, "row"),
            (meta, "row"),
            (key_documents, "row"),
            (attended, "flat"),
            (denominator, "flat"),
            (grad_attended.astype(jnp.bfloat16), "flat"),
            (cosine, "all"),
            (sine, "all"),
            (map_query, "all"),
        ],
        [
            (low((tokens_here, query_width)), "flat"),
            (wide((tokens_here, own_lanes)), "flat"),
            (low((row_count, WIN, own_lanes)), "row"),
            (states, "row"),
            (wide(map_query.shape), "all"),
        ],
        26,
    )
    carry_grads, back = after((carry_grads, back), down_sum, *scatter_late.edge())
    layer_rows = head_gather((hidden_state + down_sum).astype(jnp.bfloat16))
    returned = shifted(back, -1)
    grad_whole, grad_first = carries.backward(carry_grads)
    scatter_late.advance(grad_whole)
    grad_w_query = left_dot(normalized_input, grad_query_lin).astype(jnp.bfloat16)
    query_part = right_dot(grad_query_lin, complete_qkv[:, :query_width])
    grad_key_lin, map_key_pairs = by_row(
        functools.partial(key_kernel, sizes),
        "keys",
        row_count,
        [
            (rotated, "flat"),
            (phi, "flat"),
            (meta, "row"),
            (own_grads, "flat"),
            (returned, "row"),
            (grad_whole, "row"),
            (grad_first, "row"),
            (cosine, "all"),
            (sine, "all"),
            (map_key, "all"),
        ],
        [
            (low((tokens_here, sizes.kv_lanes)), "flat"),
            (wide(map_key.shape), "all"),
        ],
        7,
    )
    grad_linear = jnp.concatenate([grad_query_lin, grad_key_lin], axis=1)
    lowrank_gradient = (adapter_scale * right_dot(grad_linear, adapters)).astype(jnp.bfloat16)
    normed_part = (
        query_part
        + right_dot(grad_key_lin, complete_qkv[:, query_width:])
        + right_dot(lowrank_gradient, adapter_down_weight)
    ).astype(jnp.bfloat16)
    normalized_gradient = head_scatter(after(normed_part, layer_rows))
    grad_w_kv = left_dot(normalized_input, grad_key_lin).astype(jnp.bfloat16)
    last_scatter = Scatter([grad_w_query, grad_w_out, grad_w_kv], block_rows)
    last_scatter.advance(*scatter_late.edge())
    adapter_gradient = adapter_scale * left_dot(lowrank_input, grad_linear)
    down_gradient = left_dot(lowrank_gradient, normalized_input)
    gain_one = normed_part.astype(jnp.float32) * (tokens.reshape(tokens_here, width) * scale_one)
    grad_gain_one = jnp.sum(gain_one, axis=0, keepdims=True)
    own_scale = lax.rsqrt(jnp.mean(own_tokens * own_tokens, axis=-1, keepdims=True) + epsilon)
    own_unit = own_tokens * own_scale
    inner_one = normalized_gradient * first_norm_gain.astype(jnp.float32)
    own_grad_tokens = grad_hidden + own_scale * (
        inner_one - own_unit * jnp.mean(inner_one * own_unit, axis=-1, keepdims=True)
    )
    grad_tokens_rows = head_gather(own_grad_tokens.astype(jnp.bfloat16)).astype(jnp.float32)
    last_sum = last_scatter.total()
    mlp_sums = [scatter_early.total(), scatter_late.total()]

    everywhere = jnp.concatenate(
        [down_gradient, out_up_gradient, grad_gain_one, grad_gain_two], axis=0
    )
    adapter_part = jnp.concatenate(
        [
            adapter_gradient[:rank, :query_width],
            adapter_gradient[rank : 2 * rank, query_width:key_end],
            adapter_gradient[2 * rank :, key_end:],
            out_down_gradient,
        ],
        axis=1,
    )
    maps_part = jnp.concatenate(
        [maps_from_pairs(map_query_pairs, heads_here), maps_from_pairs(map_key_pairs, kv_here)]
    )
    maps_part = jnp.pad(maps_part.reshape(-1, 64), ((0, 0), (0, LANES - 64)))
    small = jnp.concatenate(
        [everywhere.reshape(-1, LANES), adapter_part.reshape(-1, LANES), maps_part], axis=0
    )
    small = after(small.astype(jnp.bfloat16), *scatter_late.edge())
    small = exchange_sum(small, "seq", bits_of("seq"))
    first, second = everywhere.size // LANES, (everywhere.size + adapter_part.size) // LANES
    everywhere = exchange_sum(small[:first], "head", bits_of("head")).astype(jnp.float32)
    everywhere = everywhere.reshape(-1, width)
    small = small.astype(jnp.float32)
    adapter_sum = small[first:second].reshape(adapter_part.shape)
    maps_sum = small[second:, :64].reshape(-1, 64, 64)
    end = 3 * rank + rank

    def columns(at):
        return jnp.concatenate([part[:, at * chunk : (at + 1) * chunk] for part in mlp_sums], axis=1)

    return (
        layer_rows.reshape(row_count, shard, width),
        grad_tokens_rows.reshape(row_count, shard, width),
        everywhere[end],
        everywhere[end + 1],
        last_sum[:, :query_width],
        last_sum[:, query_width + out_width : key_end + out_width],
        last_sum[:, key_end + out_width :],
        last_sum[:, query_width : query_width + out_width].T,
        columns(0),
        columns(1),
        columns(2).T,
        everywhere[: 3 * rank].T,
        adapter_sum[:, :query_width],
        adapter_sum[:, query_width:key_end],
        adapter_sum[:, key_end : sizes.linear],
        adapter_sum[:, sizes.linear :].T,
        everywhere[3 * rank : end],
        maps_sum[:heads_here],
        maps_sum[heads_here:],
    )


def solution(mesh):
    in_specs = (
        P(None, "seq", None),
        P(None, "seq", None),
        P(),
        P(),
        P("seq", "head"),
        P("seq", "head"),
        P("seq", "head"),
        P("head", "seq"),
        P("seq", "head"),
        P("seq", "head"),
        P("head", "seq"),
        P(),
        P(None, "head"),
        P(None, "head"),
        P(None, "head"),
        P("head", None),
        P(),
        P("head", None, None),
        P("head", None, None),
        P(),
    )
    out_specs = (
        P(None, "seq", None),
        P(None, "seq", None),
        P(),
        P(),
        P("seq", "head"),
        P("seq", "head"),
        P("seq", "head"),
        P("head", "seq"),
        P("seq", "head"),
        P("seq", "head"),
        P("head", "seq"),
        P(),
        P(None, "head"),
        P(None, "head"),
        P(None, "head"),
        P("head", None),
        P(),
        P("head", None, None),
        P("head", None, None),
    )
    return jax.shard_map(body, mesh=mesh, in_specs=in_specs, out_specs=out_specs, check_vma=False)
```

```python
import functools

import jax
import jax.numpy as jnp
from jax import lax
from jax.experimental import pallas as pl
from jax.experimental.pallas import tpu as pltpu
from jax.sharding import PartitionSpec as P

WIN = 64
LANES = 128
STATE_ROWS = 80
TOLD = 10_000_000

epsilon = 1e-05
rope_base = 500000.0
adapter_scale = 2.0


def forward_product(left, right):
    return jnp.dot(left, right, preferred_element_type=jnp.float32)


def left_dot(left, right):
    return lax.dot_general(
        left, right, (((0,), (0,)), ((), ())), preferred_element_type=jnp.float32
    )


def right_dot(left, right):
    return lax.dot_general(
        left, right, (((1,), (1,)), ((), ())), preferred_element_type=jnp.float32
    )


def shifted(block, distance):
    devices = range(lax.axis_size("seq"))
    route = [(i - distance, i) for i in devices if i - distance in devices]
    return lax.ppermute(block, "seq", route)


def ring_order(count):
    return list(range(0, count, 2)) + list(range(count - 1, 0, -2))


def ring_move(block, step):
    order = ring_order(lax.axis_size("seq"))
    count = len(order)
    return lax.ppermute(block, "seq", [(order[i], order[(i + step) % count]) for i in range(count)])


def ring_index(offset):
    count = lax.axis_size("seq")
    mine = lax.axis_index("seq")
    place = jnp.where(mine % 2 == 0, mine // 2, count - 1 - mine // 2)
    there = (place + offset + count) % count
    return jnp.where(there < count // 2, 2 * there, 2 * (count - 1 - there) + 1).astype(jnp.int32)


def after(value, *others):
    return lax.optimization_barrier((value,) + others)[0]


def told(microseconds):
    return pl.CostEstimate(flops=int(microseconds * TOLD), bytes_accessed=0, transcendentals=0)


def kernel_params():
    return pltpu.CompilerParams(vmem_limit_bytes=56 * 1024 * 1024)


def place_rows(pieces, places, origins, rows, widths):
    starts = [sum(widths[:i]) for i in range(len(widths))]

    def kernel(places_ref, *refs):
        sources, rest = refs[: len(pieces)], refs[len(pieces) :]
        targets, buffers, semaphores = rest[: len(widths)], rest[len(widths) : -1], rest[-1]
        inward, outward = [], []
        for turn, (source, (at, shift)) in enumerate(zip(sources, origins, strict=True)):
            length = source.shape[0]
            held = buffers[turn]
            inward.append(pltpu.make_async_copy(source, held, semaphores.at[turn]))
            first = pl.multiple_of(places_ref[at] + shift, length)
            for target, start, width in zip(targets, starts, widths, strict=True):
                outward.append(
                    pltpu.make_async_copy(
                        held.at[:, pl.ds(start, width)],
                        target.at[pl.ds(first, length), :],
                        semaphores.at[len(sources) + len(outward)],
                    )
                )
        for copy in inward:
            copy.start()
        for turn, copy in enumerate(inward):
            copy.wait()
            for back in outward[turn * len(widths) : (turn + 1) * len(widths)]:
                back.start()
        for copy in outward:
            copy.wait()

    anywhere = pl.BlockSpec(memory_space=pl.ANY)
    size = sum(piece.size for piece in pieces) * 2
    return pl.pallas_call(
        kernel,
        grid_spec=pltpu.PrefetchScalarGridSpec(
            num_scalar_prefetch=1,
            grid=(1,),
            in_specs=[anywhere] * len(pieces),
            out_specs=[anywhere] * len(widths),
            scratch_shapes=[pltpu.VMEM(piece.shape, piece.dtype) for piece in pieces]
            + [pltpu.SemaphoreType.DMA((len(pieces) * (1 + len(widths)),))],
        ),
        out_shape=[jax.ShapeDtypeStruct((rows, width), pieces[0].dtype) for width in widths],
        compiler_params=pltpu.CompilerParams(vmem_limit_bytes=size + 4 * 1024 * 1024),
        cost_estimate=told(1 + size // 4_000_000),
        name="place_rows",
    )(places, *pieces)


class Gather:
    def __init__(self, own):
        self.half = lax.axis_size("seq") // 2
        self.found = {0: own}
        self.up = self.down = own
        self.step = 0

    def advance(self, *gates, quarters=1):
        for _ in range(quarters * max(1, self.half // 4)):
            if self.step == self.half:
                return
            self.step += 1
            cut = self.up.shape[0] // 2
            up, down = self.up, self.down
            if gates:
                up, down = after(up, *gates), after(down, *gates)
            if self.step < self.half:
                self.up, self.down = ring_move(up, 1), ring_move(down, -1)
                self.found[-self.step], self.found[self.step] = self.up, self.down
            else:
                self.found[self.half] = (ring_move(up[:cut], 1), ring_move(down[cut:], -1))

    def edge(self):
        return self.found[self.half] if self.step == self.half else (self.up, self.down)

    def assemble(self, *widths):
        self.advance(quarters=4)
        rows = self.found[0].shape[0]
        offsets = sorted(self.found)
        places = jnp.stack([ring_index(offset) * rows for offset in offsets])
        pieces, origins = [], []
        for at, offset in enumerate(offsets):
            block, shift = self.found[offset], 0
            for part in block if isinstance(block, tuple) else (block,):
                pieces.append(part)
                origins.append((at, shift))
                shift += part.shape[0]
        return place_rows(pieces, places, origins, lax.axis_size("seq") * rows, widths)


def on_block(kernel, grads, others, outs, offset, rows, name):
    cut, columns = rows // 2, grads.shape[1]

    def half_of(length):
        if length == rows:
            return pl.BlockSpec((cut, columns), lambda h, at: (h, 0))
        return pl.BlockSpec((cut, columns), lambda h, at: (0, 0))

    return pl.pallas_call(
        kernel,
        grid_spec=pltpu.PrefetchScalarGridSpec(
            num_scalar_prefetch=1,
            grid=(2,),
            in_specs=[pl.BlockSpec((cut, columns), lambda h, at: (2 * at[0] + h, 0))]
            + [half_of(other.shape[0]) for other in others],
            out_specs=[spec if spec else half_of(shape.shape[0]) for shape, spec in outs],
        ),
        out_shape=[shape for shape, _ in outs],
        compiler_params=kernel_params(),
        cost_estimate=told(2),
        name=name,
    )(ring_index(offset)[None], grads, *others)


class Scatter:
    def __init__(self, grads, rows):
        self.grads, self.rows = grads, rows
        self.half = lax.axis_size("seq") // 2
        self.step = 0

    def shape(self, rows):
        return jax.ShapeDtypeStruct((rows, self.grads.shape[1]), self.grads.dtype)

    def far(self):
        def kernel(at_ref, own_ref, up_ref, down_ref):
            @pl.when(pl.program_id(0) == 0)
            def _():
                up_ref[...] = own_ref[...]

            @pl.when(pl.program_id(0) == 1)
            def _():
                down_ref[...] = own_ref[...]

        outs = [(self.shape(self.rows // 2), None)] * 2
        return on_block(kernel, self.grads, [], outs, self.half, self.rows, "far_block")

    def joined(self, received, offset, which):
        full = received.shape[0] == self.rows

        def kernel(at_ref, own_ref, got_ref, out_ref):
            own, got = own_ref[...].astype(jnp.float32), got_ref[...].astype(jnp.float32)
            if not full:
                got = jnp.where(pl.program_id(0) == which, got, 0.0)
            out_ref[...] = (own + got).astype(out_ref.dtype)

        outs = [(self.shape(self.rows), None)]
        (out,) = on_block(kernel, self.grads, [received], outs, offset, self.rows, "join_block")
        return out

    def advance(self, *gates, quarters=1):
        for _ in range(quarters * max(1, self.half // 4)):
            if self.step == self.half:
                return
            self.step += 1
            offset = self.half - self.step + 1
            if self.step == 1:
                up, down = self.far()
            else:
                up, down = self.joined(self.up, offset, 0), self.joined(self.down, -offset, 1)
            if gates:
                up, down = after(up, *gates), after(down, *gates)
            self.sending = up, down
            self.up, self.down = ring_move(up, 1), ring_move(down, -1)

    def edge(self):
        return self.up, self.down

    def total(self, widths, turned):
        self.advance(quarters=4)
        starts = [sum(widths[:i]) for i in range(len(widths))]
        cut = self.rows // 2
        later = [turn and cut % LANES != 0 for turn in turned]
        turned = [turn and not late for turn, late in zip(turned, later, strict=True)]

        def kernel(at_ref, own_ref, up_ref, down_ref, *out_refs):
            for start, width, turn, out_ref in zip(starts, widths, turned, out_refs, strict=True):
                lanes = slice(start, start + width)
                total = own_ref[:, lanes].astype(jnp.float32) + up_ref[:, lanes].astype(jnp.float32)
                total = total + down_ref[:, lanes].astype(jnp.float32)
                out_ref[...] = total.T if turn else total

        outs = []
        for width, turn in zip(widths, turned, strict=True):
            shape = (width, self.rows) if turn else (self.rows, width)
            block = (width, cut) if turn else (cut, width)
            spec = pl.BlockSpec(block, (lambda h, at: (0, h)) if turn else (lambda h, at: (h, 0)))
            outs.append((jax.ShapeDtypeStruct(shape, jnp.float32), spec))
        sums = on_block(
            kernel, self.grads, [self.up, self.down], outs, 0, self.rows, "own_block"
        )
        return [part.T if late else part for part, late in zip(sums, later, strict=True)]


def core_swap(block):
    count = lax.axis_size("head")
    return lax.ppermute(block, "head", [(i, i ^ 1) for i in range(count)])


def chip_move(block, step):
    count = lax.axis_size("head")
    return lax.ppermute(block, "head", [(i, (i + 2 * step) % count) for i in range(count)])


class HeadSum:
    def __init__(self, mine, *theirs):
        self.mine = mine
        self.got = [core_swap(piece) for piece in theirs]

    def pair(self):
        chips, rows, width = self.mine.shape
        tile = self.tile = min(128, rows)
        chip = (lax.axis_index("head") // 2).astype(jnp.int32)
        cuts, tiles = len(self.got), rows // tile

        def kernel(chip_ref, mine_ref, *refs):
            got_refs, kept_ref, sent_refs = refs[:cuts], refs[cuts], refs[cuts + 1 :]

            def both(step, out_ref):
                at = (chip_ref[0] + step) % chips
                for turn, got_ref in enumerate(got_refs):
                    lanes = slice(turn * got_ref.shape[2], (turn + 1) * got_ref.shape[2])
                    total = mine_ref[at, :, lanes].astype(jnp.float32)
                    total = total + got_ref[at].astype(jnp.float32)
                    out_ref[:, lanes] = total.astype(out_ref.dtype)

            both(0, kept_ref)
            for turn, sent_ref in enumerate(sent_refs):
                pl.when(pl.program_id(0) == turn % tiles)(
                    functools.partial(both, 1 + turn // tiles, sent_ref)
                )

        def cut(size, *first):
            return pl.BlockSpec(first + (tile, size), lambda t, at: (0,) * len(first) + (t, 0))

        count = (chips - 1) * tiles
        piece = pl.BlockSpec((tile, width), lambda t, at: (0, 0))
        self.kept, *self.sent = pl.pallas_call(
            kernel,
            grid_spec=pltpu.PrefetchScalarGridSpec(
                num_scalar_prefetch=1,
                grid=(tiles,),
                in_specs=[cut(width, chips)] + [cut(piece.shape[2], chips) for piece in self.got],
                out_specs=[cut(width)] + [piece] * count,
            ),
            out_shape=[jax.ShapeDtypeStruct((rows, width), jnp.float32)]
            + [jax.ShapeDtypeStruct((tile, width), jnp.bfloat16)] * count,
            compiler_params=kernel_params(),
            cost_estimate=told(2),
            name="pair_sum",
        )(chip[None], self.mine, *self.got)
        return self.sent

    def finish(self, formula, blocks, gain, keep, add, name, *gates):
        rows, width = self.kept.shape
        tile, tiles = self.tile, self.kept.shape[0] // self.tile
        moved = []
        for turn, sent in enumerate(self.sent):
            sent = after(sent, *gates) if gates else sent
            moved.append(chip_move(sent, 1 + turn // tiles))
        kept = after(self.kept, *moved)

        def kernel(kept_ref, *refs):
            moved_refs, refs = refs[: len(moved)], refs[len(moved) :]
            block_refs, gain_ref, out_refs = refs[: len(blocks)], refs[len(blocks)], refs[len(blocks) + 1 :]
            piece_refs = out_refs[keep : keep + tiles]

            def one(turn):
                total = kept_ref[...]
                for moved_ref in moved_refs[turn::tiles]:
                    total = total + moved_ref[...].astype(jnp.float32)
                values = [ref[...].astype(jnp.float32) for ref in block_refs]
                first, piece, column = formula(total, *values, gain_ref[...])
                if keep:
                    out_refs[0][...] = first
                piece_refs[turn][...] = piece.astype(jnp.bfloat16)
                if add:
                    column = jnp.sum(column, axis=0, keepdims=True)
                    out_refs[-1][...] = column if turn == 0 else out_refs[-1][...] + column

            for turn in range(tiles):
                pl.when(pl.program_id(0) == turn)(functools.partial(one, turn))

        block = pl.BlockSpec((tile, width), lambda t: (t, 0))
        piece = pl.BlockSpec((tile, width), lambda t: (0, 0))
        line = pl.BlockSpec((1, width), lambda t: (0, 0))
        wide = functools.partial(jax.ShapeDtypeStruct, dtype=jnp.float32)
        outs = pl.pallas_call(
            kernel,
            grid=(tiles,),
            in_specs=[block] + [piece] * len(moved) + [block] * len(blocks) + [line],
            out_specs=[block] * keep + [piece] * tiles + [line] * add,
            out_shape=[wide((rows, width))] * keep
            + [jax.ShapeDtypeStruct((tile, width), jnp.bfloat16)] * tiles
            + [wide((1, width))] * add,
            compiler_params=kernel_params(),
            cost_estimate=told(3),
            name=name,
        )(kept, *moved, *blocks, gain.astype(jnp.float32)[None])
        pieces = outs[keep : keep + tiles]
        return (outs[0] if keep else None), pieces, (outs[-1] if add else None)


class HeadGather:
    def __init__(self, own):
        chips = lax.axis_size("head") // 2
        self.steps = [own] + [[chip_move(part, step) for part in own] for step in range(1, chips)]

    def edge(self):
        return tuple(part for parts in self.steps[1:] for part in parts)

    def rows(self, *gates):
        chips = len(self.steps)
        place = lax.axis_index("head")
        chip, core = place // 2, place % 2
        height = self.steps[0][0].shape[0]
        count = len(self.steps[0])
        pieces, places, origins = [], [], []
        for step, parts in enumerate(self.steps):
            at = 2 * ((chip - step + chips) % chips)
            for other in range(2):
                for turn, part in enumerate(parts):
                    if other:
                        part = core_swap(after(part, *gates) if gates and step else part)
                    origins.append((len(places), turn * height))
                    pieces.append(part)
                places.append((at + (1 - core if other else core)) * count * height)
        places = jnp.stack(places).astype(jnp.int32)
        rows = 2 * chips * count * height
        (whole,) = place_rows(pieces, places, origins, rows, [pieces[0].shape[1]])
        return whole


def exchange_sum(block, axis, bits):
    devices = range(lax.axis_size(axis))
    block = block.astype(jnp.bfloat16)
    for bit in bits:
        other = lax.ppermute(block, axis, [(i, i ^ bit) for i in devices])
        block = (block.astype(jnp.float32) + other.astype(jnp.float32)).astype(jnp.bfloat16)
    return block


def bits_of(axis):
    bits, bit = [], 1
    while bit < lax.axis_size(axis):
        bits.append(bit)
        bit *= 2
    return bits


def lane_of(shape):
    return lax.broadcasted_iota(jnp.int32, shape, 1)


def rolled(values, shift):
    return pltpu.roll(values, shift % LANES, 1)


def swapped_halves(values):
    lane = lane_of(values.shape)
    return jnp.where(lane % 64 < 32, rolled(values, -32), rolled(values, 32))


def half_lanes(values, half):
    lane = lane_of(values.shape)
    return jnp.where(lane < 64 if half == 0 else lane >= 64, values, 0.0)


def in_half(values, have, want):
    kept = half_lanes(values, have)
    return kept if have == want else rolled(kept, 64)


def half_sums(values):
    row = lax.broadcasted_iota(jnp.int32, (LANES, LANES), 0)
    ones = jnp.where(row // 64 == lane_of((LANES, LANES)) // 64, 1.0, 0.0).astype(jnp.bfloat16)
    return forward_product(values.astype(jnp.bfloat16), ones)


def half_softmax(values):
    lane = lane_of(values.shape)
    low = lane < 64
    first = jnp.max(jnp.where(low, values, -jnp.inf), axis=1, keepdims=True)
    second = jnp.max(jnp.where(low, -jnp.inf, values), axis=1, keepdims=True)
    powers = jnp.exp(values - jnp.where(low, first, second))
    first = jnp.sum(jnp.where(low, powers, 0.0), axis=1, keepdims=True)
    second = jnp.sum(jnp.where(low, 0.0, powers), axis=1, keepdims=True)
    return powers * jnp.where(low, 1.0 / first, 1.0 / second)


def group(ref_or_value, index):
    return ref_or_value[:, index * LANES : (index + 1) * LANES]


class Sizes:
    def __init__(self, shard, heads, kv_heads):
        self.shard, self.heads, self.kv = shard, heads, kv_heads
        self.each = heads // kv_heads
        self.query_groups = heads // 2
        self.key_groups = (kv_heads + 1) // 2
        self.linear = (heads + 2 * kv_heads) * 64
        self.span = shard + WIN
        self.kv_lanes = 2 * kv_heads * 64
        self.halo_lanes = self.kv_lanes + kv_heads * LANES

    def key_place(self, g):
        return g // 2, g % 2

    def value_place(self, g):
        return (self.kv + g) // 2, (self.kv + g) % 2


def prepare_kernel(sizes, lin_ref, cos_ref, sin_ref, meta_ref, mapq_ref, mapk_ref, rot_ref, phi_ref, halo_ref, whole_ref, first_ref):
    shard = sizes.shard
    wide = []
    for index in range(sizes.linear // LANES):
        part = group(lin_ref, index)
        turned = part * group(cos_ref, index) + swapped_halves(part) * group(sin_ref, index)
        rot_ref[:, index * LANES : (index + 1) * LANES] = turned.astype(jnp.bfloat16)
        wide.append(turned.astype(jnp.bfloat16))
    for index in range(sizes.query_groups):
        both = forward_product(wide[index], mapq_ref[index])
        for half in range(2):
            at = (2 * index + half) * LANES
            phi = half_softmax(group(both, half))
            phi_ref[:, at : at + LANES] = phi.astype(jnp.bfloat16)
    kv_groups = wide[sizes.query_groups :]
    phis = []
    for index in range(sizes.key_groups):
        both = forward_product(kv_groups[index], mapk_ref[index])
        for half in range(min(2, sizes.kv - 2 * index)):
            at = (sizes.heads + 2 * index + half) * LANES
            phi = half_softmax(group(both, half)).astype(jnp.bfloat16)
            phi_ref[:, at : at + LANES] = phi
            phis.append(phi)
    halo_ref[:, : sizes.kv_lanes] = jnp.concatenate(kv_groups, axis=1)[shard - WIN :]
    halo_ref[:, sizes.kv_lanes :] = jnp.concatenate(phis, axis=1)[shard - WIN :]
    keep_whole, keep_first = meta_ref[:, 0:1], meta_ref[:, 1:2]
    for g in range(sizes.kv):
        at, half = sizes.value_place(g)
        values = in_half(kv_groups[at].astype(jnp.float32), half, 0)
        values = jnp.where(lane_of(values.shape) == 64, 1.0, values).astype(jnp.bfloat16)
        phi = phis[g].astype(jnp.float32)
        for keep, ref in ((keep_whole, whole_ref), (keep_first, first_ref)):
            state = left_dot(values, (phi * keep).astype(jnp.bfloat16))
            ref[g] = state[:STATE_ROWS].astype(jnp.bfloat16)


def near_and_far(sizes, meta_ref, keys_ref):
    shape = (sizes.shard, sizes.span)
    row = lax.broadcasted_iota(jnp.int32, shape, 0)
    column = lax.broadcasted_iota(jnp.int32, shape, 1)
    same = meta_ref[:, 2:3] == keys_ref[0:1, :]
    near = same & (column > row) & (column <= row + WIN)
    far = same & (column <= row)
    return near, far


def twice(values):
    return jnp.concatenate([values] * 2, axis=0)


def stacked(parts):
    return jnp.concatenate(parts, axis=0)


def with_halo(sizes, rot_ref, phi_ref, halo_ref, g):
    out = []
    for at, half in (sizes.key_place(g), sizes.value_place(g)):
        own = group(rot_ref, sizes.query_groups + at)
        before = group(halo_ref, at)
        wide = stacked([before, own]).astype(jnp.float32)
        out.append([in_half(wide, half, want) for want in range(2)])
    phi = stacked(
        [
            halo_ref[:, sizes.kv_lanes + g * LANES : sizes.kv_lanes + (g + 1) * LANES],
            group(phi_ref, sizes.heads + g),
        ]
    )
    return out[0], out[1], phi


def value_sides(values, weight):
    ones = jnp.full(values[0].shape, weight, jnp.float32)
    sides = []
    for half in range(2):
        side = jnp.concatenate([values[half], half_lanes(ones, half)], axis=1)
        sides.append(side.astype(jnp.bfloat16))
    return sides


def state_sides(state, weight):
    totals = jnp.broadcast_to(state[64:65].astype(jnp.float32) * weight, (64, LANES))
    totals = totals.astype(jnp.bfloat16)
    none = jnp.zeros_like(totals)
    return [
        stacked([state[:64], none, totals, none]),
        stacked([none, state[:64], none, totals]),
    ]


def pairs_of(sizes, g):
    return range(g * sizes.each // 2, (g + 1) * sizes.each // 2)


def attend_kernel(sizes, rot_ref, phi_ref, halo_ref, state_ref, meta_ref, keys_ref, att_ref, den_ref):
    shard = sizes.shard
    near, far = near_and_far(sizes, meta_ref, keys_ref)
    reach = meta_ref[:, 3:4]
    for g in range(sizes.kv):
        pairs = pairs_of(sizes, g)
        count = len(pairs)
        near_all, far_all = stacked([near] * count), stacked([far] * count)
        keys, values, phi_key = with_halo(sizes, rot_ref, phi_ref, halo_ref, g)
        value_pair = value_sides(values, 1.0)
        state_pair = state_sides(state_ref[g], 1.0)
        queries = stacked([group(rot_ref, p) for p in pairs])
        total = None
        for half in range(2):
            scores = right_dot(queries, keys[half].astype(jnp.bfloat16)) * 0.125
            phi = stacked([group(phi_ref, 2 * p + half) for p in pairs])
            kernel = right_dot(phi, phi_key)
            weights = jnp.where(near_all, jnp.exp(scores), jnp.where(far_all, kernel, 0.0))
            reached = (phi.astype(jnp.float32) * stacked([reach] * count)).astype(jnp.bfloat16)
            term = forward_product(weights.astype(jnp.bfloat16), value_pair[half])
            term = term + right_dot(reached, state_pair[half])
            total = term if total is None else total + term
        mixed = total[:, :LANES] / total[:, LANES:]
        for turn, p in enumerate(pairs):
            rows = slice(turn * shard, (turn + 1) * shard)
            lanes = slice(p * LANES, (p + 1) * LANES)
            att_ref[:, lanes] = mixed[rows].astype(jnp.bfloat16)
            den_ref[:, lanes] = total[rows, LANES:]


def feature_back(phi, grads):
    phi = phi.astype(jnp.float32)
    return (phi * (grads - half_sums(phi * grads))).astype(jnp.bfloat16)


def unrotated(grads, cos, sin):
    return grads * cos - swapped_halves(grads) * sin


def output_grads(sizes, pairs, att_ref, den_ref, grad_ref):
    grads = stacked([group(grad_ref, p) for p in pairs]).astype(jnp.float32)
    mixed = stacked([group(att_ref, p) for p in pairs]).astype(jnp.float32)
    inverse = 1.0 / stacked([group(den_ref, p) for p in pairs])
    grad_num = (grads * inverse).astype(jnp.bfloat16)
    grad_den = -half_sums(grads * mixed) * inverse
    rough = grad_den.astype(jnp.bfloat16)
    rest = (grad_den - rough.astype(jnp.float32)).astype(jnp.bfloat16)
    lane = lane_of(grad_den.shape)
    grad_den = jnp.where(lane % 64 < 32, rough.astype(jnp.float32), rest.astype(jnp.float32))
    return jnp.concatenate([grad_num, grad_den.astype(jnp.bfloat16)], axis=1)


def carry_kernel(sizes, phi_ref, meta_ref, att_ref, den_ref, grad_ref, carry_ref):
    reach = meta_ref[:, 3:4]
    for g in range(sizes.kv):
        pairs = pairs_of(sizes, g)
        reach_all = stacked([reach] * len(pairs))
        both = output_grads(sizes, pairs, att_ref, den_ref, grad_ref)
        state_sum = []
        for half in range(2):
            phi = stacked([group(phi_ref, 2 * p + half) for p in pairs])
            reached = (phi.astype(jnp.float32) * reach_all).astype(jnp.bfloat16)
            state_sum.append(left_dot(both, reached))
        low, high = state_sum
        totals = low[128:129] + low[160:161] + high[192:193] + high[224:225]
        state_grad = stacked(
            [low[:64] + high[64:128], jnp.broadcast_to(totals, (STATE_ROWS - 64, LANES))]
        )
        carry_ref[g] = state_grad.astype(jnp.bfloat16)


def backward_kernel(sizes, rot_ref, phi_ref, halo_ref, state_ref, meta_ref, keys_ref, att_ref, den_ref, grad_ref, cos_ref, sin_ref, mapq_ref, lin_ref, own_ref, back_ref, map_ref):
    shard = sizes.shard
    near, far = near_and_far(sizes, meta_ref, keys_ref)
    reach = meta_ref[:, 3:4]

    @pl.when(pl.program_id(0) == 0)
    def _():
        map_ref[...] = jnp.zeros_like(map_ref)

    kv_grads = [jnp.zeros((sizes.span, LANES), jnp.float32) for _ in range(sizes.kv_lanes // LANES)]
    for g in range(sizes.kv):
        pairs = pairs_of(sizes, g)
        count = len(pairs)
        near_all, far_all = stacked([near] * count), stacked([far] * count)
        reach_all = stacked([reach] * count)
        keys, values, phi_key = with_halo(sizes, rot_ref, phi_ref, halo_ref, g)
        value_pair = value_sides(values, 1.0 / 32.0)
        state_pair = state_sides(state_ref[g], 1.0 / 32.0)
        queries = stacked([group(rot_ref, p) for p in pairs])
        both = output_grads(sizes, pairs, att_ref, den_ref, grad_ref)
        grad_num = both[:, :LANES]
        grad_query = None
        key_sum, value_sum, phi_sum = [], [], None
        back = [[None, None] for _ in pairs]
        for half in range(2):
            key_half = keys[half].astype(jnp.bfloat16)
            scores = right_dot(queries, key_half) * 0.125
            phi = stacked([group(phi_ref, 2 * p + half) for p in pairs])
            kernel = right_dot(phi, phi_key)
            powers = jnp.exp(scores)
            weights = jnp.where(near_all, powers, jnp.where(far_all, kernel, 0.0))
            weights = weights.astype(jnp.bfloat16)
            grad_weights = right_dot(both, value_pair[half])
            grad_scores = jnp.where(near_all, grad_weights * powers, 0.0).astype(jnp.bfloat16)
            grad_kernel = jnp.where(far_all, grad_weights, 0.0).astype(jnp.bfloat16)
            term = forward_product(grad_scores, key_half)
            grad_query = term if grad_query is None else grad_query + term
            key_sum.append(left_dot(grad_scores, queries))
            value_sum.append(left_dot(weights, grad_num))
            term = left_dot(grad_kernel, phi)
            phi_sum = term if phi_sum is None else phi_sum + term
            grad_phi = forward_product(grad_kernel, phi_key)
            grad_phi = grad_phi + forward_product(both, state_pair[half]) * reach_all
            projected = feature_back(phi, grad_phi)
            for turn in range(count):
                back[turn][half] = projected[turn * shard : (turn + 1) * shard]
        for turn, p in enumerate(pairs):
            pair = jnp.concatenate(back[turn], axis=1)
            grad = grad_query[turn * shard : (turn + 1) * shard] * 0.125
            grad = grad + right_dot(pair, mapq_ref[p])
            grad = unrotated(grad, group(cos_ref, p), group(sin_ref, p))
            lin_ref[:, p * LANES : (p + 1) * LANES] = grad.astype(jnp.bfloat16)
            map_ref[p] += left_dot(group(rot_ref, p), pair)
        for (at, half), sums, scale in (
            (sizes.key_place(g), key_sum, 0.125),
            (sizes.value_place(g), value_sum, 1.0),
        ):
            total = in_half(sums[0], 0, half) + in_half(sums[1], 1, half)
            kv_grads[at] = kv_grads[at] + total * scale
        at = sizes.kv_lanes + g * LANES
        own_ref[:, at : at + LANES] = phi_sum[WIN:]
        back_ref[:, at : at + LANES] = phi_sum[:WIN].astype(jnp.bfloat16)
    for at, grads in enumerate(kv_grads):
        lanes = slice(at * LANES, (at + 1) * LANES)
        own_ref[:, lanes] = grads[WIN:]
        back_ref[:, lanes] = grads[:WIN].astype(jnp.bfloat16)


def key_kernel(sizes, rot_ref, phi_ref, meta_ref, own_ref, back_ref, whole_ref, first_ref, cos_ref, sin_ref, mapk_ref, lin_ref, map_ref):
    shard = sizes.shard

    @pl.when(pl.program_id(0) == 0)
    def _():
        map_ref[...] = jnp.zeros_like(map_ref)

    total = own_ref[...]
    returned = back_ref[...].astype(jnp.float32)
    if shard > WIN:
        total = stacked([total[: shard - WIN], total[shard - WIN :] + returned])
    else:
        total = total + returned
    kv_groups = sizes.kv_lanes // LANES
    kv_grads = [group(total, at) for at in range(kv_groups)]
    back = []
    for g in range(sizes.kv):
        at, half = sizes.value_place(g)
        values = in_half(group(rot_ref, sizes.query_groups + at).astype(jnp.float32), half, 0)
        values = jnp.where(lane_of(values.shape) == 64, 1.0, values).astype(jnp.bfloat16)
        phi = group(phi_ref, sizes.heads + g)
        grad_phi = total[:, sizes.kv_lanes + g * LANES : sizes.kv_lanes + (g + 1) * LANES]
        grad_value = None
        for column, ref in ((0, whole_ref), (1, first_ref)):
            keep = meta_ref[:, column : column + 1]
            state = stacked([ref[g], jnp.zeros((LANES - STATE_ROWS, LANES), jnp.bfloat16)])
            grad_phi = grad_phi + forward_product(values, state) * keep
            term = right_dot(phi, state) * keep
            grad_value = term if grad_value is None else grad_value + term
        kv_grads[at] = kv_grads[at] + in_half(grad_value, 0, half)
        back.append(feature_back(phi, grad_phi))
    if len(back) % 2:
        back.append(jnp.zeros_like(back[0]))
    for index in range(sizes.key_groups):
        pair = jnp.concatenate(back[2 * index : 2 * index + 2], axis=1)
        kv_grads[index] = kv_grads[index] + right_dot(pair, mapk_ref[index])
        map_ref[index] += left_dot(group(rot_ref, sizes.query_groups + index), pair)
    for at in range(kv_groups):
        cos = group(cos_ref, sizes.query_groups + at)
        sin = group(sin_ref, sizes.query_groups + at)
        lanes = slice(at * LANES, (at + 1) * LANES)
        lin_ref[:, lanes] = unrotated(kv_grads[at], cos, sin).astype(jnp.bfloat16)


def by_row(kernel, name, rows, inputs, outputs, microseconds):
    def spec(shape, kind):
        rest = tuple(shape[1:])
        none = (0,) * len(rest)
        if kind == "all":
            return pl.BlockSpec(shape, lambda r: (0,) + none)
        first = shape[0] // rows if kind == "flat" else None
        return pl.BlockSpec((first,) + rest, lambda r: (r,) + none)

    return pl.pallas_call(
        kernel,
        grid=(rows,),
        in_specs=[spec(a.shape, kind) for a, kind in inputs],
        out_specs=[spec(shape.shape, kind) for shape, kind in outputs],
        out_shape=[shape for shape, _ in outputs],
        compiler_params=pltpu.CompilerParams(vmem_limit_bytes=48 * 1024 * 1024),
        cost_estimate=told(microseconds),
        name=name,
    )(*[a for a, _ in inputs])


def map_pairs(maps):
    count = maps.shape[0]
    wide = jnp.concatenate([maps, -maps], axis=2)
    if count % 2:
        wide = jnp.concatenate([wide, jnp.zeros_like(wide[:1])], axis=0)
    wide = wide.reshape(-1, 2, 64, LANES)
    none = jnp.zeros_like(wide[:, 0])
    return jnp.concatenate(
        [
            jnp.concatenate([wide[:, 0], none], axis=2),
            jnp.concatenate([none, wide[:, 1]], axis=2),
        ],
        axis=1,
    )


def maps_from_pairs(pairs, count):
    first = pairs[:, :64, :64] - pairs[:, :64, 64:128]
    second = pairs[:, 64:, 128:192] - pairs[:, 64:, 192:]
    return jnp.stack([first, second], axis=1).reshape(-1, 64, 64)[:count]


def rope_tables(positions, sizes):
    inverse = rope_base ** (-jnp.arange(0, 64, 2, dtype=jnp.float32) / 64)
    angle = positions.astype(jnp.float32)[:, None] * inverse[None, :]
    cosine, sine = jnp.cos(angle), jnp.sin(angle)
    turning = sizes.heads + sizes.kv
    cosine = jnp.tile(jnp.concatenate([cosine, cosine], axis=1), (1, turning))
    sine = jnp.tile(jnp.concatenate([-sine, sine], axis=1), (1, turning))
    rest = (positions.shape[0], sizes.kv * 64)
    return (
        jnp.concatenate([cosine, jnp.ones(rest, jnp.float32)], axis=1),
        jnp.concatenate([sine, jnp.zeros(rest, jnp.float32)], axis=1),
    )


def fixed(shape):
    return pl.BlockSpec(shape, lambda t: (0,) * len(shape), pipeline_mode=pl.Buffered(1))


def mlp_forward(rows, cotangent, weights, microseconds):
    count, width = rows.shape
    chunk = weights.shape[1] // 3
    tile = min(256, chunk)
    tiles = chunk // tile
    part = min(512, count)

    def kernel(x_ref, c_ref, gate_ref, up_ref, down_ref, grad_gate_ref, grad_up_ref, inner_ref):
        def one(turn, nothing):
            at = pl.ds(pl.multiple_of(turn * part, part), part)
            x = x_ref[at, :]
            gate = forward_product(x, gate_ref[...])
            up = forward_product(x, up_ref[...])
            grad_inner = forward_product(c_ref[at, :], down_ref[...])
            sigmoid = 1.0 / (1.0 + jnp.exp(-gate))
            swish = gate * sigmoid
            grad_gate = grad_inner * up * (sigmoid * (1.0 + gate * (1.0 - sigmoid)))
            grad_gate_ref[at, :] = grad_gate.astype(jnp.bfloat16)
            grad_up_ref[at, :] = (grad_inner * swish).astype(jnp.bfloat16)
            inner_ref[at, :] = (swish * up).astype(jnp.bfloat16)
            return nothing

        lax.fori_loop(0, count // part, one, 0)

    def columns(shift):
        return pl.BlockSpec((width, tile), lambda t: (0, t + shift))

    out = pl.BlockSpec((count, tile), lambda t: (0, t))
    shape = jax.ShapeDtypeStruct((count, chunk), jnp.bfloat16)
    return pl.pallas_call(
        kernel,
        grid=(tiles,),
        in_specs=[fixed(rows.shape), fixed(cotangent.shape)]
        + [columns(shift * tiles) for shift in range(3)],
        out_specs=[out] * 3,
        out_shape=[shape] * 3,
        compiler_params=kernel_params(),
        cost_estimate=told(microseconds),
        name="hidden_units",
    )(rows, cotangent, weights, weights, weights)


def turned_product(terms, before, dtype, microseconds, split=False, weigh=None):
    count, width = terms[0][0].shape[0], terms[0][1].shape[0]
    tile = min(512, width)
    tiles = width // tile
    chips = lax.axis_size("head") // 2
    rows = count // (2 * chips)
    core = (lax.axis_index("head") % 2).astype(jnp.int32)
    extra = [] if before is None else [before]
    extra += [] if weigh is None else [weigh[0], weigh[1].astype(jnp.float32)[None]]

    def kernel(core_ref, *refs):
        total = None if before is None else refs[2 * len(terms)][...]
        for left_ref, weight_ref in zip(refs, refs[len(terms) : 2 * len(terms)], strict=False):
            term = right_dot(left_ref[...], weight_ref[...])
            total = term if total is None else total + term
        if weigh is not None:
            rows_ref, factors_ref = refs[2 * len(terms) + len(extra) - 2 :][:2]
            column = jnp.sum(total * rows_ref[...].astype(jnp.float32), axis=0, keepdims=True)
            refs[-2][...] = column * factors_ref[...]
            refs = refs[:-2] + refs[-1:]
        if not split:
            refs[-1][...] = total.astype(dtype)
            return
        mine_ref, *their_refs, held_ref = refs[-2 - tiles :]
        held_ref[...] = total.astype(dtype)

        def take(out_ref, which):
            for chip in range(chips):
                at = pl.multiple_of((2 * chip + which) * rows, rows)
                out_ref[chip] = held_ref[pl.ds(at, rows), :]

        take(mine_ref, core_ref[0])
        for turn, their_ref in enumerate(their_refs):
            pl.when(pl.program_id(0) == turn)(
                functools.partial(take, their_ref, 1 - core_ref[0])
            )

    def rows_of(section, chunk):
        return pl.BlockSpec((tile, chunk), lambda t, at: (t, section))

    def whole(shape):
        return pl.BlockSpec(shape, lambda t, at: (0, 0), pipeline_mode=pl.Buffered(1))

    out = pl.BlockSpec((count, tile), lambda t, at: (0, t))
    part = pl.BlockSpec((chips, rows, tile), lambda t, at: (0, 0, t))
    piece = pl.BlockSpec((chips, rows, tile), lambda t, at: (0, 0, 0))
    line = pl.BlockSpec((1, tile), lambda t, at: (0, t))
    added = [] if before is None else [out]
    added += [] if weigh is None else [out, line]
    lefts = [left for left, _, _ in terms]
    result = pl.pallas_call(
        kernel,
        grid_spec=pltpu.PrefetchScalarGridSpec(
            num_scalar_prefetch=1,
            grid=(tiles,),
            in_specs=[whole(left.shape) for left in lefts]
            + [rows_of(section, left.shape[1]) for left, _, section in terms]
            + added,
            out_specs=([part] + [piece] * tiles if split else [out])
            + ([] if weigh is None else [line]),
            scratch_shapes=[pltpu.VMEM((count, tile), dtype)] if split else [],
        ),
        out_shape=(
            [jax.ShapeDtypeStruct((chips, rows, width), dtype)]
            + [jax.ShapeDtypeStruct((chips, rows, tile), dtype)] * tiles
            if split
            else [jax.ShapeDtypeStruct((count, width), dtype)]
        )
        + ([] if weigh is None else [jax.ShapeDtypeStruct((1, width), jnp.float32)]),
        compiler_params=kernel_params(),
        cost_estimate=told(microseconds),
        name="turned_product",
    )(core[None], *lefts, *[weights for _, weights, _ in terms], *extra)
    return result if split else result[0]


def weight_gradients(sides, microseconds):
    count, width = sides[0][0].shape
    tile = min(512, width)
    lefts, which = [], []
    for left, _ in sides:
        at = next((i for i, other in enumerate(lefts) if other is left), len(lefts))
        if at == len(lefts):
            lefts.append(left)
        which.append(at)
    widths = [right.shape[1] for _, right in sides]
    starts = [sum(widths[:i]) for i in range(len(widths))]

    def kernel(*refs):
        for at, right_ref, start, size in zip(
            which, refs[len(lefts) : -1], starts, widths, strict=True
        ):
            total = left_dot(refs[at][...], right_ref[...])
            refs[-1][:, start : start + size] = total.astype(jnp.bfloat16)

    column = pl.BlockSpec((count, tile), lambda t: (0, t))
    return pl.pallas_call(
        kernel,
        grid=(width // tile,),
        in_specs=[column] * len(lefts) + [fixed(right.shape) for _, right in sides],
        out_specs=pl.BlockSpec((tile, sum(widths)), lambda t: (t, 0)),
        out_shape=jax.ShapeDtypeStruct((width, sum(widths)), jnp.bfloat16),
        compiler_params=kernel_params(),
        cost_estimate=told(microseconds),
        name="weight_gradients",
    )(*lefts, *[right for _, right in sides])


def attended_back(grads, weights, lowrank_up, lowrank_down, microseconds):
    count, width = grads.shape
    heads, rank = lowrank_down.shape
    part = min(256, count)

    def kernel(x_ref, w_ref, up_ref, down_ref, out_ref, low_ref):
        low = (adapter_scale * right_dot(x_ref[...], up_ref[...])).astype(jnp.bfloat16)
        total = forward_product(x_ref[...], w_ref[...]) + right_dot(low, down_ref[...])
        out_ref[...] = total.astype(jnp.bfloat16)
        low_ref[...] = low

    def rows(size):
        return pl.BlockSpec((part, size), lambda t: (t, 0))

    return pl.pallas_call(
        kernel,
        grid=(count // part,),
        in_specs=[rows(width), fixed(weights.shape), fixed(lowrank_up.shape), fixed(lowrank_down.shape)],
        out_specs=[rows(heads), rows(rank)],
        out_shape=[
            jax.ShapeDtypeStruct((count, heads), jnp.bfloat16),
            jax.ShapeDtypeStruct((count, rank), jnp.bfloat16),
        ],
        compiler_params=kernel_params(),
        cost_estimate=told(microseconds),
        name="attended_back",
    )(grads, weights, lowrank_up, lowrank_down)


def document_facts(document_index, shard):
    seq_index = lax.axis_index("seq")
    count = lax.axis_size("seq")
    rows = document_index.shape[0]
    documents = document_index.astype(jnp.float32)
    missing = jnp.full((rows, 1), -1.0, jnp.float32)

    def last_of(block):
        at = jnp.clip(block * shard + shard - 1, 0, count * shard - 1)
        found = lax.dynamic_slice_in_dim(documents, at, 1, 1)
        return jnp.where((block >= 0) & (block < count), found, missing)

    def carried_of(block):
        at = jnp.clip(block * shard - WIN - 1, 0, count * shard - 1)
        found = lax.dynamic_slice_in_dim(documents, at, 1, 1)
        return jnp.where((block >= 1) & (block < count), found, missing - 1.0)

    padded = jnp.concatenate([jnp.broadcast_to(missing, (rows, WIN)), documents], axis=1)
    key_documents = lax.dynamic_slice_in_dim(padded, seq_index * shard, shard + WIN, 1)
    own = key_documents[:, WIN:]
    position = jnp.arange(shard)[None, :]
    keep_whole = own == own[:, shard - 1 :]
    keep_first = (position < shard - WIN) & (own == own[:, shard - WIN - 1 : shard - WIN])
    reach = own == carried_of(seq_index)
    columns = [keep_whole, keep_first, own, reach]
    meta = jnp.stack([column.astype(jnp.float32) for column in columns], axis=-1)
    meta = jnp.concatenate([meta, jnp.zeros_like(meta)], axis=-1)
    return meta, key_documents[:, None, :], last_of, carried_of


def masked(block, mask):
    return block.astype(jnp.float32) * mask.astype(jnp.float32).reshape(-1, 1, 1, 1)


class Carries:
    def __init__(self, last_of, carried_of, rows):
        self.index = lax.axis_index("seq")
        self.count = lax.axis_size("seq")
        self.even = self.index % 2 == 0
        self.rows = rows // 2
        self.pair = self.index - self.index % 2
        self.last_of, self.carried_of = last_of, carried_of
        self.steps = []
        distance = 1
        while distance < self.count // 2:
            self.steps.append(distance)
            distance *= 2

    def half(self, values, own):
        at = jnp.where(self.even == own, 0, self.rows)
        return lax.dynamic_slice_in_dim(values, at, self.rows, 0)

    def end(self, back):
        return self.half(self.last_of(self.pair - back), True)

    def other(self, values):
        values = values.astype(jnp.bfloat16)
        return lax.ppermute(values, "seq", [(i, i ^ 1) for i in range(self.count)])

    def pick(self, first, second):
        return jnp.where(self.even, first.astype(jnp.float32), second.astype(jnp.float32))

    def split(self, values):
        mine, theirs = self.half(values, True), self.other(self.half(values, False))
        return self.pick(mine, theirs), self.pick(theirs, mine)

    def join(self, even, odd):
        kept, got = self.pick(even, odd), self.other(self.pick(odd, even))
        return jnp.concatenate([self.pick(kept, got), self.pick(got, kept)], axis=0)

    def reach(self):
        even = self.half(self.carried_of(self.pair), True) == self.end(2)
        odd = self.half(self.carried_of(self.pair + 1), True) == self.end(1)
        return even, odd

    def forward(self, whole, first, tail):
        before, halo = shifted(first, 1), shifted(tail, 1)
        even, odd = self.split(whole)
        window = odd + masked(even, self.end(0) == self.end(-1))
        sums = None
        for distance in self.steps:
            if sums is None:
                got = shifted(jnp.stack([window, even]).astype(jnp.bfloat16), 2)
                got = got.astype(jnp.float32)
                sums = got[1], got[0]
                got = got[0]
            else:
                got = shifted(window.astype(jnp.bfloat16), 2 * distance)
                there = self.end(2 * distance - 1)
                sums = (
                    sums[0] + masked(got, there == self.end(2)),
                    sums[1] + masked(got, there == self.end(1)),
                )
            window = window + masked(got, self.end(2 * distance - 1) == self.end(-1))
        reach = self.reach()
        sums = after(sums, before, halo)
        total = self.join(masked(sums[0], reach[0]), masked(sums[1], reach[1]))
        return (total + before.astype(jnp.float32)).astype(jnp.bfloat16), halo

    def backward(self, grads, back, other):
        first, returned = shifted(grads, -1), shifted(back, -1)
        even, odd = self.split(grads)
        reach = self.reach()
        even, odd = masked(even, reach[0]), masked(odd, reach[1])
        even, odd = after((even, odd), other)
        window = None
        for distance in reversed(self.steps):
            there = self.end(2 * distance - 1)
            linked = 0.0 if window is None else masked(window, there == self.end(-1))
            if distance == 1:
                sent = jnp.stack([linked + odd, even]).astype(jnp.bfloat16)
                got = shifted(sent, -2).astype(jnp.float32)
                window = got[0] if window is None else window + got[0]
                direct = got[1]
            else:
                sent = linked + masked(odd, there == self.end(1))
                sent = sent + masked(even, there == self.end(2))
                got = shifted(sent.astype(jnp.bfloat16), -2 * distance).astype(jnp.float32)
                window = got if window is None else window + got
        even = masked(window, self.end(0) == self.end(-1)) + direct
        even, window = after((even, window), first, returned)
        return self.join(even, window).astype(jnp.bfloat16), first, returned


def body(
    tokens,
    cotangent,
    first_norm_gain,
    second_norm_gain,
    query_weight,
    key_weight,
    value_weight,
    output_weight,
    gate_weight,
    up_weight,
    down_weight,
    adapter_down_weight,
    adapter_query_weight,
    adapter_key_weight,
    adapter_value_weight,
    adapter_output_down,
    adapter_output_up,
    hedgehog_query_weight,
    hedgehog_key_weight,
    document_index,
):
    row_count, shard, width = tokens.shape
    seq_index = lax.axis_index("seq")
    heads_here = hedgehog_query_weight.shape[0]
    kv_here = hedgehog_key_weight.shape[0]
    sizes = Sizes(shard, heads_here, kv_here)
    rank = adapter_query_weight.shape[0]
    tokens_here = row_count * shard
    block_rows = query_weight.shape[0]
    hidden_units = gate_weight.shape[1]
    chunk = hidden_units // 2
    query_width, key_width = query_weight.shape[1], key_weight.shape[1]
    key_end = query_width + key_width

    out_width = output_weight.shape[0]
    first_gather = Gather(
        jnp.concatenate([query_weight, key_weight, value_weight, output_weight.T], axis=1)
    )
    first_gather.advance(quarters=4)
    down_turned = down_weight.T
    early, late = [
        Gather(
            jnp.concatenate(
                [gate_weight[:, span], up_weight[:, span], down_turned[:, span]], axis=1
            )
        )
        for span in (slice(0, chunk), slice(chunk, hidden_units))
    ]
    early.advance(*first_gather.edge())
    complete_qkv, out_turned = first_gather.assemble(sizes.linear, out_width)

    adapters = jnp.zeros((3 * rank, sizes.linear), jnp.bfloat16)
    adapters = lax.dynamic_update_slice(adapters, adapter_query_weight, (0, 0))
    adapters = lax.dynamic_update_slice(adapters, adapter_key_weight, (rank, query_width))
    adapters = lax.dynamic_update_slice(adapters, adapter_value_weight, (2 * rank, key_end))
    positions = seq_index * shard + jnp.arange(shard)
    cosine, sine = rope_tables(positions, sizes)
    map_query, map_key = map_pairs(hedgehog_query_weight), map_pairs(hedgehog_key_weight)
    meta, key_documents, last_of, carried_of = document_facts(document_index, shard)

    flattened = tokens.reshape(tokens_here, width).astype(jnp.float32)
    scale_one = lax.rsqrt(jnp.mean(flattened * flattened, axis=-1, keepdims=True) + epsilon)
    normalized_input = flattened * scale_one * first_norm_gain.astype(jnp.float32)
    normalized_input = normalized_input.astype(jnp.bfloat16)
    lowrank_input = forward_product(normalized_input, adapter_down_weight).astype(jnp.bfloat16)
    linear = forward_product(normalized_input, complete_qkv) + adapter_scale * forward_product(
        lowrank_input, adapters
    )
    low = functools.partial(jax.ShapeDtypeStruct, dtype=jnp.bfloat16)
    wide = functools.partial(jax.ShapeDtypeStruct, dtype=jnp.float32)
    phi_lanes = (heads_here + kv_here) * LANES
    states = low((row_count, kv_here, STATE_ROWS, LANES))
    rotated, phi, tail, whole, first = by_row(
        functools.partial(prepare_kernel, sizes),
        "prepare",
        row_count,
        [
            (linear, "flat"),
            (cosine, "all"),
            (sine, "all"),
            (meta, "row"),
            (map_query, "all"),
            (map_key, "all"),
        ],
        [
            (low((tokens_here, sizes.linear)), "flat"),
            (low((tokens_here, phi_lanes)), "flat"),
            (low((row_count, WIN, sizes.halo_lanes)), "row"),
            (states, "row"),
            (states, "row"),
        ],
        16,
    )
    early.advance(rotated)
    tail, whole, first = after((tail, whole, first), *early.edge())
    carries = Carries(last_of, carried_of, row_count)
    carry, halo = carries.forward(whole, first, tail)
    early.advance(carry, halo)
    attended, denominator = by_row(
        functools.partial(attend_kernel, sizes),
        "attend",
        row_count,
        [
            (rotated, "flat"),
            (phi, "flat"),
            (halo, "row"),
            (carry, "row"),
            (meta, "row"),
            (key_documents, "row"),
        ],
        [
            (low((tokens_here, query_width)), "flat"),
            (wide((tokens_here, query_width)), "flat"),
        ],
        8,
    )

    lowrank_output = forward_product(attended, adapter_output_down).astype(jnp.bfloat16)
    out_sum = HeadSum(
        *turned_product(
            [(attended, out_turned, 0), (lowrank_output, (adapter_scale * adapter_output_up.T).astype(jnp.bfloat16), 0)],
            None,
            jnp.bfloat16,
            5,
            split=True,
        )
    )
    out_sent = out_sum.pair()
    own_rows = row_count // lax.axis_size("head")
    first_row = lax.axis_index("head") * own_rows
    own_tokens = lax.dynamic_slice_in_dim(tokens, first_row, own_rows, 0)
    own_tokens = own_tokens.reshape(own_rows * shard, width)
    own_cotangent = lax.dynamic_slice_in_dim(cotangent, first_row, own_rows, 0)
    own_cotangent = own_cotangent.reshape(own_rows * shard, width)

    def normed_forward(total, own, gain):
        hidden = own + total
        scale = lax.rsqrt(jnp.mean(hidden * hidden, axis=1, keepdims=True) + epsilon)
        return hidden, hidden * scale * gain, None

    def normed_backward(total, own, values, gain):
        scale = lax.rsqrt(jnp.mean(values * values, axis=1, keepdims=True) + epsilon)
        unit = values * scale
        inner = total * gain
        inner = inner - unit * jnp.mean(inner * unit, axis=1, keepdims=True)
        grad = own + scale * inner
        return grad, grad, total * unit

    out_sum.kept = after(out_sum.kept, *early.edge())
    early.advance(*out_sent)
    hidden_state, own_normed, _ = out_sum.finish(
        normed_forward, [own_tokens], second_norm_gain, True, False, "second_norm"
    )
    normed_gather = HeadGather(own_normed)
    late.advance(*early.edge())
    first_edge = late.edge()
    late.advance(*normed_gather.edge())
    normed_rows = normed_gather.rows(*first_edge)

    grad_out = cotangent.reshape(tokens_here, width)
    (weights_early,) = early.assemble(3 * chunk)
    gate_early, up_early, inner_early = mlp_forward(normed_rows, grad_out, weights_early, 22)
    gate_early = after(gate_early, *late.edge())
    late.advance(up_early)
    part_early = turned_product(
        [(gate_early, weights_early, 0), (up_early, weights_early, 1)], None, jnp.float32, 14
    )
    grads_early = weight_gradients(
        [
            (normed_rows, gate_early),
            (normed_rows, up_early),
            (grad_out, after(inner_early, part_early)),
        ],
        19,
    )
    late.advance(grads_early)
    scatter_early = Scatter(grads_early, block_rows)
    scatter_early.advance(*late.edge())
    (weights_late,) = late.assemble(3 * chunk)
    gate_late, up_late, inner_late = mlp_forward(normed_rows, grad_out, weights_late, 22)
    gate_late = after(gate_late, *scatter_early.edge())
    scatter_early.advance(up_late)
    normed_two_sum = HeadSum(
        *turned_product(
            [(gate_late, weights_late, 0), (up_late, weights_late, 1)],
            part_early,
            jnp.bfloat16,
            15,
            split=True,
        )
    )
    normed_two_sent = normed_two_sum.pair()
    inner_late = after(inner_late, *normed_two_sent, *scatter_early.edge())
    scatter_early.advance(*normed_two_sent)
    grads_late = weight_gradients(
        [(normed_rows, gate_late), (normed_rows, up_late), (grad_out, inner_late)], 19
    )
    normed_two_sum.kept = after(normed_two_sum.kept, grads_late)
    grad_hidden, branch_pieces, grad_gain_two = normed_two_sum.finish(
        normed_backward,
        [own_cotangent, hidden_state],
        second_norm_gain,
        True,
        True,
        "second_norm_back",
    )
    branch_gather = HeadGather(branch_pieces)
    scatter_early.advance(grad_hidden)
    down_sum = HeadSum(
        *turned_product(
            [(inner_early, weights_early, 2), (after(inner_late, grad_hidden, *scatter_early.sending), weights_late, 2)],
            None,
            jnp.bfloat16,
            1500,
            split=True,
        )
    )
    grad_branch = branch_gather.rows(down_sum.mine)
    scatter_late = Scatter(grads_late, block_rows)
    scatter_late.advance(grad_branch)
    down_sum.mine = after(down_sum.mine, grad_branch)
    down_sum.pair()
    grad_attended, grad_lowrank_out = attended_back(
        grad_branch, out_turned, adapter_output_up, adapter_output_down, 4
    )
    grad_attended = after(grad_attended, *scatter_early.edge(), *down_sum.sent)
    (carry_grads,) = by_row(
        functools.partial(carry_kernel, sizes),
        "carry_back",
        row_count,
        [
            (phi, "flat"),
            (meta, "row"),
            (attended, "flat"),
            (denominator, "flat"),
            (grad_attended, "flat"),
        ],
        [(states, "row")],
        5,
    )
    scatter_late.up, scatter_late.down = after(scatter_late.edge(), carry_grads)
    scatter_late.advance()
    grad_attended = after(grad_attended, *scatter_late.sending)

    own_lanes = sizes.halo_lanes
    grad_query_lin, own_grads, back, map_query_pairs = by_row(
        functools.partial(backward_kernel, sizes),
        "backward",
        row_count,
        [
            (rotated, "flat"),
            (phi, "flat"),
            (halo, "row"),
            (carry, "row"),
            (meta, "row"),
            (key_documents, "row"),
            (attended, "flat"),
            (denominator, "flat"),
            (grad_attended, "flat"),
            (cosine, "all"),
            (sine, "all"),
            (map_query, "all"),
        ],
        [
            (low((tokens_here, query_width)), "flat"),
            (wide((tokens_here, own_lanes)), "flat"),
            (low((row_count, WIN, own_lanes)), "row"),
            (wide(map_query.shape), "all"),
        ],
        2000,
    )
    grad_whole, grad_first, returned = carries.backward(
        carry_grads, back, (grad_query_lin, *scatter_late.edge())
    )
    out_up_gradient = adapter_scale * left_dot(lowrank_output, grad_branch)
    late_edge = scatter_late.edge()
    scatter_late.advance(grad_whole)
    grad_whole = after(grad_whole, *late_edge)
    down_sum.kept = after(down_sum.kept, grad_whole)
    _, layer_pieces, _ = down_sum.finish(
        lambda total, values, gain: (None, values + total, None),
        [hidden_state],
        second_norm_gain,
        False,
        False,
        "layer_rows",
        *branch_gather.edge(),
    )
    layer_gather = HeadGather(layer_pieces)
    layer_rows = layer_gather.rows()
    out_down_gradient = left_dot(grad_lowrank_out, attended)
    fill = scatter_early.total([chunk] * 3, [False, False, True])
    grad_whole = after(grad_whole, out_down_gradient, out_up_gradient, *fill, *layer_pieces)
    mlp_sums = [fill]
    grad_key_lin, map_key_pairs = by_row(
        functools.partial(key_kernel, sizes),
        "keys",
        row_count,
        [
            (rotated, "flat"),
            (phi, "flat"),
            (meta, "row"),
            (own_grads, "flat"),
            (returned, "row"),
            (grad_whole, "row"),
            (grad_first, "row"),
            (cosine, "all"),
            (sine, "all"),
            (map_key, "all"),
        ],
        [
            (low((tokens_here, sizes.kv_lanes)), "flat"),
            (wide(map_key.shape), "all"),
        ],
        7,
    )
    grad_linear = jnp.concatenate([grad_query_lin, grad_key_lin], axis=1)
    lowrank_gradient = (adapter_scale * right_dot(grad_linear, adapters)).astype(jnp.bfloat16)
    kv_section = query_width // sizes.kv_lanes
    normed_sum = HeadSum(
        *turned_product(
            [
                (grad_query_lin, complete_qkv, 0),
                (grad_key_lin, complete_qkv, kv_section),
                (lowrank_gradient, adapter_down_weight, 0),
            ],
            None,
            jnp.bfloat16,
            7,
            split=True,
        )
    )
    normed_sent = normed_sum.pair()
    late_edge = scatter_late.edge()
    scatter_late.advance(*normed_sent)
    last_grads = weight_gradients(
        [
            (normalized_input, grad_query_lin),
            (normalized_input, grad_key_lin),
            (grad_branch, after(attended, *normed_sent, *scatter_late.sending)),
        ],
        10,
    )
    adapter_gradient = adapter_scale * left_dot(lowrank_input, grad_linear)
    down_gradient = left_dot(lowrank_gradient, normalized_input)
    last_scatter = Scatter(last_grads, block_rows)
    last_scatter.advance(*scatter_late.sending)
    normed_sum.kept = after(normed_sum.kept, last_grads, *scatter_late.sending, layer_rows)
    _, tokens_pieces, grad_gain_one = normed_sum.finish(
        normed_backward,
        [grad_hidden, own_tokens],
        first_norm_gain,
        False,
        True,
        "first_norm_back",
    )
    tokens_gather = HeadGather(tokens_pieces)
    grad_tokens_rows = tokens_gather.rows().astype(jnp.float32)
    last_sums = last_scatter.total(
        [query_width, key_width, key_width, out_width], [False, False, False, True]
    )
    mlp_sums.append(scatter_late.total([chunk] * 3, [False, False, True]))

    everywhere = jnp.concatenate(
        [down_gradient, out_up_gradient, grad_gain_one, grad_gain_two], axis=0
    )
    adapter_part = jnp.concatenate(
        [
            adapter_gradient[:rank, :query_width],
            adapter_gradient[rank : 2 * rank, query_width:key_end],
            adapter_gradient[2 * rank :, key_end:],
            out_down_gradient,
        ],
        axis=1,
    )
    maps_part = jnp.concatenate(
        [maps_from_pairs(map_query_pairs, heads_here), maps_from_pairs(map_key_pairs, kv_here)]
    )
    maps_part = jnp.pad(maps_part.reshape(-1, 64), ((0, 0), (0, LANES - 64)))
    small = jnp.concatenate(
        [everywhere.reshape(-1, LANES), adapter_part.reshape(-1, LANES), maps_part], axis=0
    )
    small = after(small.astype(jnp.bfloat16), *scatter_late.edge())
    small = exchange_sum(small, "seq", bits_of("seq"))
    first, second = everywhere.size // LANES, (everywhere.size + adapter_part.size) // LANES
    everywhere = exchange_sum(small[:first], "head", bits_of("head")).astype(jnp.float32)
    everywhere = everywhere.reshape(-1, width)
    small = small.astype(jnp.float32)
    adapter_sum = small[first:second].reshape(adapter_part.shape)
    maps_sum = small[second:, :64].reshape(-1, 64, 64)
    end = 3 * rank + rank

    return (
        layer_rows.reshape(row_count, shard, width),
        grad_tokens_rows.reshape(row_count, shard, width),
        everywhere[end],
        everywhere[end + 1],
        *last_sums,
        jnp.concatenate([part[0] for part in mlp_sums], axis=1),
        jnp.concatenate([part[1] for part in mlp_sums], axis=1),
        jnp.concatenate([part[2] for part in mlp_sums], axis=0),
        everywhere[: 3 * rank].T,
        adapter_sum[:, :query_width],
        adapter_sum[:, query_width:key_end],
        adapter_sum[:, key_end : sizes.linear],
        adapter_sum[:, sizes.linear :].T,
        everywhere[3 * rank : end],
        maps_sum[:heads_here],
        maps_sum[heads_here:],
    )


def solution(mesh):
    in_specs = (
        P(None, "seq", None),
        P(None, "seq", None),
        P(),
        P(),
        P("seq", "head"),
        P("seq", "head"),
        P("seq", "head"),
        P("head", "seq"),
        P("seq", "head"),
        P("seq", "head"),
        P("head", "seq"),
        P(),
        P(None, "head"),
        P(None, "head"),
        P(None, "head"),
        P("head", None),
        P(),
        P("head", None, None),
        P("head", None, None),
        P(),
    )
    out_specs = (
        P(None, "seq", None),
        P(None, "seq", None),
        P(),
        P(),
        P("seq", "head"),
        P("seq", "head"),
        P("seq", "head"),
        P("head", "seq"),
        P("seq", "head"),
        P("seq", "head"),
        P("head", "seq"),
        P(),
        P(None, "head"),
        P(None, "head"),
        P(None, "head"),
        P("head", None),
        P(),
        P("head", None, None),
        P("head", None, None),
    )
    return jax.shard_map(body, mesh=mesh, in_specs=in_specs, out_specs=out_specs, check_vma=False)
```

```python
import functools

import jax
import jax.numpy as jnp
from jax import lax
from jax.experimental import pallas as pl
from jax.experimental.pallas import tpu as pltpu
from jax.sharding import PartitionSpec as P

WIN = 64
LANES = 128
STATE_ROWS = 80
TOLD = 10_000_000

epsilon = 1e-05
rope_base = 500000.0
adapter_scale = 2.0


def forward_product(left, right):
    return jnp.dot(left, right, preferred_element_type=jnp.float32)


def left_dot(left, right):
    return lax.dot_general(
        left, right, (((0,), (0,)), ((), ())), preferred_element_type=jnp.float32
    )


def right_dot(left, right):
    return lax.dot_general(
        left, right, (((1,), (1,)), ((), ())), preferred_element_type=jnp.float32
    )


def shifted(block, distance):
    devices = range(lax.axis_size("seq"))
    route = [(i - distance, i) for i in devices if i - distance in devices]
    return lax.ppermute(block, "seq", route)


def ring_order(count):
    return list(range(0, count, 2)) + list(range(count - 1, 0, -2))


def ring_move(block, step):
    order = ring_order(lax.axis_size("seq"))
    count = len(order)
    return lax.ppermute(block, "seq", [(order[i], order[(i + step) % count]) for i in range(count)])


def ring_index(offset):
    count = lax.axis_size("seq")
    mine = lax.axis_index("seq")
    place = jnp.where(mine % 2 == 0, mine // 2, count - 1 - mine // 2)
    there = (place + offset + count) % count
    return jnp.where(there < count // 2, 2 * there, 2 * (count - 1 - there) + 1).astype(jnp.int32)


def after(value, *others):
    return lax.optimization_barrier((value,) + others)[0]


def told(microseconds):
    return pl.CostEstimate(flops=int(microseconds * TOLD), bytes_accessed=0, transcendentals=0)


def kernel_params():
    return pltpu.CompilerParams(vmem_limit_bytes=56 * 1024 * 1024)


def place_rows(pieces, places, origins, rows, widths):
    starts = [sum(widths[:i]) for i in range(len(widths))]

    def kernel(places_ref, *refs):
        sources, rest = refs[: len(pieces)], refs[len(pieces) :]
        targets, buffers, semaphores = rest[: len(widths)], rest[len(widths) : -1], rest[-1]
        inward, outward = [], []
        for turn, (source, (at, shift)) in enumerate(zip(sources, origins, strict=True)):
            length = source.shape[0]
            held = buffers[turn]
            inward.append(pltpu.make_async_copy(source, held, semaphores.at[turn]))
            first = pl.multiple_of(places_ref[at] + shift, length)
            for target, start, width in zip(targets, starts, widths, strict=True):
                outward.append(
                    pltpu.make_async_copy(
                        held.at[:, pl.ds(start, width)],
                        target.at[pl.ds(first, length), :],
                        semaphores.at[len(sources) + len(outward)],
                    )
                )
        for copy in inward:
            copy.start()
        for turn, copy in enumerate(inward):
            copy.wait()
            for back in outward[turn * len(widths) : (turn + 1) * len(widths)]:
                back.start()
        for copy in outward:
            copy.wait()

    anywhere = pl.BlockSpec(memory_space=pl.ANY)
    size = sum(piece.size for piece in pieces) * 2
    return pl.pallas_call(
        kernel,
        grid_spec=pltpu.PrefetchScalarGridSpec(
            num_scalar_prefetch=1,
            grid=(1,),
            in_specs=[anywhere] * len(pieces),
            out_specs=[anywhere] * len(widths),
            scratch_shapes=[pltpu.VMEM(piece.shape, piece.dtype) for piece in pieces]
            + [pltpu.SemaphoreType.DMA((len(pieces) * (1 + len(widths)),))],
        ),
        out_shape=[jax.ShapeDtypeStruct((rows, width), pieces[0].dtype) for width in widths],
        compiler_params=pltpu.CompilerParams(vmem_limit_bytes=size + 4 * 1024 * 1024),
        cost_estimate=told(1 + size // 4_000_000),
        name="place_rows",
    )(places, *pieces)


class Gather:
    def __init__(self, own):
        self.half = lax.axis_size("seq") // 2
        self.found = {0: own}
        self.up = self.down = own
        self.step = 0

    def advance(self, *gates, quarters=1):
        for _ in range(quarters * max(1, self.half // 4)):
            if self.step == self.half:
                return
            self.step += 1
            cut = self.up.shape[0] // 2
            up, down = self.up, self.down
            if gates:
                up, down = after(up, *gates), after(down, *gates)
            if self.step < self.half:
                self.up, self.down = ring_move(up, 1), ring_move(down, -1)
                self.found[-self.step], self.found[self.step] = self.up, self.down
            else:
                self.found[self.half] = (ring_move(up[:cut], 1), ring_move(down[cut:], -1))

    def edge(self):
        return self.found[self.half] if self.step == self.half else (self.up, self.down)

    def assemble(self, *widths):
        self.advance(quarters=4)
        rows = self.found[0].shape[0]
        offsets = sorted(self.found)
        places = jnp.stack([ring_index(offset) * rows for offset in offsets])
        pieces, origins = [], []
        for at, offset in enumerate(offsets):
            block, shift = self.found[offset], 0
            for part in block if isinstance(block, tuple) else (block,):
                pieces.append(part)
                origins.append((at, shift))
                shift += part.shape[0]
        return place_rows(pieces, places, origins, lax.axis_size("seq") * rows, widths)


def on_block(kernel, grads, others, outs, offset, rows, name):
    cut, columns = rows // 2, grads.shape[1]

    def half_of(length):
        if length == rows:
            return pl.BlockSpec((cut, columns), lambda h, at: (h, 0))
        return pl.BlockSpec((cut, columns), lambda h, at: (0, 0))

    return pl.pallas_call(
        kernel,
        grid_spec=pltpu.PrefetchScalarGridSpec(
            num_scalar_prefetch=1,
            grid=(2,),
            in_specs=[pl.BlockSpec((cut, columns), lambda h, at: (2 * at[0] + h, 0))]
            + [half_of(other.shape[0]) for other in others],
            out_specs=[spec if spec else half_of(shape.shape[0]) for shape, spec in outs],
        ),
        out_shape=[shape for shape, _ in outs],
        compiler_params=kernel_params(),
        cost_estimate=told(2),
        name=name,
    )(ring_index(offset)[None], grads, *others)


class Scatter:
    def __init__(self, grads, rows):
        self.grads, self.rows = grads, rows
        self.half = lax.axis_size("seq") // 2
        self.step = 0

    def shape(self, rows):
        return jax.ShapeDtypeStruct((rows, self.grads.shape[1]), self.grads.dtype)

    def far(self):
        def kernel(at_ref, own_ref, up_ref, down_ref):
            @pl.when(pl.program_id(0) == 0)
            def _():
                up_ref[...] = own_ref[...]

            @pl.when(pl.program_id(0) == 1)
            def _():
                down_ref[...] = own_ref[...]

        outs = [(self.shape(self.rows // 2), None)] * 2
        return on_block(kernel, self.grads, [], outs, self.half, self.rows, "far_block")

    def joined(self, received, offset, which):
        full = received.shape[0] == self.rows

        def kernel(at_ref, own_ref, got_ref, out_ref):
            own, got = own_ref[...].astype(jnp.float32), got_ref[...].astype(jnp.float32)
            if not full:
                got = jnp.where(pl.program_id(0) == which, got, 0.0)
            out_ref[...] = (own + got).astype(out_ref.dtype)

        outs = [(self.shape(self.rows), None)]
        (out,) = on_block(kernel, self.grads, [received], outs, offset, self.rows, "join_block")
        return out

    def advance(self, *gates, quarters=1):
        for _ in range(quarters * max(1, self.half // 4)):
            if self.step == self.half:
                return
            self.step += 1
            offset = self.half - self.step + 1
            if self.step == 1:
                up, down = self.far()
            else:
                up, down = self.joined(self.up, offset, 0), self.joined(self.down, -offset, 1)
            if gates:
                up, down = after(up, *gates), after(down, *gates)
            self.sending = up, down
            self.up, self.down = ring_move(up, 1), ring_move(down, -1)

    def edge(self):
        return self.up, self.down

    def total(self, widths, turned):
        self.advance(quarters=4)
        starts = [sum(widths[:i]) for i in range(len(widths))]
        cut = self.rows // 2
        later = [turn and cut % LANES != 0 for turn in turned]
        turned = [turn and not late for turn, late in zip(turned, later, strict=True)]

        def kernel(at_ref, own_ref, up_ref, down_ref, *out_refs):
            for start, width, turn, out_ref in zip(starts, widths, turned, out_refs, strict=True):
                lanes = slice(start, start + width)
                total = own_ref[:, lanes].astype(jnp.float32) + up_ref[:, lanes].astype(jnp.float32)
                total = total + down_ref[:, lanes].astype(jnp.float32)
                out_ref[...] = total.T if turn else total

        outs = []
        for width, turn in zip(widths, turned, strict=True):
            shape = (width, self.rows) if turn else (self.rows, width)
            block = (width, cut) if turn else (cut, width)
            spec = pl.BlockSpec(block, (lambda h, at: (0, h)) if turn else (lambda h, at: (h, 0)))
            outs.append((jax.ShapeDtypeStruct(shape, jnp.float32), spec))
        sums = on_block(
            kernel, self.grads, [self.up, self.down], outs, 0, self.rows, "own_block"
        )
        return [part.T if late else part for part, late in zip(sums, later, strict=True)]


def core_swap(block):
    count = lax.axis_size("head")
    return lax.ppermute(block, "head", [(i, i ^ 1) for i in range(count)])


def chip_move(block, step):
    count = lax.axis_size("head")
    return lax.ppermute(block, "head", [(i, (i + 2 * step) % count) for i in range(count)])


class HeadSum:
    def __init__(self, mine, *theirs):
        self.mine = mine
        self.got = [core_swap(piece) for piece in theirs]

    def pair(self):
        chips, rows, width = self.mine.shape
        tile = self.tile = min(128, rows)
        chip = (lax.axis_index("head") // 2).astype(jnp.int32)
        cuts, tiles = len(self.got), rows // tile

        def kernel(chip_ref, mine_ref, *refs):
            got_refs, kept_ref, sent_refs = refs[:cuts], refs[cuts], refs[cuts + 1 :]

            def both(step, out_ref):
                at = (chip_ref[0] + step) % chips
                for turn, got_ref in enumerate(got_refs):
                    lanes = slice(turn * got_ref.shape[2], (turn + 1) * got_ref.shape[2])
                    total = mine_ref[at, :, lanes].astype(jnp.float32)
                    total = total + got_ref[at].astype(jnp.float32)
                    out_ref[:, lanes] = total.astype(out_ref.dtype)

            both(0, kept_ref)
            for turn, sent_ref in enumerate(sent_refs):
                pl.when(pl.program_id(0) == turn % tiles)(
                    functools.partial(both, 1 + turn // tiles, sent_ref)
                )

        def cut(size, *first):
            return pl.BlockSpec(first + (tile, size), lambda t, at: (0,) * len(first) + (t, 0))

        count = (chips - 1) * tiles
        piece = pl.BlockSpec((tile, width), lambda t, at: (0, 0))
        self.kept, *self.sent = pl.pallas_call(
            kernel,
            grid_spec=pltpu.PrefetchScalarGridSpec(
                num_scalar_prefetch=1,
                grid=(tiles,),
                in_specs=[cut(width, chips)] + [cut(piece.shape[2], chips) for piece in self.got],
                out_specs=[cut(width)] + [piece] * count,
            ),
            out_shape=[jax.ShapeDtypeStruct((rows, width), jnp.float32)]
            + [jax.ShapeDtypeStruct((tile, width), jnp.bfloat16)] * count,
            compiler_params=kernel_params(),
            cost_estimate=told(2),
            name="pair_sum",
        )(chip[None], self.mine, *self.got)
        return self.sent

    def finish(self, formula, blocks, gain, keep, add, name, *gates):
        rows, width = self.kept.shape
        tile, tiles = self.tile, self.kept.shape[0] // self.tile
        moved = []
        for turn, sent in enumerate(self.sent):
            sent = after(sent, *gates) if gates else sent
            moved.append(chip_move(sent, 1 + turn // tiles))
        kept = after(self.kept, *moved)

        def kernel(kept_ref, *refs):
            moved_refs, refs = refs[: len(moved)], refs[len(moved) :]
            block_refs, gain_ref, out_refs = refs[: len(blocks)], refs[len(blocks)], refs[len(blocks) + 1 :]
            piece_refs = out_refs[keep : keep + tiles]

            def one(turn):
                total = kept_ref[...]
                for moved_ref in moved_refs[turn::tiles]:
                    total = total + moved_ref[...].astype(jnp.float32)
                values = [ref[...].astype(jnp.float32) for ref in block_refs]
                first, piece, column = formula(total, *values, gain_ref[...])
                if keep:
                    out_refs[0][...] = first
                piece_refs[turn][...] = piece.astype(jnp.bfloat16)
                if add:
                    column = jnp.sum(column, axis=0, keepdims=True)
                    out_refs[-1][...] = column if turn == 0 else out_refs[-1][...] + column

            for turn in range(tiles):
                pl.when(pl.program_id(0) == turn)(functools.partial(one, turn))

        block = pl.BlockSpec((tile, width), lambda t: (t, 0))
        piece = pl.BlockSpec((tile, width), lambda t: (0, 0))
        line = pl.BlockSpec((1, width), lambda t: (0, 0))
        wide = functools.partial(jax.ShapeDtypeStruct, dtype=jnp.float32)
        outs = pl.pallas_call(
            kernel,
            grid=(tiles,),
            in_specs=[block] + [piece] * len(moved) + [block] * len(blocks) + [line],
            out_specs=[block] * keep + [piece] * tiles + [line] * add,
            out_shape=[wide((rows, width))] * keep
            + [jax.ShapeDtypeStruct((tile, width), jnp.bfloat16)] * tiles
            + [wide((1, width))] * add,
            compiler_params=kernel_params(),
            cost_estimate=told(3),
            name=name,
        )(kept, *moved, *blocks, gain.astype(jnp.float32)[None])
        pieces = outs[keep : keep + tiles]
        return (outs[0] if keep else None), pieces, (outs[-1] if add else None)


class HeadGather:
    def __init__(self, own):
        chips = lax.axis_size("head") // 2
        self.steps = [own] + [[chip_move(part, step) for part in own] for step in range(1, chips)]

    def edge(self):
        return tuple(part for parts in self.steps[1:] for part in parts)

    def rows(self, *gates):
        chips = len(self.steps)
        place = lax.axis_index("head")
        chip, core = place // 2, place % 2
        height = self.steps[0][0].shape[0]
        count = len(self.steps[0])
        pieces, places, origins = [], [], []
        for step, parts in enumerate(self.steps):
            at = 2 * ((chip - step + chips) % chips)
            for other in range(2):
                for turn, part in enumerate(parts):
                    if other:
                        part = core_swap(after(part, *gates) if gates and step else part)
                    origins.append((len(places), turn * height))
                    pieces.append(part)
                places.append((at + (1 - core if other else core)) * count * height)
        places = jnp.stack(places).astype(jnp.int32)
        rows = 2 * chips * count * height
        (whole,) = place_rows(pieces, places, origins, rows, [pieces[0].shape[1]])
        return whole


def exchange_sum(block, axis, bits):
    devices = range(lax.axis_size(axis))
    block = block.astype(jnp.bfloat16)
    for bit in bits:
        other = lax.ppermute(block, axis, [(i, i ^ bit) for i in devices])
        block = (block.astype(jnp.float32) + other.astype(jnp.float32)).astype(jnp.bfloat16)
    return block


def bits_of(axis):
    bits, bit = [], 1
    while bit < lax.axis_size(axis):
        bits.append(bit)
        bit *= 2
    return bits


def lane_of(shape):
    return lax.broadcasted_iota(jnp.int32, shape, 1)


def rolled(values, shift):
    return pltpu.roll(values, shift % LANES, 1)


def swapped_halves(values):
    lane = lane_of(values.shape)
    return jnp.where(lane % 64 < 32, rolled(values, -32), rolled(values, 32))


def half_lanes(values, half):
    lane = lane_of(values.shape)
    return jnp.where(lane < 64 if half == 0 else lane >= 64, values, 0.0)


def in_half(values, have, want):
    kept = half_lanes(values, have)
    return kept if have == want else rolled(kept, 64)


def half_sums(values):
    row = lax.broadcasted_iota(jnp.int32, (LANES, LANES), 0)
    ones = jnp.where(row // 64 == lane_of((LANES, LANES)) // 64, 1.0, 0.0).astype(jnp.bfloat16)
    return forward_product(values.astype(jnp.bfloat16), ones)


def half_softmax(values):
    lane = lane_of(values.shape)
    low = lane < 64
    first = jnp.max(jnp.where(low, values, -jnp.inf), axis=1, keepdims=True)
    second = jnp.max(jnp.where(low, -jnp.inf, values), axis=1, keepdims=True)
    powers = jnp.exp(values - jnp.where(low, first, second))
    first = jnp.sum(jnp.where(low, powers, 0.0), axis=1, keepdims=True)
    second = jnp.sum(jnp.where(low, 0.0, powers), axis=1, keepdims=True)
    return powers * jnp.where(low, 1.0 / first, 1.0 / second)


def group(ref_or_value, index):
    return ref_or_value[:, index * LANES : (index + 1) * LANES]


class Sizes:
    def __init__(self, shard, heads, kv_heads):
        self.shard, self.heads, self.kv = shard, heads, kv_heads
        self.each = heads // kv_heads
        self.query_groups = heads // 2
        self.key_groups = (kv_heads + 1) // 2
        self.linear = (heads + 2 * kv_heads) * 64
        self.span = shard + WIN
        self.kv_lanes = 2 * kv_heads * 64
        self.halo_lanes = self.kv_lanes + kv_heads * LANES

    def key_place(self, g):
        return g // 2, g % 2

    def value_place(self, g):
        return (self.kv + g) // 2, (self.kv + g) % 2


def prepare_kernel(sizes, lin_ref, cos_ref, sin_ref, meta_ref, mapq_ref, mapk_ref, rot_ref, phi_ref, halo_ref, whole_ref, first_ref):
    shard = sizes.shard
    wide = []
    for index in range(sizes.linear // LANES):
        part = group(lin_ref, index)
        turned = part * group(cos_ref, index) + swapped_halves(part) * group(sin_ref, index)
        rot_ref[:, index * LANES : (index + 1) * LANES] = turned.astype(jnp.bfloat16)
        wide.append(turned.astype(jnp.bfloat16))
    for index in range(sizes.query_groups):
        both = forward_product(wide[index], mapq_ref[index])
        for half in range(2):
            at = (2 * index + half) * LANES
            phi = half_softmax(group(both, half))
            phi_ref[:, at : at + LANES] = phi.astype(jnp.bfloat16)
    kv_groups = wide[sizes.query_groups :]
    phis = []
    for index in range(sizes.key_groups):
        both = forward_product(kv_groups[index], mapk_ref[index])
        for half in range(min(2, sizes.kv - 2 * index)):
            at = (sizes.heads + 2 * index + half) * LANES
            phi = half_softmax(group(both, half)).astype(jnp.bfloat16)
            phi_ref[:, at : at + LANES] = phi
            phis.append(phi)
    halo_ref[:, : sizes.kv_lanes] = jnp.concatenate(kv_groups, axis=1)[shard - WIN :]
    halo_ref[:, sizes.kv_lanes :] = jnp.concatenate(phis, axis=1)[shard - WIN :]
    keep_whole, keep_first = meta_ref[:, 0:1], meta_ref[:, 1:2]
    for g in range(sizes.kv):
        at, half = sizes.value_place(g)
        values = in_half(kv_groups[at].astype(jnp.float32), half, 0)
        values = jnp.where(lane_of(values.shape) == 64, 1.0, values).astype(jnp.bfloat16)
        phi = phis[g].astype(jnp.float32)
        for keep, ref in ((keep_whole, whole_ref), (keep_first, first_ref)):
            state = left_dot(values, (phi * keep).astype(jnp.bfloat16))
            ref[g] = state[:STATE_ROWS].astype(jnp.bfloat16)


def near_and_far(sizes, meta_ref, keys_ref):
    shape = (sizes.shard, sizes.span)
    row = lax.broadcasted_iota(jnp.int32, shape, 0)
    column = lax.broadcasted_iota(jnp.int32, shape, 1)
    same = meta_ref[:, 2:3] == keys_ref[0:1, :]
    near = same & (column > row) & (column <= row + WIN)
    far = same & (column <= row)
    return near, far


def twice(values):
    return jnp.concatenate([values] * 2, axis=0)


def stacked(parts):
    return jnp.concatenate(parts, axis=0)


def with_halo(sizes, rot_ref, phi_ref, halo_ref, g):
    out = []
    for at, half in (sizes.key_place(g), sizes.value_place(g)):
        own = group(rot_ref, sizes.query_groups + at)
        before = group(halo_ref, at)
        wide = stacked([before, own]).astype(jnp.float32)
        out.append([in_half(wide, half, want) for want in range(2)])
    phi = stacked(
        [
            halo_ref[:, sizes.kv_lanes + g * LANES : sizes.kv_lanes + (g + 1) * LANES],
            group(phi_ref, sizes.heads + g),
        ]
    )
    return out[0], out[1], phi


def value_sides(values, weight):
    ones = jnp.full(values[0].shape, weight, jnp.float32)
    sides = []
    for half in range(2):
        side = jnp.concatenate([values[half], half_lanes(ones, half)], axis=1)
        sides.append(side.astype(jnp.bfloat16))
    return sides


def state_sides(state, weight):
    totals = jnp.broadcast_to(state[64:65].astype(jnp.float32) * weight, (64, LANES))
    totals = totals.astype(jnp.bfloat16)
    none = jnp.zeros_like(totals)
    return [
        stacked([state[:64], none, totals, none]),
        stacked([none, state[:64], none, totals]),
    ]


def pairs_of(sizes, g):
    return range(g * sizes.each // 2, (g + 1) * sizes.each // 2)


def attend_kernel(sizes, rot_ref, phi_ref, halo_ref, state_ref, meta_ref, keys_ref, att_ref, den_ref):
    shard = sizes.shard
    near, far = near_and_far(sizes, meta_ref, keys_ref)
    reach = meta_ref[:, 3:4]
    for g in range(sizes.kv):
        pairs = pairs_of(sizes, g)
        count = len(pairs)
        near_all, far_all = stacked([near] * count), stacked([far] * count)
        keys, values, phi_key = with_halo(sizes, rot_ref, phi_ref, halo_ref, g)
        value_pair = value_sides(values, 1.0)
        state_pair = state_sides(state_ref[g], 1.0)
        queries = stacked([group(rot_ref, p) for p in pairs])
        total = None
        for half in range(2):
            scores = right_dot(queries, keys[half].astype(jnp.bfloat16)) * 0.125
            phi = stacked([group(phi_ref, 2 * p + half) for p in pairs])
            kernel = right_dot(phi, phi_key)
            weights = jnp.where(near_all, jnp.exp(scores), jnp.where(far_all, kernel, 0.0))
            reached = (phi.astype(jnp.float32) * stacked([reach] * count)).astype(jnp.bfloat16)
            term = forward_product(weights.astype(jnp.bfloat16), value_pair[half])
            term = term + right_dot(reached, state_pair[half])
            total = term if total is None else total + term
        mixed = total[:, :LANES] / total[:, LANES:]
        for turn, p in enumerate(pairs):
            rows = slice(turn * shard, (turn + 1) * shard)
            lanes = slice(p * LANES, (p + 1) * LANES)
            att_ref[:, lanes] = mixed[rows].astype(jnp.bfloat16)
            den_ref[:, lanes] = total[rows, LANES:]


def feature_back(phi, grads):
    phi = phi.astype(jnp.float32)
    return (phi * (grads - half_sums(phi * grads))).astype(jnp.bfloat16)


def unrotated(grads, cos, sin):
    return grads * cos - swapped_halves(grads) * sin


def output_grads(sizes, pairs, att_ref, den_ref, grad_ref):
    grads = stacked([group(grad_ref, p) for p in pairs]).astype(jnp.float32)
    mixed = stacked([group(att_ref, p) for p in pairs]).astype(jnp.float32)
    inverse = 1.0 / stacked([group(den_ref, p) for p in pairs])
    grad_num = (grads * inverse).astype(jnp.bfloat16)
    grad_den = -half_sums(grads * mixed) * inverse
    rough = grad_den.astype(jnp.bfloat16)
    rest = (grad_den - rough.astype(jnp.float32)).astype(jnp.bfloat16)
    lane = lane_of(grad_den.shape)
    grad_den = jnp.where(lane % 64 < 32, rough.astype(jnp.float32), rest.astype(jnp.float32))
    return jnp.concatenate([grad_num, grad_den.astype(jnp.bfloat16)], axis=1)


def carry_kernel(sizes, phi_ref, meta_ref, att_ref, den_ref, grad_ref, carry_ref):
    reach = meta_ref[:, 3:4]
    for g in range(sizes.kv):
        pairs = pairs_of(sizes, g)
        reach_all = stacked([reach] * len(pairs))
        both = output_grads(sizes, pairs, att_ref, den_ref, grad_ref)
        state_sum = []
        for half in range(2):
            phi = stacked([group(phi_ref, 2 * p + half) for p in pairs])
            reached = (phi.astype(jnp.float32) * reach_all).astype(jnp.bfloat16)
            state_sum.append(left_dot(both, reached))
        low, high = state_sum
        totals = low[128:129] + low[160:161] + high[192:193] + high[224:225]
        state_grad = stacked(
            [low[:64] + high[64:128], jnp.broadcast_to(totals, (STATE_ROWS - 64, LANES))]
        )
        carry_ref[g] = state_grad.astype(jnp.bfloat16)


def backward_kernel(sizes, rot_ref, phi_ref, halo_ref, state_ref, meta_ref, keys_ref, att_ref, den_ref, grad_ref, cos_ref, sin_ref, mapq_ref, lin_ref, own_ref, back_ref, map_ref):
    shard = sizes.shard
    near, far = near_and_far(sizes, meta_ref, keys_ref)
    reach = meta_ref[:, 3:4]

    @pl.when(pl.program_id(0) == 0)
    def _():
        map_ref[...] = jnp.zeros_like(map_ref)

    kv_grads = [jnp.zeros((sizes.span, LANES), jnp.float32) for _ in range(sizes.kv_lanes // LANES)]
    for g in range(sizes.kv):
        pairs = pairs_of(sizes, g)
        count = len(pairs)
        near_all, far_all = stacked([near] * count), stacked([far] * count)
        reach_all = stacked([reach] * count)
        keys, values, phi_key = with_halo(sizes, rot_ref, phi_ref, halo_ref, g)
        value_pair = value_sides(values, 1.0 / 32.0)
        state_pair = state_sides(state_ref[g], 1.0 / 32.0)
        queries = stacked([group(rot_ref, p) for p in pairs])
        both = output_grads(sizes, pairs, att_ref, den_ref, grad_ref)
        grad_num = both[:, :LANES]
        grad_query = None
        key_sum, value_sum, phi_sum = [], [], None
        back = [[None, None] for _ in pairs]
        for half in range(2):
            key_half = keys[half].astype(jnp.bfloat16)
            scores = right_dot(queries, key_half) * 0.125
            phi = stacked([group(phi_ref, 2 * p + half) for p in pairs])
            kernel = right_dot(phi, phi_key)
            powers = jnp.exp(scores)
            weights = jnp.where(near_all, powers, jnp.where(far_all, kernel, 0.0))
            weights = weights.astype(jnp.bfloat16)
            grad_weights = right_dot(both, value_pair[half])
            grad_scores = jnp.where(near_all, grad_weights * powers, 0.0).astype(jnp.bfloat16)
            grad_kernel = jnp.where(far_all, grad_weights, 0.0).astype(jnp.bfloat16)
            term = forward_product(grad_scores, key_half)
            grad_query = term if grad_query is None else grad_query + term
            key_sum.append(left_dot(grad_scores, queries))
            value_sum.append(left_dot(weights, grad_num))
            term = left_dot(grad_kernel, phi)
            phi_sum = term if phi_sum is None else phi_sum + term
            grad_phi = forward_product(grad_kernel, phi_key)
            grad_phi = grad_phi + forward_product(both, state_pair[half]) * reach_all
            projected = feature_back(phi, grad_phi)
            for turn in range(count):
                back[turn][half] = projected[turn * shard : (turn + 1) * shard]
        for turn, p in enumerate(pairs):
            pair = jnp.concatenate(back[turn], axis=1)
            grad = grad_query[turn * shard : (turn + 1) * shard] * 0.125
            grad = grad + right_dot(pair, mapq_ref[p])
            grad = unrotated(grad, group(cos_ref, p), group(sin_ref, p))
            lin_ref[:, p * LANES : (p + 1) * LANES] = grad.astype(jnp.bfloat16)
            map_ref[p] += left_dot(group(rot_ref, p), pair)
        for (at, half), sums, scale in (
            (sizes.key_place(g), key_sum, 0.125),
            (sizes.value_place(g), value_sum, 1.0),
        ):
            total = in_half(sums[0], 0, half) + in_half(sums[1], 1, half)
            kv_grads[at] = kv_grads[at] + total * scale
        at = sizes.kv_lanes + g * LANES
        own_ref[:, at : at + LANES] = phi_sum[WIN:]
        back_ref[:, at : at + LANES] = phi_sum[:WIN].astype(jnp.bfloat16)
    for at, grads in enumerate(kv_grads):
        lanes = slice(at * LANES, (at + 1) * LANES)
        own_ref[:, lanes] = grads[WIN:]
        back_ref[:, lanes] = grads[:WIN].astype(jnp.bfloat16)


def key_kernel(sizes, rot_ref, phi_ref, meta_ref, own_ref, back_ref, whole_ref, first_ref, cos_ref, sin_ref, mapk_ref, lin_ref, map_ref):
    shard = sizes.shard

    @pl.when(pl.program_id(0) == 0)
    def _():
        map_ref[...] = jnp.zeros_like(map_ref)

    total = own_ref[...]
    returned = back_ref[...].astype(jnp.float32)
    if shard > WIN:
        total = stacked([total[: shard - WIN], total[shard - WIN :] + returned])
    else:
        total = total + returned
    kv_groups = sizes.kv_lanes // LANES
    kv_grads = [group(total, at) for at in range(kv_groups)]
    back = []
    for g in range(sizes.kv):
        at, half = sizes.value_place(g)
        values = in_half(group(rot_ref, sizes.query_groups + at).astype(jnp.float32), half, 0)
        values = jnp.where(lane_of(values.shape) == 64, 1.0, values).astype(jnp.bfloat16)
        phi = group(phi_ref, sizes.heads + g)
        grad_phi = total[:, sizes.kv_lanes + g * LANES : sizes.kv_lanes + (g + 1) * LANES]
        grad_value = None
        for column, ref in ((0, whole_ref), (1, first_ref)):
            keep = meta_ref[:, column : column + 1]
            state = stacked([ref[g], jnp.zeros((LANES - STATE_ROWS, LANES), jnp.bfloat16)])
            grad_phi = grad_phi + forward_product(values, state) * keep
            term = right_dot(phi, state) * keep
            grad_value = term if grad_value is None else grad_value + term
        kv_grads[at] = kv_grads[at] + in_half(grad_value, 0, half)
        back.append(feature_back(phi, grad_phi))
    if len(back) % 2:
        back.append(jnp.zeros_like(back[0]))
    for index in range(sizes.key_groups):
        pair = jnp.concatenate(back[2 * index : 2 * index + 2], axis=1)
        kv_grads[index] = kv_grads[index] + right_dot(pair, mapk_ref[index])
        map_ref[index] += left_dot(group(rot_ref, sizes.query_groups + index), pair)
    for at in range(kv_groups):
        cos = group(cos_ref, sizes.query_groups + at)
        sin = group(sin_ref, sizes.query_groups + at)
        lanes = slice(at * LANES, (at + 1) * LANES)
        lin_ref[:, lanes] = unrotated(kv_grads[at], cos, sin).astype(jnp.bfloat16)


def by_row(kernel, name, rows, inputs, outputs, microseconds):
    def spec(shape, kind):
        rest = tuple(shape[1:])
        none = (0,) * len(rest)
        if kind == "all":
            return pl.BlockSpec(shape, lambda r: (0,) + none)
        first = shape[0] // rows if kind == "flat" else None
        return pl.BlockSpec((first,) + rest, lambda r: (r,) + none)

    return pl.pallas_call(
        kernel,
        grid=(rows,),
        in_specs=[spec(a.shape, kind) for a, kind in inputs],
        out_specs=[spec(shape.shape, kind) for shape, kind in outputs],
        out_shape=[shape for shape, _ in outputs],
        compiler_params=pltpu.CompilerParams(vmem_limit_bytes=48 * 1024 * 1024),
        cost_estimate=told(microseconds),
        name=name,
    )(*[a for a, _ in inputs])


def map_pairs(maps):
    count = maps.shape[0]
    wide = jnp.concatenate([maps, -maps], axis=2)
    if count % 2:
        wide = jnp.concatenate([wide, jnp.zeros_like(wide[:1])], axis=0)
    wide = wide.reshape(-1, 2, 64, LANES)
    none = jnp.zeros_like(wide[:, 0])
    return jnp.concatenate(
        [
            jnp.concatenate([wide[:, 0], none], axis=2),
            jnp.concatenate([none, wide[:, 1]], axis=2),
        ],
        axis=1,
    )


def maps_from_pairs(pairs, count):
    first = pairs[:, :64, :64] - pairs[:, :64, 64:128]
    second = pairs[:, 64:, 128:192] - pairs[:, 64:, 192:]
    return jnp.stack([first, second], axis=1).reshape(-1, 64, 64)[:count]


def rope_tables(positions, sizes):
    inverse = rope_base ** (-jnp.arange(0, 64, 2, dtype=jnp.float32) / 64)
    angle = positions.astype(jnp.float32)[:, None] * inverse[None, :]
    cosine, sine = jnp.cos(angle), jnp.sin(angle)
    turning = sizes.heads + sizes.kv
    cosine = jnp.tile(jnp.concatenate([cosine, cosine], axis=1), (1, turning))
    sine = jnp.tile(jnp.concatenate([-sine, sine], axis=1), (1, turning))
    rest = (positions.shape[0], sizes.kv * 64)
    return (
        jnp.concatenate([cosine, jnp.ones(rest, jnp.float32)], axis=1),
        jnp.concatenate([sine, jnp.zeros(rest, jnp.float32)], axis=1),
    )


def fixed(shape):
    return pl.BlockSpec(shape, lambda t: (0,) * len(shape), pipeline_mode=pl.Buffered(1))


def mlp_forward(rows, cotangent, weights, microseconds):
    count, width = rows.shape
    chunk = weights.shape[1] // 3
    tile = min(256, chunk)
    tiles = chunk // tile
    part = min(512, count)

    def kernel(x_ref, c_ref, gate_ref, up_ref, down_ref, grad_gate_ref, grad_up_ref, inner_ref):
        def one(turn, nothing):
            at = pl.ds(pl.multiple_of(turn * part, part), part)
            x = x_ref[at, :]
            gate = forward_product(x, gate_ref[...])
            up = forward_product(x, up_ref[...])
            grad_inner = forward_product(c_ref[at, :], down_ref[...])
            sigmoid = 1.0 / (1.0 + jnp.exp(-gate))
            swish = gate * sigmoid
            grad_gate = grad_inner * up * (sigmoid * (1.0 + gate * (1.0 - sigmoid)))
            grad_gate_ref[at, :] = grad_gate.astype(jnp.bfloat16)
            grad_up_ref[at, :] = (grad_inner * swish).astype(jnp.bfloat16)
            inner_ref[at, :] = (swish * up).astype(jnp.bfloat16)
            return nothing

        lax.fori_loop(0, count // part, one, 0)

    def columns(shift):
        return pl.BlockSpec((width, tile), lambda t: (0, t + shift))

    out = pl.BlockSpec((count, tile), lambda t: (0, t))
    shape = jax.ShapeDtypeStruct((count, chunk), jnp.bfloat16)
    return pl.pallas_call(
        kernel,
        grid=(tiles,),
        in_specs=[fixed(rows.shape), fixed(cotangent.shape)]
        + [columns(shift * tiles) for shift in range(3)],
        out_specs=[out] * 3,
        out_shape=[shape] * 3,
        compiler_params=kernel_params(),
        cost_estimate=told(microseconds),
        name="hidden_units",
    )(rows, cotangent, weights, weights, weights)


def turned_product(terms, before, dtype, microseconds, split=False, weigh=None):
    count, width = terms[0][0].shape[0], terms[0][1].shape[0]
    tile = min(512, width)
    tiles = width // tile
    chips = lax.axis_size("head") // 2
    rows = count // (2 * chips)
    core = (lax.axis_index("head") % 2).astype(jnp.int32)
    extra = [] if before is None else [before]
    extra += [] if weigh is None else [weigh[0], weigh[1].astype(jnp.float32)[None]]

    def kernel(core_ref, *refs):
        total = None if before is None else refs[2 * len(terms)][...]
        for left_ref, weight_ref in zip(refs, refs[len(terms) : 2 * len(terms)], strict=False):
            term = right_dot(left_ref[...], weight_ref[...])
            total = term if total is None else total + term
        if weigh is not None:
            rows_ref, factors_ref = refs[2 * len(terms) + len(extra) - 2 :][:2]
            column = jnp.sum(total * rows_ref[...].astype(jnp.float32), axis=0, keepdims=True)
            refs[-2][...] = column * factors_ref[...]
            refs = refs[:-2] + refs[-1:]
        if not split:
            refs[-1][...] = total.astype(dtype)
            return
        mine_ref, *their_refs, held_ref = refs[-2 - tiles :]
        held_ref[...] = total.astype(dtype)

        def take(out_ref, which):
            for chip in range(chips):
                at = pl.multiple_of((2 * chip + which) * rows, rows)
                out_ref[chip] = held_ref[pl.ds(at, rows), :]

        take(mine_ref, core_ref[0])
        for turn, their_ref in enumerate(their_refs):
            pl.when(pl.program_id(0) == turn)(
                functools.partial(take, their_ref, 1 - core_ref[0])
            )

    def rows_of(section, chunk):
        return pl.BlockSpec((tile, chunk), lambda t, at: (t, section))

    def whole(shape):
        return pl.BlockSpec(shape, lambda t, at: (0, 0), pipeline_mode=pl.Buffered(1))

    out = pl.BlockSpec((count, tile), lambda t, at: (0, t))
    part = pl.BlockSpec((chips, rows, tile), lambda t, at: (0, 0, t))
    piece = pl.BlockSpec((chips, rows, tile), lambda t, at: (0, 0, 0))
    line = pl.BlockSpec((1, tile), lambda t, at: (0, t))
    added = [] if before is None else [out]
    added += [] if weigh is None else [out, line]
    lefts = [left for left, _, _ in terms]
    result = pl.pallas_call(
        kernel,
        grid_spec=pltpu.PrefetchScalarGridSpec(
            num_scalar_prefetch=1,
            grid=(tiles,),
            in_specs=[whole(left.shape) for left in lefts]
            + [rows_of(section, left.shape[1]) for left, _, section in terms]
            + added,
            out_specs=([part] + [piece] * tiles if split else [out])
            + ([] if weigh is None else [line]),
            scratch_shapes=[pltpu.VMEM((count, tile), dtype)] if split else [],
        ),
        out_shape=(
            [jax.ShapeDtypeStruct((chips, rows, width), dtype)]
            + [jax.ShapeDtypeStruct((chips, rows, tile), dtype)] * tiles
            if split
            else [jax.ShapeDtypeStruct((count, width), dtype)]
        )
        + ([] if weigh is None else [jax.ShapeDtypeStruct((1, width), jnp.float32)]),
        compiler_params=kernel_params(),
        cost_estimate=told(microseconds),
        name="turned_product",
    )(core[None], *lefts, *[weights for _, weights, _ in terms], *extra)
    return result if split else result[0]


def weight_gradients(sides, microseconds):
    count, width = sides[0][0].shape
    tile = min(512, width)
    lefts, which = [], []
    for left, _ in sides:
        at = next((i for i, other in enumerate(lefts) if other is left), len(lefts))
        if at == len(lefts):
            lefts.append(left)
        which.append(at)
    widths = [right.shape[1] for _, right in sides]
    starts = [sum(widths[:i]) for i in range(len(widths))]

    def kernel(*refs):
        for at, right_ref, start, size in zip(
            which, refs[len(lefts) : -1], starts, widths, strict=True
        ):
            total = left_dot(refs[at][...], right_ref[...])
            refs[-1][:, start : start + size] = total.astype(jnp.bfloat16)

    column = pl.BlockSpec((count, tile), lambda t: (0, t))
    return pl.pallas_call(
        kernel,
        grid=(width // tile,),
        in_specs=[column] * len(lefts) + [fixed(right.shape) for _, right in sides],
        out_specs=pl.BlockSpec((tile, sum(widths)), lambda t: (t, 0)),
        out_shape=jax.ShapeDtypeStruct((width, sum(widths)), jnp.bfloat16),
        compiler_params=kernel_params(),
        cost_estimate=told(microseconds),
        name="weight_gradients",
    )(*lefts, *[right for _, right in sides])


def attended_back(grads, weights, lowrank_up, lowrank_down, microseconds):
    count, width = grads.shape
    heads, rank = lowrank_down.shape
    part = min(256, count)

    def kernel(x_ref, w_ref, up_ref, down_ref, out_ref, low_ref):
        low = (adapter_scale * right_dot(x_ref[...], up_ref[...])).astype(jnp.bfloat16)
        total = forward_product(x_ref[...], w_ref[...]) + right_dot(low, down_ref[...])
        out_ref[...] = total.astype(jnp.bfloat16)
        low_ref[...] = low

    def rows(size):
        return pl.BlockSpec((part, size), lambda t: (t, 0))

    return pl.pallas_call(
        kernel,
        grid=(count // part,),
        in_specs=[rows(width), fixed(weights.shape), fixed(lowrank_up.shape), fixed(lowrank_down.shape)],
        out_specs=[rows(heads), rows(rank)],
        out_shape=[
            jax.ShapeDtypeStruct((count, heads), jnp.bfloat16),
            jax.ShapeDtypeStruct((count, rank), jnp.bfloat16),
        ],
        compiler_params=kernel_params(),
        cost_estimate=told(microseconds),
        name="attended_back",
    )(grads, weights, lowrank_up, lowrank_down)


def document_facts(document_index, shard):
    seq_index = lax.axis_index("seq")
    count = lax.axis_size("seq")
    rows = document_index.shape[0]
    documents = document_index.astype(jnp.float32)
    missing = jnp.full((rows, 1), -1.0, jnp.float32)

    def last_of(block):
        at = jnp.clip(block * shard + shard - 1, 0, count * shard - 1)
        found = lax.dynamic_slice_in_dim(documents, at, 1, 1)
        return jnp.where((block >= 0) & (block < count), found, missing)

    def carried_of(block):
        at = jnp.clip(block * shard - WIN - 1, 0, count * shard - 1)
        found = lax.dynamic_slice_in_dim(documents, at, 1, 1)
        return jnp.where((block >= 1) & (block < count), found, missing - 1.0)

    padded = jnp.concatenate([jnp.broadcast_to(missing, (rows, WIN)), documents], axis=1)
    key_documents = lax.dynamic_slice_in_dim(padded, seq_index * shard, shard + WIN, 1)
    own = key_documents[:, WIN:]
    position = jnp.arange(shard)[None, :]
    keep_whole = own == own[:, shard - 1 :]
    keep_first = (position < shard - WIN) & (own == own[:, shard - WIN - 1 : shard - WIN])
    reach = own == carried_of(seq_index)
    columns = [keep_whole, keep_first, own, reach]
    meta = jnp.stack([column.astype(jnp.float32) for column in columns], axis=-1)
    meta = jnp.concatenate([meta, jnp.zeros_like(meta)], axis=-1)
    return meta, key_documents[:, None, :], last_of, carried_of


def masked(block, mask):
    return block.astype(jnp.float32) * mask.astype(jnp.float32).reshape(-1, 1, 1, 1)


class Carries:
    def __init__(self, last_of, carried_of, rows):
        self.index = lax.axis_index("seq")
        self.count = lax.axis_size("seq")
        self.even = self.index % 2 == 0
        self.rows = rows // 2
        self.pair = self.index - self.index % 2
        self.last_of, self.carried_of = last_of, carried_of
        self.steps = []
        distance = 1
        while distance < self.count // 2:
            self.steps.append(distance)
            distance *= 2

    def half(self, values, own):
        at = jnp.where(self.even == own, 0, self.rows)
        return lax.dynamic_slice_in_dim(values, at, self.rows, 0)

    def end(self, back):
        return self.half(self.last_of(self.pair - back), True)

    def other(self, values):
        values = values.astype(jnp.bfloat16)
        return lax.ppermute(values, "seq", [(i, i ^ 1) for i in range(self.count)])

    def pick(self, first, second):
        return jnp.where(self.even, first.astype(jnp.float32), second.astype(jnp.float32))

    def split(self, values):
        mine, theirs = self.half(values, True), self.other(self.half(values, False))
        return self.pick(mine, theirs), self.pick(theirs, mine)

    def join(self, even, odd):
        kept, got = self.pick(even, odd), self.other(self.pick(odd, even))
        return jnp.concatenate([self.pick(kept, got), self.pick(got, kept)], axis=0)

    def reach(self):
        even = self.half(self.carried_of(self.pair), True) == self.end(2)
        odd = self.half(self.carried_of(self.pair + 1), True) == self.end(1)
        return even, odd

    def forward(self, whole, first, tail):
        before, halo = shifted(first, 1), shifted(tail, 1)
        even, odd = self.split(whole)
        window = odd + masked(even, self.end(0) == self.end(-1))
        sums = None
        for distance in self.steps:
            if sums is None:
                got = shifted(jnp.stack([window, even]).astype(jnp.bfloat16), 2)
                got = got.astype(jnp.float32)
                sums = got[1], got[0]
                got = got[0]
            else:
                got = shifted(window.astype(jnp.bfloat16), 2 * distance)
                there = self.end(2 * distance - 1)
                sums = (
                    sums[0] + masked(got, there == self.end(2)),
                    sums[1] + masked(got, there == self.end(1)),
                )
            window = window + masked(got, self.end(2 * distance - 1) == self.end(-1))
        reach = self.reach()
        sums = after(sums, before, halo)
        total = self.join(masked(sums[0], reach[0]), masked(sums[1], reach[1]))
        return (total + before.astype(jnp.float32)).astype(jnp.bfloat16), halo

    def backward(self, grads, back, other):
        first, returned = shifted(grads, -1), shifted(back, -1)
        even, odd = self.split(grads)
        reach = self.reach()
        even, odd = masked(even, reach[0]), masked(odd, reach[1])
        even, odd = after((even, odd), other)
        window = None
        for distance in reversed(self.steps):
            there = self.end(2 * distance - 1)
            linked = 0.0 if window is None else masked(window, there == self.end(-1))
            if distance == 1:
                sent = jnp.stack([linked + odd, even]).astype(jnp.bfloat16)
                got = shifted(sent, -2).astype(jnp.float32)
                window = got[0] if window is None else window + got[0]
                direct = got[1]
            else:
                sent = linked + masked(odd, there == self.end(1))
                sent = sent + masked(even, there == self.end(2))
                got = shifted(sent.astype(jnp.bfloat16), -2 * distance).astype(jnp.float32)
                window = got if window is None else window + got
        even = masked(window, self.end(0) == self.end(-1)) + direct
        even, window = after((even, window), first, returned)
        return self.join(even, window).astype(jnp.bfloat16), first, returned


def body(
    tokens,
    cotangent,
    first_norm_gain,
    second_norm_gain,
    query_weight,
    key_weight,
    value_weight,
    output_weight,
    gate_weight,
    up_weight,
    down_weight,
    adapter_down_weight,
    adapter_query_weight,
    adapter_key_weight,
    adapter_value_weight,
    adapter_output_down,
    adapter_output_up,
    hedgehog_query_weight,
    hedgehog_key_weight,
    document_index,
):
    row_count, shard, width = tokens.shape
    seq_index = lax.axis_index("seq")
    heads_here = hedgehog_query_weight.shape[0]
    kv_here = hedgehog_key_weight.shape[0]
    sizes = Sizes(shard, heads_here, kv_here)
    rank = adapter_query_weight.shape[0]
    tokens_here = row_count * shard
    block_rows = query_weight.shape[0]
    hidden_units = gate_weight.shape[1]
    chunk = hidden_units // 2
    query_width, key_width = query_weight.shape[1], key_weight.shape[1]
    key_end = query_width + key_width

    out_width = output_weight.shape[0]
    first_gather = Gather(
        jnp.concatenate([query_weight, key_weight, value_weight, output_weight.T], axis=1)
    )
    first_gather.advance(quarters=4)
    down_turned = down_weight.T
    early, late = [
        Gather(
            jnp.concatenate(
                [gate_weight[:, span], up_weight[:, span], down_turned[:, span]], axis=1
            )
        )
        for span in (slice(0, chunk), slice(chunk, hidden_units))
    ]
    early.advance(*first_gather.edge())
    complete_qkv, out_turned = first_gather.assemble(sizes.linear, out_width)

    adapters = jnp.zeros((3 * rank, sizes.linear), jnp.bfloat16)
    adapters = lax.dynamic_update_slice(adapters, adapter_query_weight, (0, 0))
    adapters = lax.dynamic_update_slice(adapters, adapter_key_weight, (rank, query_width))
    adapters = lax.dynamic_update_slice(adapters, adapter_value_weight, (2 * rank, key_end))
    positions = seq_index * shard + jnp.arange(shard)
    cosine, sine = rope_tables(positions, sizes)
    map_query, map_key = map_pairs(hedgehog_query_weight), map_pairs(hedgehog_key_weight)
    meta, key_documents, last_of, carried_of = document_facts(document_index, shard)

    flattened = tokens.reshape(tokens_here, width).astype(jnp.float32)
    scale_one = lax.rsqrt(jnp.mean(flattened * flattened, axis=-1, keepdims=True) + epsilon)
    normalized_input = flattened * scale_one * first_norm_gain.astype(jnp.float32)
    normalized_input = normalized_input.astype(jnp.bfloat16)
    lowrank_input = forward_product(normalized_input, adapter_down_weight).astype(jnp.bfloat16)
    linear = forward_product(normalized_input, complete_qkv) + adapter_scale * forward_product(
        lowrank_input, adapters
    )
    low = functools.partial(jax.ShapeDtypeStruct, dtype=jnp.bfloat16)
    wide = functools.partial(jax.ShapeDtypeStruct, dtype=jnp.float32)
    phi_lanes = (heads_here + kv_here) * LANES
    states = low((row_count, kv_here, STATE_ROWS, LANES))
    rotated, phi, tail, whole, first = by_row(
        functools.partial(prepare_kernel, sizes),
        "prepare",
        row_count,
        [
            (linear, "flat"),
            (cosine, "all"),
            (sine, "all"),
            (meta, "row"),
            (map_query, "all"),
            (map_key, "all"),
        ],
        [
            (low((tokens_here, sizes.linear)), "flat"),
            (low((tokens_here, phi_lanes)), "flat"),
            (low((row_count, WIN, sizes.halo_lanes)), "row"),
            (states, "row"),
            (states, "row"),
        ],
        16,
    )
    early.advance(rotated)
    tail, whole, first = after((tail, whole, first), *early.edge())
    carries = Carries(last_of, carried_of, row_count)
    carry, halo = carries.forward(whole, first, tail)
    early.advance(carry, halo)
    attended, denominator = by_row(
        functools.partial(attend_kernel, sizes),
        "attend",
        row_count,
        [
            (rotated, "flat"),
            (phi, "flat"),
            (halo, "row"),
            (carry, "row"),
            (meta, "row"),
            (key_documents, "row"),
        ],
        [
            (low((tokens_here, query_width)), "flat"),
            (wide((tokens_here, query_width)), "flat"),
        ],
        8,
    )

    lowrank_output = forward_product(attended, adapter_output_down).astype(jnp.bfloat16)
    out_sum = HeadSum(
        *turned_product(
            [(attended, out_turned, 0), (lowrank_output, (adapter_scale * adapter_output_up.T).astype(jnp.bfloat16), 0)],
            None,
            jnp.bfloat16,
            5,
            split=True,
        )
    )
    out_sent = out_sum.pair()
    own_rows = row_count // lax.axis_size("head")
    first_row = lax.axis_index("head") * own_rows
    own_tokens = lax.dynamic_slice_in_dim(tokens, first_row, own_rows, 0)
    own_tokens = own_tokens.reshape(own_rows * shard, width)
    own_cotangent = lax.dynamic_slice_in_dim(cotangent, first_row, own_rows, 0)
    own_cotangent = own_cotangent.reshape(own_rows * shard, width)

    def normed_forward(total, own, gain):
        hidden = own + total
        scale = lax.rsqrt(jnp.mean(hidden * hidden, axis=1, keepdims=True) + epsilon)
        return hidden, hidden * scale * gain, None

    def normed_backward(total, own, values, gain):
        scale = lax.rsqrt(jnp.mean(values * values, axis=1, keepdims=True) + epsilon)
        unit = values * scale
        inner = total * gain
        inner = inner - unit * jnp.mean(inner * unit, axis=1, keepdims=True)
        grad = own + scale * inner
        return grad, grad, total * unit

    out_sum.kept = after(out_sum.kept, *early.edge())
    early.advance(*out_sent)
    hidden_state, own_normed, _ = out_sum.finish(
        normed_forward, [own_tokens], second_norm_gain, True, False, "second_norm"
    )
    normed_gather = HeadGather(own_normed)
    late.advance(*early.edge(), *own_normed)
    normed_rows = normed_gather.rows()
    late_edge = late.edge()
    late.advance(normed_rows)

    grad_out = cotangent.reshape(tokens_here, width)
    (weights_early,) = early.assemble(3 * chunk)
    gate_early, up_early, inner_early = mlp_forward(
        normed_rows, after(grad_out, *late_edge), weights_early, 22
    )
    gate_early = after(gate_early, *late.edge())
    late.advance(up_early)
    part_early = turned_product(
        [(gate_early, weights_early, 0), (up_early, weights_early, 1)], None, jnp.float32, 14
    )
    grads_early = weight_gradients(
        [
            (normed_rows, gate_early),
            (normed_rows, up_early),
            (grad_out, after(inner_early, part_early)),
        ],
        19,
    )
    late.advance(grads_early)
    scatter_early = Scatter(grads_early, block_rows)
    scatter_early.advance(*late.edge())
    (weights_late,) = late.assemble(3 * chunk)
    gate_late, up_late, inner_late = mlp_forward(normed_rows, grad_out, weights_late, 22)
    gate_late = after(gate_late, *scatter_early.edge())
    scatter_early.advance(up_late)
    normed_two_sum = HeadSum(
        *turned_product(
            [(gate_late, weights_late, 0), (up_late, weights_late, 1)],
            part_early,
            jnp.bfloat16,
            15,
            split=True,
        )
    )
    normed_two_sent = normed_two_sum.pair()
    inner_late = after(inner_late, *normed_two_sent, *scatter_early.edge())
    scatter_early.advance(*normed_two_sent)
    grads_late = weight_gradients(
        [(normed_rows, gate_late), (normed_rows, up_late), (grad_out, inner_late)], 19
    )
    normed_two_sum.kept = after(normed_two_sum.kept, grads_late)
    grad_hidden, branch_pieces, grad_gain_two = normed_two_sum.finish(
        normed_backward,
        [own_cotangent, hidden_state],
        second_norm_gain,
        True,
        True,
        "second_norm_back",
    )
    branch_gather = HeadGather(branch_pieces)
    scatter_early.advance(grad_hidden)
    down_sum = HeadSum(
        *turned_product(
            [(inner_early, weights_early, 2), (after(inner_late, grad_hidden, *scatter_early.sending), weights_late, 2)],
            None,
            jnp.bfloat16,
            1500,
            split=True,
        )
    )
    grad_branch = branch_gather.rows(down_sum.mine)
    scatter_late = Scatter(grads_late, block_rows)
    scatter_late.advance(grad_branch)
    down_sum.mine = after(down_sum.mine, grad_branch)
    down_sum.pair()
    grad_attended, grad_lowrank_out = attended_back(
        grad_branch, out_turned, adapter_output_up, adapter_output_down, 4
    )
    grad_attended = after(grad_attended, *scatter_early.edge(), *down_sum.sent)
    (carry_grads,) = by_row(
        functools.partial(carry_kernel, sizes),
        "carry_back",
        row_count,
        [
            (phi, "flat"),
            (meta, "row"),
            (attended, "flat"),
            (denominator, "flat"),
            (grad_attended, "flat"),
        ],
        [(states, "row")],
        5,
    )
    scatter_late.up, scatter_late.down = after(scatter_late.edge(), carry_grads)
    scatter_late.advance()
    grad_attended = after(grad_attended, *scatter_late.sending)

    own_lanes = sizes.halo_lanes
    grad_query_lin, own_grads, back, map_query_pairs = by_row(
        functools.partial(backward_kernel, sizes),
        "backward",
        row_count,
        [
            (rotated, "flat"),
            (phi, "flat"),
            (halo, "row"),
            (carry, "row"),
            (meta, "row"),
            (key_documents, "row"),
            (attended, "flat"),
            (denominator, "flat"),
            (grad_attended, "flat"),
            (cosine, "all"),
            (sine, "all"),
            (map_query, "all"),
        ],
        [
            (low((tokens_here, query_width)), "flat"),
            (wide((tokens_here, own_lanes)), "flat"),
            (low((row_count, WIN, own_lanes)), "row"),
            (wide(map_query.shape), "all"),
        ],
        2000,
    )
    grad_whole, grad_first, returned = carries.backward(
        carry_grads, back, (grad_query_lin, *scatter_late.edge())
    )
    out_up_gradient = adapter_scale * left_dot(lowrank_output, grad_branch)
    late_edge = scatter_late.edge()
    scatter_late.advance(grad_whole)
    grad_whole = after(grad_whole, *late_edge)
    down_sum.kept = after(down_sum.kept, grad_whole)
    _, layer_pieces, _ = down_sum.finish(
        lambda total, values, gain: (None, values + total, None),
        [hidden_state],
        second_norm_gain,
        False,
        False,
        "layer_rows",
        *branch_gather.edge(),
    )
    layer_gather = HeadGather(layer_pieces)
    layer_rows = layer_gather.rows()
    out_down_gradient = left_dot(grad_lowrank_out, attended)
    fill = scatter_early.total([chunk] * 3, [False, False, True])
    grad_whole = after(grad_whole, out_down_gradient, out_up_gradient, *fill, *layer_pieces)
    mlp_sums = [fill]
    grad_key_lin, map_key_pairs = by_row(
        functools.partial(key_kernel, sizes),
        "keys",
        row_count,
        [
            (rotated, "flat"),
            (phi, "flat"),
            (meta, "row"),
            (own_grads, "flat"),
            (returned, "row"),
            (grad_whole, "row"),
            (grad_first, "row"),
            (cosine, "all"),
            (sine, "all"),
            (map_key, "all"),
        ],
        [
            (low((tokens_here, sizes.kv_lanes)), "flat"),
            (wide(map_key.shape), "all"),
        ],
        7,
    )
    grad_linear = jnp.concatenate([grad_query_lin, grad_key_lin], axis=1)
    lowrank_gradient = (adapter_scale * right_dot(grad_linear, adapters)).astype(jnp.bfloat16)
    kv_section = query_width // sizes.kv_lanes
    normed_sum = HeadSum(
        *turned_product(
            [
                (grad_query_lin, complete_qkv, 0),
                (grad_key_lin, complete_qkv, kv_section),
                (lowrank_gradient, adapter_down_weight, 0),
            ],
            None,
            jnp.bfloat16,
            7,
            split=True,
        )
    )
    normed_sent = normed_sum.pair()
    late_edge = scatter_late.edge()
    scatter_late.advance(*normed_sent)
    last_grads = weight_gradients(
        [
            (normalized_input, grad_query_lin),
            (normalized_input, grad_key_lin),
            (grad_branch, after(attended, *normed_sent, *scatter_late.sending)),
        ],
        10,
    )
    adapter_gradient = adapter_scale * left_dot(lowrank_input, grad_linear)
    down_gradient = left_dot(lowrank_gradient, normalized_input)
    last_scatter = Scatter(last_grads, block_rows)
    last_scatter.advance(*scatter_late.sending)
    normed_sum.kept = after(normed_sum.kept, last_grads, *scatter_late.sending, layer_rows)
    _, tokens_pieces, grad_gain_one = normed_sum.finish(
        normed_backward,
        [grad_hidden, own_tokens],
        first_norm_gain,
        False,
        True,
        "first_norm_back",
    )
    tokens_gather = HeadGather(tokens_pieces)
    grad_tokens_rows = tokens_gather.rows().astype(jnp.float32)
    last_sums = last_scatter.total(
        [query_width, key_width, key_width, out_width], [False, False, False, True]
    )
    mlp_sums.append(scatter_late.total([chunk] * 3, [False, False, True]))

    everywhere = jnp.concatenate(
        [down_gradient, out_up_gradient, grad_gain_one, grad_gain_two], axis=0
    )
    adapter_part = jnp.concatenate(
        [
            adapter_gradient[:rank, :query_width],
            adapter_gradient[rank : 2 * rank, query_width:key_end],
            adapter_gradient[2 * rank :, key_end:],
            out_down_gradient,
        ],
        axis=1,
    )
    maps_part = jnp.concatenate(
        [maps_from_pairs(map_query_pairs, heads_here), maps_from_pairs(map_key_pairs, kv_here)]
    )
    maps_part = jnp.pad(maps_part.reshape(-1, 64), ((0, 0), (0, LANES - 64)))
    small = jnp.concatenate(
        [everywhere.reshape(-1, LANES), adapter_part.reshape(-1, LANES), maps_part], axis=0
    )
    small = after(small.astype(jnp.bfloat16), *scatter_late.edge())
    small = exchange_sum(small, "seq", bits_of("seq"))
    first, second = everywhere.size // LANES, (everywhere.size + adapter_part.size) // LANES
    everywhere = exchange_sum(small[:first], "head", bits_of("head")).astype(jnp.float32)
    everywhere = everywhere.reshape(-1, width)
    small = small.astype(jnp.float32)
    adapter_sum = small[first:second].reshape(adapter_part.shape)
    maps_sum = small[second:, :64].reshape(-1, 64, 64)
    end = 3 * rank + rank

    return (
        layer_rows.reshape(row_count, shard, width),
        grad_tokens_rows.reshape(row_count, shard, width),
        everywhere[end],
        everywhere[end + 1],
        *last_sums,
        jnp.concatenate([part[0] for part in mlp_sums], axis=1),
        jnp.concatenate([part[1] for part in mlp_sums], axis=1),
        jnp.concatenate([part[2] for part in mlp_sums], axis=0),
        everywhere[: 3 * rank].T,
        adapter_sum[:, :query_width],
        adapter_sum[:, query_width:key_end],
        adapter_sum[:, key_end : sizes.linear],
        adapter_sum[:, sizes.linear :].T,
        everywhere[3 * rank : end],
        maps_sum[:heads_here],
        maps_sum[heads_here:],
    )


def solution(mesh):
    in_specs = (
        P(None, "seq", None),
        P(None, "seq", None),
        P(),
        P(),
        P("seq", "head"),
        P("seq", "head"),
        P("seq", "head"),
        P("head", "seq"),
        P("seq", "head"),
        P("seq", "head"),
        P("head", "seq"),
        P(),
        P(None, "head"),
        P(None, "head"),
        P(None, "head"),
        P("head", None),
        P(),
        P("head", None, None),
        P("head", None, None),
        P(),
    )
    out_specs = (
        P(None, "seq", None),
        P(None, "seq", None),
        P(),
        P(),
        P("seq", "head"),
        P("seq", "head"),
        P("seq", "head"),
        P("head", "seq"),
        P("seq", "head"),
        P("seq", "head"),
        P("head", "seq"),
        P(),
        P(None, "head"),
        P(None, "head"),
        P(None, "head"),
        P("head", None),
        P(),
        P("head", None, None),
        P("head", None, None),
    )
    return jax.shard_map(body, mesh=mesh, in_specs=in_specs, out_specs=out_specs, check_vma=False)
```
